32 devices in a mesh: dp: 8 (over z, y), inner: 4 (over x, core).
Axes of the slice: x: 2, y: 2, z: 4, core: 2. Of those that a mesh axis runs over, the one named last changes fastest.
Arguments:
- inputs: bfloat16 [32768, 768], P(('dp', 'inner')), may hold values from -6 to 6
- qkv_weight: bfloat16 [1769472], P(('dp', 'inner')), may hold values from -0.21875 to 0.21875
- out_weight: bfloat16 [589824], P(('dp', 'inner')), may hold values from -0.625 to 0.625
- up_weight: bfloat16 [2359296], P(('dp', 'inner')), may hold values from -0.21875 to 0.21875
- down_weight: bfloat16 [2359296], P(('dp', 'inner')), may hold values from -0.109375 to 0.109375
- vectors: bfloat16 [9216], P(('dp', 'inner')), may hold values from -1 to 2
- lengths: int32 [64], P(('dp', 'inner')), may hold values from 128 to 512, as said below
- counts: int32 [64], P(('dp', 'inner')), may hold values from 42 to 128, as said below
- positions: int32 [64, 128], P(('dp', 'inner')), may hold values from 0 to 511, as said below
- grad_values: bfloat16 [64, 128, 768], P(('dp', 'inner')), may hold values from -6 to 6
Outputs:
- layer_out: bfloat16 [32768, 768], P(('dp', 'inner'))
- input_grad: bfloat16 [32768, 768], P(('dp', 'inner'))
- qkv_grad: float32 [1769472], P(('dp', 'inner'))
- attn_out_grad: float32 [589824], P(('dp', 'inner'))
- up_weight_gradient: float32 [2359296], P(('dp', 'inner'))
- down_grad: float32 [2359296], P(('dp', 'inner'))
- vector_grad: float32 [9216], P(('dp', 'inner'))
The draws below stay inside these ranges and needn't reach their ends.
Inputs may be any that keep to these rules, and one draw needn't show every extreme that they name: `lengths`: some sequence has all 512 tokens valid and some has exactly 128. counts[s] is at most lengths[s]; some sequence uses all 128 slots. Each row holds distinct positions, all below that sequence's length.
All inputs are finite; a program needn't handle non-finite values.
Results may differ from the reference program's by a relative error of at most 0.012.
Values may be sent and summed in bfloat16 or wider, within the bound.
A program may use at most 192 MiB of HBM per device.

```python
import jax
import jax.numpy as jnp
from jax import lax

D = 768
H = 12
HD = 64
FF = 3072
SEQ_LEN = 512
PMAX = 128
VEC = 9216
SEQS = 64
TOKENS = 32768


def draw_plan(key):
    first_key = jax.random.fold_in(key, 11)
    second_key = jax.random.fold_in(key, 12)
    third_key = jax.random.fold_in(key, 13)
    length_keys = jax.random.split(first_key, 2)
    lengths = jax.random.randint(length_keys[0], (SEQS,), PMAX, SEQ_LEN + 1)
    chosen = jax.random.randint(length_keys[1], (), 0, SEQS)
    lengths = lengths.at[chosen].set(SEQ_LEN)
    lengths = lengths.at[(chosen + SEQS // 2) % SEQS].set(PMAX)
    count_keys = jax.random.split(second_key, 4)
    common = jax.random.randint(count_keys[0], (SEQS,), SEQ_LEN // 12, SEQ_LEN // 6 + 1)
    heavy = jax.random.randint(count_keys[1], (SEQS,), SEQ_LEN // 6, PMAX + 1)
    picker = jax.random.randint(count_keys[2], (SEQS,), 0, 8)
    counts = jnp.where(picker == 0, heavy, common)
    target = jax.random.randint(count_keys[3], (), 0, SEQS)
    counts = counts.at[target].set(PMAX)
    counts = counts.at[(target + SEQS // 2) % SEQS].set(SEQ_LEN // 12)
    ranks = jax.random.randint(third_key, (SEQS, SEQ_LEN), 0, 2 ** 20)
    places = jnp.arange(SEQ_LEN, dtype=jnp.int32)[None, :]
    order_keys = jnp.where(places < lengths[:, None], ranks * SEQ_LEN + places, 2 ** 30 + places)
    positions = jnp.argsort(order_keys, axis=1, stable=True)[:, :PMAX].astype(jnp.int32)
    return (lengths.astype(jnp.int32), counts.astype(jnp.int32), positions)


def draw_lengths(key, part):
    return draw_plan(key)[0]


def draw_counts(key, part):
    return draw_plan(key)[1]


def draw_positions(key, part):
    return draw_plan(key)[2]


def draw_vectors(key, part):
    places = jnp.arange(VEC)
    gain_part = (places >= 3 * D) & (places < 4 * D) | (places >= 6 * D + FF) & (places < 7 * D + FF)
    key_pair = jax.random.split(key, 2)
    gains = 0.5 + jax.random.uniform(key_pair[0], (VEC,))
    biases = jnp.clip(0.3 * jax.random.normal(key_pair[1], (VEC,)), -1.0, 1.0)
    return jnp.where(gain_part, gains, biases).astype(jnp.float32).astype(jnp.bfloat16)


def block_scale(stream_key, extent, cuts, least, high):
    level = 1.0
    for axis_at, blocks in cuts:
        steps = jax.random.uniform(jax.random.fold_in(jax.random.fold_in(stream_key, 6), axis_at), (blocks,), jnp.float32, least / len(cuts), high / len(cuts))
        level = level * jnp.repeat(jnp.exp(steps), extent[axis_at] // blocks).reshape((-1,) + (1,) * (len(extent) - 1 - axis_at))
    return level


def centred(own_key, shape, width, most, cuts=(), held_as=jnp.bfloat16):
    result = jax.random.normal(own_key, shape, jnp.float32) * width
    if len(cuts) > 0:
        result = block_scale(own_key, shape, cuts, -0.22, 0.18) * result
    return jnp.clip(result, min=-most, max=most).astype(held_as)


def setup_inputs(seed: int = 0) -> dict:
    key_list = jax.random.split(jax.random.key(seed), 11)
    inputs = centred(key_list[0], (TOKENS, D), 1.0, 6.0, ((0, 32),))
    qkv_weight = centred(key_list[1], (3 * D * D,), D ** -0.5, 0.21875, ((0, 32),))
    out_weight = centred(key_list[2], (D * D,), (D // 8) ** -0.5, 0.625, ((0, 32),))
    up_weight = centred(key_list[3], (D * FF,), D ** -0.5, 0.21875, ((0, 32),))
    down_weight = centred(key_list[4], (FF * D,), FF ** -0.5, 0.109375, ((0, 32),))
    vectors = draw_vectors(jax.random.fold_in(key_list[10], 71), 0)
    lengths = draw_lengths(jax.random.fold_in(key_list[10], 71), 0)
    counts = draw_counts(jax.random.fold_in(key_list[10], 71), 0)
    positions = draw_positions(jax.random.fold_in(key_list[10], 71), 0)
    grad_values = centred(key_list[9], (SEQS, PMAX, D), 1.0, 6.0, ((0, 32),))
    return dict(inputs=inputs, qkv_weight=qkv_weight, out_weight=out_weight, up_weight=up_weight, down_weight=down_weight, vectors=vectors, lengths=lengths, counts=counts, positions=positions, grad_values=grad_values)


norm_eps = 1e-05
masked_score = -1e+30

@jax.custom_vjp
def low(v):
    return lax.optimization_barrier(v.astype(jnp.bfloat16)).astype(jnp.float32)

@jax.custom_vjp
def low_back(v):
    return v

def low_keep(v):
    return (low(v), None)

def low_pass(kept, grad):
    return (grad,)

def back_keep(v):
    return (v, None)

def back_low(kept, grad):
    return (low(grad),)
low.defvjp(low_keep, low_pass)
low_back.defvjp(back_keep, back_low)

def product(left, right):
    return jnp.dot(left, right, precision=lax.Precision.HIGHEST, preferred_element_type=jnp.float32)

def split_vectors(vector_in):
    starts = [0, D, 2 * D, 3 * D, 4 * D, 5 * D, 5 * D + FF, 6 * D + FF, 7 * D + FF, 8 * D + FF]
    return tuple((vector_in[starts[item_count]:starts[item_count + 1]] for item_count in range(9)))

def layer_norm(row_data, gain_row, shift_row):
    mean_row = lax.optimization_barrier(jnp.mean(row_data, -1, keepdims=True))
    centered = row_data - mean_row
    spread = lax.optimization_barrier(jnp.mean(centered * centered, -1, keepdims=True))
    return centered * lax.rsqrt(spread + norm_eps) * gain_row + shift_row

def dense_cotangent(positions, counts, value_entries):
    places = jnp.arange(SEQ_LEN, dtype=jnp.int32)
    slot_ids = jnp.arange(PMAX, dtype=jnp.int32)
    matches = (positions[:, :, None] == places[None, None, :]) & (slot_ids[None, :, None] < counts[:, None, None])
    indicator_rows = matches.astype(jnp.float32)
    dense_matrix = jnp.einsum('jgw,jgq->jwq', indicator_rows, value_entries.astype(jnp.float32), precision=lax.Precision.HIGHEST)
    return dense_matrix.reshape(-1, D)

def forward(inputs, qkv_matrix, output_projection, up_matrix, down_matrix, vector_in, lengths):
    q_bias, v_bias, out_bias, gain_one, shift_one, up_bias, down_bias, gain_two, shift_two = split_vectors(vector_in)
    score_scale = HD ** (-0.5)
    groups = inputs.shape[0] // SEQ_LEN
    rounded = low(inputs)
    qkv_bias = jnp.concatenate([q_bias, jnp.zeros_like(q_bias), v_bias])
    joined = low(low_back(product(rounded, qkv_matrix) + qkv_bias))
    split_heads = joined.reshape(groups, SEQ_LEN, 3, H, HD)
    queries = split_heads[:, :, 0]
    keys_in = split_heads[:, :, 1]
    value_entries = split_heads[:, :, 2]
    scores = low_back(jnp.einsum('sqhd,skhd->shqk', queries, keys_in, precision=lax.Precision.HIGHEST) * score_scale)
    key_valid = jnp.arange(SEQ_LEN, dtype=jnp.int32)[None, :] < lengths[:, None]
    scores = jnp.where(key_valid[:, None, None, :], scores, masked_score)
    attn_probs = low(jax.nn.softmax(scores, axis=-1))
    context = jnp.einsum('shqk,skhd->sqhd', attn_probs, value_entries, precision=lax.Precision.HIGHEST)
    context = low(low_back(context.reshape(groups * SEQ_LEN, D)))
    attn_out = low_back(product(context, output_projection) + out_bias)
    normed_one = layer_norm(inputs + attn_out, gain_one, shift_one)
    pre_act = low_back(product(low(normed_one), up_matrix) + up_bias)
    active = low(jax.nn.gelu(pre_act, approximate=False))
    ffn_out = low_back(product(active, down_matrix) + down_bias)
    return layer_norm(normed_one + ffn_out, gain_two, shift_two)

def reference(inputs, qkv_weight, out_weight, up_weight, down_weight, vectors, lengths, counts, positions, grad_values):
    weights = (qkv_weight.astype(jnp.float32).reshape(D, 3 * D), out_weight.astype(jnp.float32).reshape(D, D), up_weight.astype(jnp.float32).reshape(D, FF), down_weight.astype(jnp.float32).reshape(FF, D), vectors.astype(jnp.float32))
    group_size = 8
    blocks = SEQS // group_size
    stacked = (inputs.reshape(blocks, group_size * SEQ_LEN, D), lengths.reshape(blocks, group_size), counts.reshape(blocks, group_size), positions.reshape(blocks, group_size, PMAX), grad_values.reshape(blocks, group_size, PMAX, D))

    def one_block(totals, pieces):
        block_in, block_len, block_count, block_pos, block_vals = pieces

        def apply_block(block_x, qkv_m, out_m, up_m, down_m, vector_m):
            return forward(block_x, qkv_m, out_m, up_m, down_m, vector_m, block_len)
        block_out, pullback = jax.vjp(apply_block, block_in.astype(jnp.float32), *weights)
        gradients = pullback(dense_cotangent(block_pos, block_count, block_vals))
        totals = tuple((running_total + update for running_total, update in zip(totals, gradients[1:])))
        return (totals, (block_out.astype(jnp.bfloat16), gradients[0].astype(jnp.bfloat16)))
    zeros = tuple((jnp.zeros_like(weight) for weight in weights))
    totals, (outputs, in_grads) = lax.scan(one_block, zeros, stacked)
    return (outputs.reshape(-1, D), in_grads.reshape(-1, D), totals[0].reshape(-1), totals[1].reshape(-1), totals[2].reshape(-1), totals[3].reshape(-1), totals[4])
```

```python
from functools import partial

import jax
import jax.numpy as jnp
from jax import lax
from jax.experimental import pallas as pl
from jax.experimental.pallas import tpu as pltpu
from jax.sharding import PartitionSpec as P

bf = jnp.bfloat16
f32 = jnp.float32
MESH = pl.DeviceIdType.MESH
NU = 12
C, X, Y, Z0, Z1 = range(5)
A = slice(None)
gather_order = (
    "0z1", "1z1", "2z1", "11z1", "8s0", "6s0", "10s0", "5s0", "9s0", "7s0", "0z0", "1z0", "3z1",
    "0B1", "0A1", "2z0", "8z1", "4z1", "1B1", "1A1", "0B2", "0A2", "2B1", "11z0", "1A2", "3z0",
    "2A1", "1B2", "4z0", "7z1", "6z1", "0C", "2A2", "4B1", "2B2", "3B1", "7z0", "11B1", "3A1",
    "1C", "11A1", "8z0", "2C", "4A1", "3A2", "6z0", "5z1", "9z1", "3B2", "7s3", "4A2", "10z1",
    "4B2", "8s3", "5z0", "3C", "9z0", "6s3", "7C", "5s3", "4C", "10z0", "9s3", "8C", "11B2",
    "10s3", "11A2", "5C", "6C", "9C", "10C", "11C",
)
scatter_order = (
    "0C", "1C", "0s3", "3C", "1s3", "4C", "2C", "4s3", "7C", "3s3", "5C", "7A2", "8C", "6C", "2s3",
    "0z0", "8B2", "7B2", "5s3", "1z0", "4z0", "8A2", "8B1", "3z0", "9C", "6A2", "0z1", "10C",
    "11C", "6B2", "11A2", "4z1", "2z0", "11B2", "1z1", "8A1", "3z1", "6B1", "6A1", "5z0", "11B1",
    "7A1", "11A1", "9A2", "9B2", "8z0", "2z1", "10B2", "6z0", "7B1", "8z1", "11z0", "5z1", "10A2",
    "7z0", "3s0", "9B1", "11z1", "9A1", "6z1", "10A1", "10B1", "7z1", "4s0", "2s0", "9z0", "5s0",
    "1s0", "10z0", "0s0", "9z1", "10z1",
)

scatter_units = (4, 5, 6, 7, 8, 9, 10, 11, 3, 1, 0, 2)
gather_types = ("ab",) * 5 + ("e", "f") * 3 + ("ab",)
scatter_types = ("f", "e") * 3 + ("ab",) * 6


def parse(order):
    digits = [2 if o[1].isdigit() else 1 for o in order]
    return [(int(o[:d]), o[d:]) for o, d in zip(order, digits)]


class Place:
    def __init__(self, dp_size, inner_size):
        n=dp_size*inner_size
        self.nsub=n//32
        self.inner=inner_size
        lin=lax.axis_index("dp")*inner_size+lax.axis_index("inner")
        self.sub=lin%self.nsub
        self.g=lin//self.nsub
        self.bit=[(self.g//(2**b))%2 for b in range(5)]
        self.c,self.x,self.y,self.z0,self.z1=self.bit
    def partner(self,b):
        g=self.g+2**b-2*(2**b)*self.bit[b]
        lin=g*self.nsub+self.sub
        return (lin//self.inner, lin%self.inner)

def remote(src,dst,ss,rs,dev):
    return pltpu.make_async_remote_copy(src_ref=src,dst_ref=dst,send_sem=ss,recv_sem=rs,device_id=dev,device_id_type=MESH)

class Gather:
    def __init__(self,pos,W,ss,rs,types):
        self.p=pos; self.W=W; self.ss=ss; self.rs=rs; self.types=types
        self.cols=pl.ds(pl.multiple_of(384*pos.c,128),384)
        z1,z0,y,x=pos.z1,pos.z0,pos.y,pos.x
        head=[("z1",(),Z1,(z1,z0,y,x)),("z0",("z1",),Z0,(A,z0,y,x))]
        whole=(A,A,A,A)
        self.legs={
            "ab":head+[("A1",("z0",),Y,(0,A,y,x)),("B1",("z0",),X,(1,A,y,x)),
                       ("A2",("A1",),X,(0,A,A,x)),("B2",("B1",),Y,(1,A,y,A)),("C",("A2","B2"),C,whole)],
            "e":[("s0",(),X,(z1,z0,y,x)),("z1",("s0",),Z1,(z1,z0,y,A)),("z0",("z1",),Z0,(A,z0,y,A)),("s3",("z0",),Y,(A,A,y,A)),("C",("s3",),C,whole)],
            "f":[("s0",(),Y,(z1,z0,y,x)),("z1",("s0",),Z1,(z1,z0,A,x)),("z0",("z1",),Z0,(A,z0,A,x)),("s3",("z0",),X,(A,A,A,x)),("C",("s3",),C,whole)],
        }
        self.got=set(); self.sent=[]
    def copy(self,m,n):
        L=self.legs[self.types[m]]
        k=[l[0] for l in L].index(n)
        _,_,b,idx=L[k]
        r=self.W.at[(m,)+idx+(A,self.cols)]
        return remote(r,r,self.ss.at[m,k],self.rs.at[m,k],self.p.partner(b)), L[k][1]
    def arrive(self,m,n):
        if (m,n) in self.got: return
        self.got.add((m,n)); self.copy(m,n)[0].wait_recv()
    def op(self,m,n):
        c,deps=self.copy(m,n)
        for d in deps: self.arrive(m,d)
        c.start(); self.sent.append((m,n))
    def drain(self):
        for m,n in self.sent: self.copy(m,n)[0].wait_send()

class Scatter:
    def __init__(self,pos,P,R,ss,rs,rdy,types,order):
        self.p=pos; self.P=P; self.R=R; self.ss=ss; self.rs=rs; self.rdy=rdy; self.types=types
        c,x,y,z0,z1=pos.c,pos.x,pos.y,pos.z0,pos.z1
        self.legs={
            "ab":[("A2",("C",),X,(0,A,A,1-x),(0,A,A,1-x),(0,A,A,x),(0,A,A,x)),
                  ("B2",("C",),Y,(1,A,1-y,A),(1,A,1-y,A),(1,A,y,A),(1,A,y,A)),
                  ("A1",("A2",),Y,(0,A,1-y,x),(0,A,1-y,1-x),(0,A,y,x),(0,A,y,1-x)),
                  ("B1",("B2",),X,(1,A,y,1-x),(1,A,1-y,1-x),(1,A,y,x),(1,A,1-y,x)),
                  ("z0",("A1","B1"),Z0,(A,1-z0,y,x),(A,1-z0,1-y,1-x),(A,z0,y,x),(A,z0,1-y,1-x)),
                  ("z1",("z0",),Z1,(1-z1,z0,y,x),(1-z1,1-z0,1-y,1-x),(z1,z0,y,x),(z1,1-z0,1-y,1-x))],
            "e":[("s3",("C",),Y,(A,A,1-y,A),(A,A,1-y,A),(A,A,y,A),(A,A,y,A)),
                 ("z0",("s3",),Z0,(A,1-z0,y,A),(A,1-z0,1-y,A),(A,z0,y,A),(A,z0,1-y,A)),
                 ("z1",("z0",),Z1,(1-z1,z0,y,A),(1-z1,1-z0,1-y,A),(z1,z0,y,A),(z1,1-z0,1-y,A)),
                 ("s0",("z1",),X,(z1,z0,y,1-x),(1-z1,1-z0,1-y,1-x),(z1,z0,y,x),(1-z1,1-z0,1-y,x))],
            "f":[("s3",("C",),X,(A,A,A,1-x),(A,A,A,1-x),(A,A,A,x),(A,A,A,x)),
                 ("z0",("s3",),Z0,(A,1-z0,A,x),(A,1-z0,A,1-x),(A,z0,A,x),(A,z0,A,1-x)),
                 ("z1",("z0",),Z1,(1-z1,z0,A,x),(1-z1,1-z0,A,1-x),(z1,z0,A,x),(z1,1-z0,A,1-x)),
                 ("s0",("z1",),Y,(z1,z0,1-y,x),(1-z1,1-z0,1-y,1-x),(z1,z0,y,x),(1-z1,1-z0,y,1-x))],
        }
        self.got=set(); self.sent=[]
        self.turn={}
        for m,n in order:
            for d in self.leg(m,n)[1]:
                if d=="C" and m not in self.turn: self.turn[m]=len(self.turn)
        self.heard={b:0 for b in (X,Y,Z0,Z1)}
    def leg(self,m,n):
        if n=="C": return ("C",(),C)
        return [l for l in self.legs[self.types[m]] if l[0]==n][0]
    def copy(self,m,n):
        c=self.p.c
        if n=="C":
            return remote(self.P.at[m,1-c],self.R.at[m],self.ss.at[m,0],self.rs.at[m,0],self.p.partner(C))
        L=self.legs[self.types[m]]
        k=[l[0] for l in L].index(n)
        _,_,b,snd,lnd,_,_=L[k]
        return remote(self.P.at[(m,c)+snd],self.P.at[(m,1-c)+lnd],self.ss.at[m,k+1],self.rs.at[m,k+1],self.p.partner(b))
    def add(self,m,n):
        if (m,n) in self.got: return
        self.got.add((m,n)); c=self.p.c
        d=self.copy(m,n)
        if n=="C":
            d.wait_send(); self.sent.remove((m,n))
            for b in (X,Y,Z0,Z1):
                pl.semaphore_signal(self.rdy.at[b-1],inc=1,device_id=self.p.partner(b),device_id_type=MESH)
            d.wait_recv()
            self.P[m,c]=self.P[m,c]+self.R[m]
            return
        d.wait_recv()
        _,_,_,_,_,own,got=self.leg(m,n)
        i=(m,c)+own
        self.P[i]=self.P[i]+self.P[(m,1-c)+got]
    def op(self,m,n):
        L=self.leg(m,n)
        for d in L[1]: self.add(m,d)
        b=L[2]
        if b!=C:
            need=self.turn[m]+1-self.heard[b]
            if need>0:
                pl.semaphore_wait(self.rdy.at[b-1],need); self.heard[b]+=need
        self.copy(m,n).start(); self.sent.append((m,n))
    def last(self,m):
        n=self.legs[self.types[m]][-1][0]
        self.copy(m,n).wait_recv()
        c=self.p.c
        _,_,_,_,_,own,got=self.leg(m,n)
        v=self.P[(m,c)+own].astype(f32)+self.P[(m,1-c)+got].astype(f32)
        top=v[0:8]; bot=v[8:16]
        return jnp.concatenate([jnp.concatenate([top[:,384*k:384*k+384],bot[:,384*k:384*k+384]],1) for k in range(3)],0)
    def drain(self):
        for m,n in self.sent: self.copy(m,n).wait_send()
        for b in (X,Y,Z0,Z1):
            left=NU-self.heard[b]
            if left>0: pl.semaphore_wait(self.rdy.at[b-1],left)
def enter(pos):
    b=pltpu.get_barrier_semaphore()
    for k in range(5):
        pl.semaphore_signal(b,inc=1,device_id=pos.partner(k),device_id_type=MESH)
    pl.semaphore_wait(b,5)


def gather_kernel(dp_size, inner_size, sh, w2, wout, W, SHR, ss, rs, fs, ls):
    pos = Place(dp_size, inner_size)
    enter(pos)
    c = pos.c
    G = Gather(pos, W, ss, rs, gather_types)
    oc = pl.ds(pl.multiple_of(384 * (1 - c), 128), 384)
    cp = remote(sh.at[:, :, oc], SHR, fs.at[0], fs.at[1], pos.partner(C))
    cp.start()
    chip = (pos.z1, pos.z0, pos.y, pos.x)
    cp2 = [
        remote(
            w2.at[j, :, oc],
            W.at[(8 + 2 * c + j,) + chip + (A, oc)],
            fs.at[2 + 2 * j],
            fs.at[3 + 2 * j],
            pos.partner(C),
        )
        for j in range(2)
    ]
    for q in cp2:
        q.start()
    for j in range(2):
        W[(8 + 2 * c + j,) + chip + (A, G.cols)] = w2[j, :, G.cols]
    cp.wait_recv()
    for u in range(8):
        own = sh[u, :, G.cols]
        oth = SHR[u]
        lo = jnp.where(c == 0, own, oth)
        hi = jnp.where(c == 0, oth, own)
        W[(u,) + chip + (A, G.cols)] = jnp.concatenate([lo, hi], 0).astype(bf)
    for q in cp2:
        q.wait_recv()
    for m, n in parse(gather_order):
        G.op(m, n)
    for m in range(NU):
        G.arrive(m, "C")
    cp.wait_send()
    for q in cp2:
        q.wait_send()
    G.drain()
    o = pltpu.make_async_copy(W, wout, ls)
    o.start()
    o.wait()


def scatter_kernel(dp_size, inner_size, p_in, gw, P, R, ss, rs, rdy, ls):
    pos = Place(dp_size, inner_size)
    o = pltpu.make_async_copy(p_in, P, ls)
    o.start()
    enter(pos)
    o.wait()
    S = Scatter(pos, P, R, ss, rs, rdy, scatter_types, parse(scatter_order))
    for m, n in parse(scatter_order):
        S.op(m, n)
    for m in range(NU):
        gw[m] = S.last(m)
    S.drain()


VM = pl.BlockSpec(memory_space=pltpu.VMEM)
ANY = pl.BlockSpec(memory_space=pl.ANY)


def gather_call(sizes, sh, w2):
    return pl.pallas_call(
        partial(gather_kernel, *sizes),
        out_shape=jax.ShapeDtypeStruct((NU, 2, 2, 2, 2, 48, 768), bf),
        in_specs=[VM] * 2,
        out_specs=ANY,
        scratch_shapes=[
            pltpu.VMEM((NU, 2, 2, 2, 2, 48, 768), bf),
            pltpu.VMEM((8, 24, 384), f32),
            pltpu.SemaphoreType.DMA((NU, 7)),
            pltpu.SemaphoreType.DMA((NU, 7)),
            pltpu.SemaphoreType.DMA((6,)),
            pltpu.SemaphoreType.DMA,
        ],
        compiler_params=pltpu.CompilerParams(
            collective_id=0, has_side_effects=True, vmem_limit_bytes=32 * 2**20
        ),
    )(sh, w2)


def scatter_call(sizes, p):
    return pl.pallas_call(
        partial(scatter_kernel, *sizes),
        out_shape=jax.ShapeDtypeStruct((NU, 24, 768), f32),
        in_specs=[ANY],
        out_specs=VM,
        scratch_shapes=[
            pltpu.VMEM((NU, 2, 2, 2, 2, 2, 16, 1152), bf),
            pltpu.VMEM((NU, 2, 2, 2, 2, 16, 1152), bf),
            pltpu.SemaphoreType.DMA((NU, 7)),
            pltpu.SemaphoreType.DMA((NU, 7)),
            pltpu.SemaphoreType.REGULAR((4,)),
            pltpu.SemaphoreType.DMA,
        ],
        compiler_params=pltpu.CompilerParams(
            collective_id=1, has_side_effects=True, vmem_limit_bytes=40 * 2**20
        ),
    )(p)


def groups_of(sizes):
    sub = sizes[0] * sizes[1] // 32
    return [[sub * i + j for j in range(sub)] for i in range(32)]


def pre(sizes, flat):
    if sizes[0] * sizes[1] == 32:
        return flat
    return lax.all_gather(flat, ("dp", "inner"), axis_index_groups=groups_of(sizes), tiled=True)


def post(sizes, flat):
    if sizes[0] * sizes[1] == 32:
        return flat
    return lax.psum_scatter(
        flat, ("dp", "inner"), axis_index_groups=groups_of(sizes), scatter_dimension=0, tiled=True
    )


def wire(unit):
    v = unit.reshape(16, 2, 3, 8, 2, 384).transpose(1, 0, 4, 3, 2, 5)
    return v.reshape(2, 2, 2, 2, 2, 16, 1152).astype(bf)


D = 768
H = 12
HD = 64
FF = 3072
SEQ_LEN = 512
PMAX = 128


norm_eps = 1e-05
masked_score = -1e30


def layer_norm(row_data, gain_row, shift_row):
    mean_row = jnp.mean(row_data, -1, keepdims=True)
    centered = row_data - mean_row
    spread = jnp.mean(centered * centered, -1, keepdims=True)
    return centered * lax.rsqrt(spread + norm_eps) * gain_row + shift_row


def split_vectors(vector_in):
    starts = [0, D, 2 * D, 3 * D, 4 * D, 5 * D, 5 * D + FF, 6 * D + FF, 7 * D + FF, 8 * D + FF]
    return tuple(
        (vector_in[starts[item_count] : starts[item_count + 1]] for item_count in range(9))
    )


def matmul(left, right):
    return jnp.dot(left, right, preferred_element_type=jnp.float32)


def contracted_row_axes(left, right):
    return lax.dot_general(
        left, right, (((0,), (0,)), ((), ())), preferred_element_type=jnp.float32
    )


def contract_cols(left, right):
    return lax.dot_general(
        left, right, (((1,), (1,)), ((), ())), preferred_element_type=jnp.float32
    )


def masked_scores(head_rows, key_valid):
    queries = head_rows[:, 0]
    keys_in = head_rows[:, 1]
    scores = jnp.einsum(
        "qhd,khd->hqk", queries, keys_in, preferred_element_type=jnp.float32
    ) * HD ** (-0.5)
    return jnp.where(key_valid[None, None, :], scores, masked_score)


def attend_forward(items):
    head_rows, key_valid = items
    scores = masked_scores(head_rows, key_valid)
    row_max = jnp.max(scores, -1, keepdims=True)
    exponent = jnp.exp(scores - row_max)
    row_total = jnp.sum(exponent, -1, keepdims=True)
    attn_probs = (exponent / row_total).astype(jnp.bfloat16)
    context = jnp.einsum(
        "hqk,khd->qhd", attn_probs, head_rows[:, 2], preferred_element_type=jnp.float32
    )
    return (context.reshape(SEQ_LEN, D), row_max + jnp.log(row_total))


def attend_backward(items):
    head_rows, key_valid, log_norm, ctx_grad = items
    queries = head_rows[:, 0]
    keys_in = head_rows[:, 1]
    value_entries = head_rows[:, 2]
    attn_probs = jnp.exp(masked_scores(head_rows, key_valid) - log_norm)
    probs_low = attn_probs.astype(jnp.bfloat16)
    prob_grad = jnp.einsum(
        "qhd,khd->hqk", ctx_grad, value_entries, preferred_element_type=jnp.float32
    )
    value_grad = jnp.einsum("hqk,qhd->khd", probs_low, ctx_grad, preferred_element_type=jnp.float32)
    row_dot = jnp.sum(prob_grad * attn_probs, -1, keepdims=True)
    score_grad = (attn_probs * (prob_grad - row_dot)).astype(jnp.bfloat16)
    query_grad = jnp.einsum(
        "hqk,khd->qhd", score_grad, keys_in, preferred_element_type=jnp.float32
    ) * HD ** (-0.5)
    key_grad = jnp.einsum(
        "hqk,qhd->khd", score_grad, queries, preferred_element_type=jnp.float32
    ) * HD ** (-0.5)
    stacked = jnp.stack([query_grad, key_grad, value_grad], 1)
    return stacked.reshape(SEQ_LEN, 3 * D).astype(jnp.bfloat16)


def on_device(
    sizes,
    inputs,
    qkv_weight,
    out_weight,
    up_weight,
    down_weight,
    vectors,
    lengths,
    counts,
    positions,
    grad_values,
):
    fq, fo, fu, fd = [pre(sizes, w) for w in (qkv_weight, out_weight, up_weight, down_weight)]
    fq = fq.reshape(24, 3, 768)
    fq = jnp.stack([fq[:, 1], fq[:, 2], fq[:, 0]])
    fu = fu.reshape(24, 4, 768).transpose(1, 0, 2)
    sh = jnp.concatenate([fq, fo.reshape(1, 24, 768), fu], 0).astype(f32)
    units = gather_call(sizes, sh, fd.reshape(2, 48, 768)).reshape(12, 768, 768)
    qkv_matrix = jnp.concatenate([units[2], units[0], units[1]], 1)
    output_projection = units[3]
    up_matrix = jnp.concatenate([units[4 + i] for i in range(4)], 1)
    down_matrix = units[8:].reshape(4, 16, 48, 768).transpose(1, 0, 2, 3).reshape(FF, D)
    vec = lax.all_gather(vectors, ("dp", "inner"), axis=0, tiled=True)
    q_bias, v_bias, out_bias, gain_one, shift_one, up_bias, down_bias, gain_two, shift_two = (
        split_vectors(vec.astype(jnp.float32))
    )
    groups = inputs.shape[0] // SEQ_LEN
    qkv_bias = jnp.concatenate([q_bias, jnp.zeros_like(q_bias), v_bias])
    joined = (matmul(inputs, qkv_matrix) + qkv_bias).astype(jnp.bfloat16)
    split_heads = joined.reshape(groups, SEQ_LEN, 3, H, HD)
    key_valid = lax.broadcasted_iota(jnp.int32, (groups, SEQ_LEN), 1) < lengths[:, None]
    context, log_norm = lax.map(attend_forward, (split_heads, key_valid))
    context_low = context.reshape(groups * SEQ_LEN, D).astype(jnp.bfloat16)
    attn_out = matmul(context_low, output_projection) + out_bias
    resid_one = inputs.astype(jnp.float32) + attn_out
    normed_one, first_pull = jax.vjp(layer_norm, resid_one, gain_one, shift_one)
    normed_low = normed_one.astype(jnp.bfloat16)
    pre_act = matmul(normed_low, up_matrix) + up_bias
    gelu_exact = partial(jax.nn.gelu, approximate=False)
    activated, gelu_pull = jax.vjp(gelu_exact, pre_act)
    active_low = activated.astype(jnp.bfloat16)
    ffn_out = matmul(active_low, down_matrix) + down_bias
    layer_out, second_pull = jax.vjp(layer_norm, normed_one + ffn_out, gain_two, shift_two)
    places = jnp.arange(SEQ_LEN, dtype=jnp.int32)
    slot_ids = jnp.arange(PMAX, dtype=jnp.int32)
    matches = (positions[:, :, None] == places[None, None, :]) & (
        slot_ids[None, :, None] < counts[:, None, None]
    )
    cotangent = jnp.einsum(
        "jgw,jgq->jwq",
        matches.astype(jnp.bfloat16),
        grad_values,
        preferred_element_type=jnp.float32,
    ).reshape(-1, D)
    d_two, gain_two_grad, shift_two_grad = second_pull(cotangent)
    ffn_grad = d_two.astype(jnp.bfloat16)
    down_grad = contracted_row_axes(active_low, ffn_grad)
    down_bias_grad = jnp.sum(ffn_grad.astype(jnp.float32), 0)
    act_grad = contract_cols(ffn_grad, down_matrix)
    pre_grad = gelu_pull(act_grad)[0].astype(jnp.bfloat16)
    up_weight_gradient = contracted_row_axes(normed_low, pre_grad)
    up_bias_grad = jnp.sum(pre_grad.astype(jnp.float32), 0)
    d_normed = d_two + contract_cols(pre_grad, up_matrix)
    d_one, gain_one_grad, shift_one_grad = first_pull(d_normed)
    attn_grad = d_one.astype(jnp.bfloat16)
    out_grad = contracted_row_axes(context_low, attn_grad)
    out_bias_grad = jnp.sum(attn_grad.astype(jnp.float32), 0)
    ctx_grad = (
        contract_cols(attn_grad, output_projection)
        .astype(jnp.bfloat16)
        .reshape(groups, SEQ_LEN, H, HD)
    )
    joined_grad = lax.map(attend_backward, (split_heads, key_valid, log_norm, ctx_grad))
    joined_grad = joined_grad.reshape(groups * SEQ_LEN, 3 * D)
    qkv_grad = contracted_row_axes(inputs, joined_grad)
    joined_sums = jnp.sum(joined_grad.astype(jnp.float32), 0)
    input_grad = (d_one + contract_cols(joined_grad, qkv_matrix)).astype(jnp.bfloat16)
    vector_grad = jnp.concatenate(
        [
            joined_sums[:D],
            joined_sums[2 * D :],
            out_bias_grad,
            gain_one_grad,
            shift_one_grad,
            up_bias_grad,
            down_bias_grad,
            gain_two_grad,
            shift_two_grad,
        ]
    )
    cols = [qkv_grad[:, 768:1536], qkv_grad[:, 1536:], qkv_grad[:, :768], out_grad]
    cols += [up_weight_gradient[:, 768 * i : 768 * i + 768] for i in range(4)]
    dg = down_grad.reshape(32, 4, 24, 768)
    cols += [dg[:, i].reshape(768, 768) for i in range(4)]
    turned = [cols[i] for i in scatter_units]
    gw = scatter_call(sizes, jnp.stack([wire(u) for u in turned]))
    back = [gw[scatter_units.index(u)] for u in range(12)]
    g_qkv = jnp.concatenate([back[2], back[0], back[1]], 1)
    g_up = jnp.concatenate(back[4:8], 1)
    g_down = jnp.concatenate(back[8:], 0)
    return (
        layer_out.astype(jnp.bfloat16),
        input_grad,
        post(sizes, g_qkv.reshape(-1)),
        post(sizes, back[3].reshape(-1)),
        post(sizes, g_up.reshape(-1)),
        post(sizes, g_down.reshape(-1)),
        lax.psum_scatter(vector_grad, ("dp", "inner"), scatter_dimension=0, tiled=True),
    )


def solution(mesh):
    placed = (
        P(("dp", "inner"), None),
        P(("dp", "inner")),
        P(("dp", "inner")),
        P(("dp", "inner")),
        P(("dp", "inner")),
        P(("dp", "inner")),
        P(("dp", "inner")),
        P(("dp", "inner")),
        P(("dp", "inner"), None),
        P(("dp", "inner"), None, None),
    )
    return jax.shard_map(
        partial(on_device, (mesh.shape["dp"], mesh.shape["inner"])),
        mesh=mesh,
        in_specs=placed,
        out_specs=(
            P(("dp", "inner"), None),
            P(("dp", "inner"), None),
            P(("dp", "inner")),
            P(("dp", "inner")),
            P(("dp", "inner")),
            P(("dp", "inner")),
            P(("dp", "inner")),
        ),
        check_vma=False,
    )
```

```python
from functools import partial

import jax
import jax.numpy as jnp
from jax import lax
from jax.experimental import pallas as pl
from jax.experimental.pallas import tpu as pltpu
from jax.sharding import PartitionSpec as P

D = 768
H = 12
HD = 64
FF = 3072
SEQ_LEN = 512
PMAX = 128
norm_eps = 1e-05
masked_score = -1e30

bf = jnp.bfloat16
f32 = jnp.float32
MESH = pl.DeviceIdType.MESH
PARTS = 32
ROWS = D // PARTS
UNITS = 12
K_UNIT, V_UNIT, Q_UNIT, OUT_UNIT, UP_UNIT, DOWN_UNIT = 0, 1, 2, 3, 4, 8
CORE, X, Y, Z0, Z1 = range(5)
ALL = slice(None)
HALF = D // 2
WIRE = 3 * HALF

gather_types = (
    "ab", "ab", "ab", "ab", "ab", "e", "f", "e", "f", "e", "f", "ab",
)
gather_order = (
    "0z1", "1z1", "2z1", "11z1", "8s0", "6s0", "10s0", "5s0", "9s0", "7s0", "0z0", "1z0", "3z1",
    "0B1", "0A1", "2z0", "8z1", "4z1", "1B1", "1A1", "0B2", "0A2", "2B1", "11z0", "1A2", "3z0",
    "2A1", "1B2", "4z0", "7z1", "6z1", "0C", "2A2", "4B1", "2B2", "3B1", "7z0", "11B1", "3A1",
    "1C", "11A1", "8z0", "2C", "4A1", "3A2", "6z0", "5z1", "9z1", "3B2", "7s3", "4A2", "10z1",
    "4B2", "8s3", "5z0", "3C", "9z0", "6s3", "7C", "5s3", "4C", "10z0", "9s3", "8C", "11B2",
    "10s3", "11A2", "5C", "6C", "9C", "10C", "11C",
)
gather_counts = (
    10, 0, 0, 0, 0, 23, 0, 3, 6, 0, 2, 6, 0, 0, 4, 0, 0, 2, 2, 0, 1, 1, 2, 3, 0, 2, 2, 0, 0, 0, 0,
)
scatter_units = (4, 5, 6, 7, 8, 9, 10, 11, 3, 1, 0, 2)
scatter_types = (
    "f", "e", "f", "e", "f", "e", "ab", "ab", "ab", "ab", "ab", "ab",
)
scatter_order = (
    "0C", "1C", "0s3", "3C", "1s3", "4C", "2C", "4s3", "7C", "3s3", "5C", "7A2", "8C", "6C", "2s3",
    "0z0", "8B2", "7B2", "5s3", "1z0", "4z0", "8A2", "8B1", "3z0", "9C", "6A2", "0z1", "10C",
    "11C", "6B2", "11A2", "4z1", "2z0", "11B2", "1z1", "8A1", "3z1", "6B1", "6A1", "5z0", "11B1",
    "7A1", "11A1", "9A2", "9B2", "8z0", "2z1", "10B2", "6z0", "7B1", "8z1", "11z0", "5z1", "10A2",
    "7z0", "3s0", "9B1", "11z1", "9A1", "6z1", "10A1", "10B1", "7z1", "4s0", "2s0", "9z0", "5s0",
    "1s0", "10z0", "0s0", "9z1", "10z1",
)
scatter_counts = (
    0, 1, 1, 1, 4, 0, 0, 4, 0, 0, 5, 0, 0, 4, 2, 0, 0, 0, 0, 6, 2, 0, 0, 0, 0, 0, 7, 0, 0, 0, 3, 5,
    3, 2, 1, 5, 1, 3, 2, 6, 2, 1, 1,
)


def parse(order):
    digits = [2 if o[1].isdigit() else 1 for o in order]
    return [(int(o[:d]), o[d:]) for o, d in zip(order, digits)]


class Place:
    def __init__(self, dp_size, inner_size):
        self.sub_size = dp_size * inner_size // PARTS
        self.inner_size = inner_size
        number = lax.axis_index("dp") * inner_size + lax.axis_index("inner")
        self.sub = number % self.sub_size
        self.group = number // self.sub_size
        self.bits = [(self.group // 2**b) % 2 for b in range(5)]
        self.c, self.x, self.y, self.z0, self.z1 = self.bits

    def partner(self, b):
        group = self.group + 2**b - 2 * 2**b * self.bits[b]
        number = group * self.sub_size + self.sub
        return (number // self.inner_size, number % self.inner_size)


def remote(src, dst, send_sem, recv_sem, device):
    return pltpu.make_async_remote_copy(
        src_ref=src,
        dst_ref=dst,
        send_sem=send_sem,
        recv_sem=recv_sem,
        device_id=device,
        device_id_type=MESH,
    )


def enter(place):
    barrier = pltpu.get_barrier_semaphore()
    for b in range(5):
        pl.semaphore_signal(barrier, inc=1, device_id=place.partner(b), device_id_type=MESH)
    pl.semaphore_wait(barrier, 5)


class Gather:
    def __init__(self, place, W, send, recv):
        self.place, self.W, self.send, self.recv = place, W, send, recv
        self.cols = pl.ds(pl.multiple_of(HALF * place.c, 128), HALF)
        x, y, z0, z1 = place.x, place.y, place.z0, place.z1
        every = (ALL, ALL, ALL, ALL)
        self.legs = {
            "ab": [
                ("z1", (), Z1, (z1, z0, y, x)),
                ("z0", ("z1",), Z0, (ALL, z0, y, x)),
                ("A1", ("z0",), Y, (0, ALL, y, x)),
                ("B1", ("z0",), X, (1, ALL, y, x)),
                ("A2", ("A1",), X, (0, ALL, ALL, x)),
                ("B2", ("B1",), Y, (1, ALL, y, ALL)),
                ("C", ("A2", "B2"), CORE, every),
            ],
            "e": [
                ("s0", (), X, (z1, z0, y, x)),
                ("z1", ("s0",), Z1, (z1, z0, y, ALL)),
                ("z0", ("z1",), Z0, (ALL, z0, y, ALL)),
                ("s3", ("z0",), Y, (ALL, ALL, y, ALL)),
                ("C", ("s3",), CORE, every),
            ],
            "f": [
                ("s0", (), Y, (z1, z0, y, x)),
                ("z1", ("s0",), Z1, (z1, z0, ALL, x)),
                ("z0", ("z1",), Z0, (ALL, z0, ALL, x)),
                ("s3", ("z0",), X, (ALL, ALL, ALL, x)),
                ("C", ("s3",), CORE, every),
            ],
        }
        self.got, self.sent = set(), []

    def copy(self, m, name):
        legs = self.legs[gather_types[m]]
        k = [leg[0] for leg in legs].index(name)
        _, after, b, index = legs[k]
        part = self.W.at[(m,) + index + (ALL, self.cols)]
        sems = self.send.at[m, k], self.recv.at[m, k]
        return remote(part, part, *sems, self.place.partner(b)), after

    def arrive(self, m, name="C"):
        if (m, name) not in self.got:
            self.got.add((m, name))
            self.copy(m, name)[0].wait_recv()

    def op(self, m, name):
        copy, after = self.copy(m, name)
        for a in after:
            self.arrive(m, a)
        copy.start()
        self.sent.append((m, name))

    def drain(self):
        for m, name in self.sent:
            self.copy(m, name)[0].wait_send()


class Scatter:
    def __init__(self, place, S, R, send, recv, ready, order):
        self.place, self.S, self.R = place, S, R
        self.send, self.recv, self.ready = send, recv, ready
        x, y, z0, z1 = place.x, place.y, place.z0, place.z1
        self.legs = {
            "ab": [
                ("A2", ("C",), X, (0, ALL, ALL, 1 - x), (0, ALL, ALL, 1 - x), (0, ALL, ALL, x), (0, ALL, ALL, x)),
                ("B2", ("C",), Y, (1, ALL, 1 - y, ALL), (1, ALL, 1 - y, ALL), (1, ALL, y, ALL), (1, ALL, y, ALL)),
                ("A1", ("A2",), Y, (0, ALL, 1 - y, x), (0, ALL, 1 - y, 1 - x), (0, ALL, y, x), (0, ALL, y, 1 - x)),
                ("B1", ("B2",), X, (1, ALL, y, 1 - x), (1, ALL, 1 - y, 1 - x), (1, ALL, y, x), (1, ALL, 1 - y, x)),
                ("z0", ("A1", "B1"), Z0, (ALL, 1 - z0, y, x), (ALL, 1 - z0, 1 - y, 1 - x), (ALL, z0, y, x), (ALL, z0, 1 - y, 1 - x)),
                ("z1", ("z0",), Z1, (1 - z1, z0, y, x), (1 - z1, 1 - z0, 1 - y, 1 - x), (z1, z0, y, x), (z1, 1 - z0, 1 - y, 1 - x)),
            ],
            "e": [
                ("s3", ("C",), Y, (ALL, ALL, 1 - y, ALL), (ALL, ALL, 1 - y, ALL), (ALL, ALL, y, ALL), (ALL, ALL, y, ALL)),
                ("z0", ("s3",), Z0, (ALL, 1 - z0, y, ALL), (ALL, 1 - z0, 1 - y, ALL), (ALL, z0, y, ALL), (ALL, z0, 1 - y, ALL)),
                ("z1", ("z0",), Z1, (1 - z1, z0, y, ALL), (1 - z1, 1 - z0, 1 - y, ALL), (z1, z0, y, ALL), (z1, 1 - z0, 1 - y, ALL)),
                ("s0", ("z1",), X, (z1, z0, y, 1 - x), (1 - z1, 1 - z0, 1 - y, 1 - x), (z1, z0, y, x), (1 - z1, 1 - z0, 1 - y, x)),
            ],
            "f": [
                ("s3", ("C",), X, (ALL, ALL, ALL, 1 - x), (ALL, ALL, ALL, 1 - x), (ALL, ALL, ALL, x), (ALL, ALL, ALL, x)),
                ("z0", ("s3",), Z0, (ALL, 1 - z0, ALL, x), (ALL, 1 - z0, ALL, 1 - x), (ALL, z0, ALL, x), (ALL, z0, ALL, 1 - x)),
                ("z1", ("z0",), Z1, (1 - z1, z0, ALL, x), (1 - z1, 1 - z0, ALL, 1 - x), (z1, z0, ALL, x), (z1, 1 - z0, ALL, 1 - x)),
                ("s0", ("z1",), Y, (z1, z0, 1 - y, x), (1 - z1, 1 - z0, 1 - y, 1 - x), (z1, z0, y, x), (1 - z1, 1 - z0, y, 1 - x)),
            ],
        }
        self.got, self.sent = set(), []
        self.turn = {}
        for m, name in order:
            if "C" in self.leg(m, name)[1] and m not in self.turn:
                self.turn[m] = len(self.turn)
        self.heard = {b: 0 for b in (X, Y, Z0, Z1)}

    def leg(self, m, name):
        if name == "C":
            return ("C", (), CORE)
        return [leg for leg in self.legs[scatter_types[m]] if leg[0] == name][0]

    def copy(self, m, name):
        c = self.place.c
        if name == "C":
            sems = self.send.at[m, 0], self.recv.at[m, 0]
            return remote(self.S.at[m, 1 - c], self.R.at[m], *sems, self.place.partner(CORE))
        k = [leg[0] for leg in self.legs[scatter_types[m]]].index(name) + 1
        _, _, b, out, land, _, _ = self.leg(m, name)
        sems = self.send.at[m, k], self.recv.at[m, k]
        return remote(
            self.S.at[(m, c) + out], self.S.at[(m, 1 - c) + land], *sems, self.place.partner(b)
        )

    def add(self, m, name):
        if (m, name) in self.got:
            return
        self.got.add((m, name))
        c = self.place.c
        copy = self.copy(m, name)
        if name == "C":
            copy.wait_send()
            self.sent.remove((m, name))
            for b in (X, Y, Z0, Z1):
                pl.semaphore_signal(
                    self.ready.at[b - 1],
                    inc=1,
                    device_id=self.place.partner(b),
                    device_id_type=MESH,
                )
            copy.wait_recv()
            self.S[m, c] = self.S[m, c] + self.R[m]
            return
        copy.wait_recv()
        own, landed = self.leg(m, name)[5:]
        self.S[(m, c) + own] = self.S[(m, c) + own] + self.S[(m, 1 - c) + landed]

    def op(self, m, name):
        after, b = self.leg(m, name)[1:3]
        for a in after:
            self.add(m, a)
        if b != CORE:
            need = self.turn[m] + 1 - self.heard[b]
            if need > 0:
                pl.semaphore_wait(self.ready.at[b - 1], need)
                self.heard[b] += need
        self.copy(m, name).start()
        self.sent.append((m, name))

    def last(self, m):
        name = self.legs[scatter_types[m]][-1][0]
        self.copy(m, name).wait_recv()
        c = self.place.c
        own, landed = self.leg(m, name)[5:]
        total = self.S[(m, c) + own].astype(f32) + self.S[(m, 1 - c) + landed].astype(f32)
        left, right = total[:8], total[8:]
        rows = [
            jnp.concatenate([v[:, HALF * k : HALF * k + HALF] for v in (left, right)], 1)
            for k in range(3)
        ]
        return jnp.concatenate(rows, 0)

    def drain(self):
        for m, name in self.sent:
            self.copy(m, name).wait_send()
        for b in (X, Y, Z0, Z1):
            if UNITS > self.heard[b]:
                pl.semaphore_wait(self.ready.at[b - 1], UNITS - self.heard[b])


def wire(rows):
    halves = [
        jnp.concatenate([rows[8 * k : 8 * k + 8, h * HALF : h * HALF + HALF] for k in range(3)], 1)
        for h in range(2)
    ]
    return jnp.concatenate(halves, 0).astype(bf)


def dot(left, right, left_axis, right_axis):
    return lax.dot_general(
        left,
        right,
        (((left_axis,), (right_axis,)), ((), ())),
        preferred_element_type=f32,
    )


def norm(rows):
    centered = rows - jnp.mean(rows, -1, keepdims=True)
    rstd = lax.rsqrt(jnp.mean(centered * centered, -1, keepdims=True) + norm_eps)
    return centered * rstd, rstd


def norm_back(grad, rhat, rstd):
    inner = jnp.mean(grad * rhat, -1, keepdims=True)
    return rstd * (grad - jnp.mean(grad, -1, keepdims=True) - rhat * inner)


def col_sum(rows):
    return jnp.sum(rows.astype(f32), 0, keepdims=True)


def gelu_parts(u):
    phi = 0.5 + 0.5 * lax.erf(u * 0.7071067811865476)
    return u * phi, phi, jnp.exp(-0.5 * u * u) * 0.3989422804014327


class Schedule:
    def __init__(self, engine, order, counts):
        self.engine, self.order, self.counts = engine, list(order), list(counts)

    def run(self, n):
        for _ in range(n):
            m, name = self.order.pop(0)
            self.engine.op(m, name)

    def before(self):
        self.run(self.counts.pop(0))

    def loop(self, n, body, needs=None):
        counts = [self.counts.pop(0) for _ in range(n)]

        @pl.loop(0, n)
        def _(i):
            for k in range(n):
                if counts[k] or needs:

                    @pl.when(i == k)
                    def _():
                        self.run(counts[k])
                        if needs:
                            needs(k)

            body(i)

    def rest(self):
        self.run(len(self.order))


def layer_kernel(
    sizes,
    lengths, counts, positions, vec_in, wq, wo, w1, w2, x_in, gv_in,
    layer_out, input_grad, g_qkv, g_out, g_up, g_down, g_vec,
    W, S, R, xs, J, ctx_t, act_g, slope_g, pick_t, pick, x_g, q_g, r1_g, n1_g, nl_g, d_two, d_one,
    f_grad, a_grad, c_grad, dq_g, ctx_gt, acc, n1_t, nl_t, out_t, gv, own_f, oth_f, vec_all, vec, vgrad,
    vsum, vland,
    g_send, g_recv, s_send, s_recv, ready, first, in_sem, out_sem, v_send, v_recv,
):
    place = Place(*sizes)
    c = place.c
    chip = (place.z1, place.z0, place.y, place.x)
    load_x = pltpu.make_async_copy(x_in, xs, in_sem.at[0])
    load_x.start()
    load_gv = pltpu.make_async_copy(gv_in, gv, in_sem.at[1])
    load_gv.start()
    G = Gather(place, W, g_send, g_recv)
    for u, src, at in (
        [(K_UNIT, wq, D), (V_UNIT, wq, 2 * D), (Q_UNIT, wq, 0), (OUT_UNIT, wo, 0)]
        + [(UP_UNIT + j, w1, D * j) for j in range(4)]
    ):
        own_f[u] = src[:, at : at + D].astype(f32)
    enter(place)
    other = pl.ds(pl.multiple_of(HALF * (1 - c), 128), HALF)
    pair = place.partner(CORE)
    halves = remote(own_f.at[:, :, other], oth_f, first.at[0], first.at[1], pair)
    halves.start()

    def vec_hop(b):
        at = [place.z1, place.z0, place.y, place.x, c]
        for done in vec_order[: vec_order.index(b)]:
            at[4 - done] = ALL
        part = vec_all.at[tuple(at)]
        return remote(part, part, v_send.at[b], v_recv.at[b], place.partner(b))

    vec_order = (CORE, X, Y, Z0, Z1)
    vec_all[tuple(chip) + (c,)] = vec_in[...]
    vec_hop(CORE).start()
    downs = []
    for j in range(2):
        at = (DOWN_UNIT + 2 * c + j,) + chip
        down = remote(w2.at[48 * j : 48 * j + 48, other], W.at[at + (ALL, other)], first.at[2 + 2 * j], first.at[3 + 2 * j], pair)
        down.start()
        downs.append(down)
        W[at + (ALL, G.cols)] = w2[48 * j : 48 * j + 48, G.cols]
    halves.wait_recv()
    for u in range(8):
        own, oth = own_f[u, :, G.cols], oth_f[u]
        low = jnp.where(c == 0, own, oth)
        high = jnp.where(c == 0, oth, own)
        W[(u,) + chip + (ALL, G.cols)] = jnp.concatenate([low, high], 0).astype(bf)
    for down in downs:
        down.wait_recv()
    plan = Schedule(G, parse(gather_order), gather_counts)
    for k in range(5):
        plan.before()
        vec_hop(vec_order[k]).wait_recv()
        if k < 4:
            vec_hop(vec_order[k + 1]).start()
    gathered = jnp.sum(vec_all[...].astype(f32).reshape(8, 4, 16, 128), 1)
    for r in range(72):
        vec[r // 6 : r // 6 + 1, 128 * (r % 6) : 128 * (r % 6) + 128] = gathered[r // 9, r % 9 : r % 9 + 1]

    def bias(i):
        return vec[pl.ds(i, 1), :]

    def unit(u):
        return W[u].reshape(D, D)

    def down_block(j):
        parts = [W[DOWN_UNIT + q, j // 2, j % 2, y, x] for y in range(2) for x in range(2) for q in range(4)]
        return jnp.concatenate(parts, 0)

    load_x.wait()
    load_gv.wait()
    for s in range(2):
        place_id = lax.broadcasted_iota(jnp.int32, (SEQ_LEN, PMAX), 0)
        slot_id = lax.broadcasted_iota(jnp.int32, (SEQ_LEN, PMAX), 1)
        match = (positions[s : s + 1, :] == place_id) & (slot_id < counts[s])
        hot = jnp.where(match, 1.0, 0.0)
        pick_t[s] = hot.astype(bf)
        pick[s] = hot.T.astype(bf)
        x_g[PMAX * s : PMAX * s + PMAX] = dot(pick[s], xs[SEQ_LEN * s : SEQ_LEN * s + SEQ_LEN], 1, 0).astype(bf)

    def project(i, u, b):
        def body(t):
            rows = pl.ds(pl.multiple_of(512 * t, 512), 512)
            y = dot(xs[rows, :], unit(u), 1, 0)
            J[i, rows, :] = (y if b is None else y + bias(b)).astype(bf)

        plan.before()
        G.arrive(u)
        plan.loop(2, body)

    project(1, K_UNIT, None)
    project(2, V_UNIT, 1)
    project(0, Q_UNIT, 0)

    lane_id = lax.broadcasted_iota(jnp.int32, (SEQ_LEN, 128), 1)
    key_id = lax.broadcasted_iota(jnp.int32, (SEQ_LEN, 128), 0)
    scale = bf(HD**-0.5)

    def pair_at(it):
        s, p = it // 6, it % 6
        rows = pl.ds(pl.multiple_of(s * SEQ_LEN, SEQ_LEN), SEQ_LEN)
        cols = pl.ds(pl.multiple_of(p * 128, 128), 128)
        mask = jnp.where(key_id < lengths[s], 0.0, masked_score).astype(bf)
        return s, rows, cols, mask

    def attend(it):
        s, rows, cols, mask = pair_at(it)
        q, k, v = J[0, rows, cols], J[1, rows, cols] * scale, J[2, rows, cols]
        v_t = v.T
        for h in range(2):
            mine = lane_id // HD == h
            scores = dot(jnp.where(mine, k, mask), jnp.where(mine, q, bf(1 / HD)), 1, 1)
            e = jnp.exp(scores - jnp.max(scores, 0, keepdims=True))
            total = jnp.sum(e, 0, keepdims=True)
            o = dot(v_t[HD * h : HD * h + HD], e.astype(bf), 1, 0) * (1.0 / total)
            at = pl.multiple_of((it % 6) * 128 + HD * h, HD)
            ctx_t[pl.ds(at, HD), rows] = o.astype(bf)

    plan.loop(12, attend)

    plan.before()
    G.arrive(OUT_UNIT)
    for s in range(2):
        rows = slice(SEQ_LEN * s, SEQ_LEN * s + SEQ_LEN)
        slots = slice(PMAX * s, PMAX * s + PMAX)
        ctx_gt[:, slots] = dot(ctx_t[:, rows], pick[s], 1, 1).astype(bf)
        q_g[slots, :] = dot(pick[s], J[0, rows, :], 1, 0).astype(bf)
    r1 = x_g[...].astype(f32) + (dot(ctx_gt[...], unit(OUT_UNIT), 0, 0) + bias(2))
    r1_g[...] = r1
    n1 = norm(r1)[0] * bias(3) + bias(4)
    n1_g[...] = n1
    nl_g[...] = n1.astype(bf)

    def up_listed(q):
        cols = pl.ds(pl.multiple_of(D * q, D), D)
        u = dot(nl_g[...], unit(UP_UNIT + q), 1, 0) + bias(5 + q)
        a, phi, density = gelu_parts(u)
        act_g[:, cols] = a.astype(bf)
        slope_g[:, cols] = (phi + u * density).astype(bf)

    plan.loop(4, up_listed, lambda q: G.arrive(UP_UNIT + q))
    plan.rest()
    for u in range(DOWN_UNIT, UNITS):
        G.arrive(u)

    acc[...] = n1_g[...] + bias(9)

    @pl.loop(0, 4)
    def _(q):
        cols = pl.ds(pl.multiple_of(D * q, D), D)
        acc[...] += dot(act_g[:, cols], down_block(q), 1, 0)

    rhat, rstd = norm(acc[...])
    used = [jnp.sum(pick[s].astype(f32), 1, keepdims=True) for s in range(2)]
    cot = jnp.where(jnp.concatenate(used, 0) > 0.5, gv[...].astype(f32), 0.0)
    vgrad[10:11, :] = col_sum(cot * rhat)
    vgrad[11:12, :] = col_sum(cot)
    two = norm_back(cot * bias(10), rhat, rstd)
    d_two[...] = two
    f_grad[...] = two.astype(bf)
    vgrad[9:10, :] = col_sum(f_grad[...])

    T = Scatter(place, S, R, s_send, s_recv, ready, parse(scatter_order))
    plan = Schedule(T, parse(scatter_order), scatter_counts)
    message = {u: m for m, u in enumerate(scatter_units)}

    def put(m, grad):
        for i in range(PARTS):
            S[m, i % 2, i // 16, i // 8 % 2, i // 4 % 2, i // 2 % 2] = wire(grad[ROWS * i : ROWS * i + ROWS])

    def ffn_back(q):
        cols = pl.ds(pl.multiple_of(D * q, D), D)
        fg = f_grad[...]
        pre = (dot(fg, down_block(q), 1, 1) * slope_g[:, cols].astype(f32)).astype(bf)
        vgrad[pl.ds(5 + q, 1), :] = col_sum(pre)
        put(message[UP_UNIT] + q, dot(nl_g[...], pre, 0, 0))
        d_two[...] += dot(pre, unit(UP_UNIT + q), 1, 1)
        down = dot(act_g[:, cols], fg, 0, 0)
        for i in range(8):
            for t in range(4):
                at = 96 * i + ROWS * t
                S[message[DOWN_UNIT] + t, i % 2, q // 2, q % 2, i // 4, i // 2 % 2] = wire(down[at : at + ROWS])

    plan.loop(4, ffn_back)
    plan.before()
    rhat, rstd = norm(r1_g[...])
    g = d_two[...]
    vgrad[3:4, :] = col_sum(g * rhat)
    vgrad[4:5, :] = col_sum(g)
    one = norm_back(g * bias(3), rhat, rstd)
    d_one[...] = one
    a_grad[...] = one.astype(bf)
    vgrad[2:3, :] = col_sum(a_grad[...])
    put(message[OUT_UNIT], dot(ctx_gt[...], a_grad[...], 1, 0))
    c_grad[...] = dot(a_grad[...], unit(OUT_UNIT), 1, 1).astype(bf)

    slot_lane = lax.broadcasted_iota(jnp.int32, (PMAX, 128), 1)

    def attend_back(it):
        s, rows, cols, mask = pair_at(it)
        slots = pl.ds(pl.multiple_of(s * PMAX, PMAX), PMAX)
        q, g = q_g[slots, cols], c_grad[slots, cols]
        k, v = J[1, rows, cols] * scale, J[2, rows, cols]
        none = jnp.zeros_like(q)
        both = lambda t: jnp.concatenate(
            [jnp.where(slot_lane < HD, t, none), jnp.where(slot_lane < HD, none, t)], 0
        )
        q2, g2 = both(q), both(g)
        ones = jnp.full((2 * PMAX, 128), 1 / 128, bf)
        scores = dot(jnp.concatenate([k, mask], 1), jnp.concatenate([q2, ones], 1), 1, 1)
        e = jnp.exp(scores - jnp.max(scores, 0, keepdims=True))
        probs = e * (1.0 / jnp.sum(e, 0, keepdims=True))
        d_probs = dot(v, g2, 1, 1)
        row_dot = jnp.sum(probs * d_probs, 0, keepdims=True)
        d_scores = (probs * (d_probs - row_dot)).astype(bf)
        dv = dot(probs.astype(bf), g2, 1, 0)
        dk = dot(d_scores, q2 * scale, 1, 0)
        dq2 = dot(d_scores, k, 0, 0)
        dq = jnp.where(slot_lane < HD, dq2[:PMAX], dq2[PMAX:])
        dq_g[slots, cols] = dq.astype(bf)
        J[1, rows, cols] = dk.astype(bf)
        J[2, rows, cols] = dv.astype(bf)

    plan.loop(12, attend_back)
    plan.before()
    put(message[V_UNIT], dot(xs[...], J[2], 0, 0))
    vgrad[1:2, :] = col_sum(J[2])
    plan.before()
    put(message[K_UNIT], dot(xs[...], J[1], 0, 0))
    plan.before()
    put(message[Q_UNIT], dot(x_g[...], dq_g[...], 0, 0))
    vgrad[0:1, :] = col_sum(dq_g[...])

    for r in range(72):
        vsum[r // 36, r // 18 % 2, r // 9 % 2, r % 9 : r % 9 + 1] = vgrad[r // 6 : r // 6 + 1, 128 * (r % 6) : 128 * (r % 6) + 128]
    y, z0, z1 = place.y, place.z0, place.z1
    hops = [
        (CORE, (ALL, ALL, ALL), (ALL, ALL, ALL)),
        (X, (ALL, ALL, ALL), (ALL, ALL, ALL)),
        (Y, (ALL, ALL, 1 - y), (ALL, ALL, y)),
        (Z0, (ALL, 1 - z0, y), (ALL, z0, y)),
        (Z1, (1 - z1, z0, y), (z1, z0, y)),
    ]

    def hop(k):
        b, out, _ = hops[k]
        return remote(vsum.at[out], vland.at[(k,) + out], v_send.at[5 + k], v_recv.at[5 + k], place.partner(b))

    def take(k):
        copy = hop(k)
        copy.wait_send()
        copy.wait_recv()
        own = hops[k][2]
        vsum[own] = vsum[own] + vland[(k,) + own]

    for k in range(5):
        plan.before()
        if k > 0:
            take(k - 1)
        hop(k).start()

    def ffn_all(it):
        t, q = it // 4, it % 4
        rows = pl.ds(pl.multiple_of(256 * t, 256), 256)

        @pl.when(q == 0)
        def _():
            r = xs[rows, :].astype(f32) + (dot(ctx_t[:, rows], unit(OUT_UNIT), 0, 0) + bias(2))
            n = norm(r)[0] * bias(3) + bias(4)
            n1_t[...] = n
            nl_t[...] = n.astype(bf)
            acc[...] = n + bias(9)

        a = gelu_parts(dot(nl_t[...], unit(UP_UNIT + q), 1, 0) + bias(5 + q))[0]
        acc[...] += dot(a.astype(bf), down_block(q), 1, 0)

        @pl.when(q == 3)
        def _():
            done = pltpu.make_async_copy(out_t, layer_out.at[rows, :], out_sem.at[0])

            @pl.when(t > 0)
            def _():
                done.wait()

            out_t[...] = (norm(acc[...])[0] * bias(10) + bias(11)).astype(bf)
            done.start()

    plan.loop(16, ffn_all)
    take(4)
    g_vec[...] = vsum[z1, z0, y]

    def grad_in(s):
        rows = pl.ds(pl.multiple_of(s * SEQ_LEN, SEQ_LEN), SEQ_LEN)
        slots = pl.ds(pl.multiple_of(s * PMAX, PMAX), PMAX)
        t = d_one[slots, :] + dot(dq_g[slots, :], unit(Q_UNIT), 1, 1)
        high = t.astype(bf)
        low = (t - high.astype(f32)).astype(bf)
        total = dot(pick_t[s], high, 1, 0) + dot(pick_t[s], low, 1, 0)
        total += dot(J[1, rows, :], unit(K_UNIT), 1, 1)
        total += dot(J[2, rows, :], unit(V_UNIT), 1, 1)
        J[0, rows, :] = total.astype(bf)

    plan.loop(2, grad_in)
    store = pltpu.make_async_copy(J.at[0], input_grad, out_sem.at[1])
    store.start()
    plan.rest()
    for m, u in enumerate(scatter_units):
        grad = T.last(m)
        if u in (K_UNIT, V_UNIT, Q_UNIT):
            at = D * ((u + 1) % 3)
            g_qkv[:, at : at + D] = grad
        elif u == OUT_UNIT:
            g_out[...] = grad
        elif u < DOWN_UNIT:
            at = D * (u - UP_UNIT)
            g_up[:, at : at + D] = grad
        else:
            at = ROWS * (u - DOWN_UNIT)
            g_down[at : at + ROWS, :] = grad
    pltpu.make_async_copy(out_t, layer_out.at[0:256, :], out_sem.at[0]).wait()
    store.wait()
    halves.wait_send()
    for down in downs:
        down.wait_send()
    for b in vec_order:
        vec_hop(b).wait_send()
    G.drain()
    T.drain()


def layer_call(sizes, *args):
    vmem = pl.BlockSpec(memory_space=pltpu.VMEM)
    smem = pl.BlockSpec(memory_space=pltpu.SMEM)
    hbm = pl.BlockSpec(memory_space=pl.ANY)
    tokens = 2 * SEQ_LEN
    slots = 2 * PMAX
    dma = pltpu.SemaphoreType.DMA
    return pl.pallas_call(
        partial(layer_kernel, sizes),
        out_shape=(
            jax.ShapeDtypeStruct((tokens, D), bf),
            jax.ShapeDtypeStruct((tokens, D), bf),
            jax.ShapeDtypeStruct((ROWS, 3 * D), f32),
            jax.ShapeDtypeStruct((ROWS, D), f32),
            jax.ShapeDtypeStruct((ROWS, FF), f32),
            jax.ShapeDtypeStruct((FF // PARTS, D), f32),
            jax.ShapeDtypeStruct((16, 128), f32),
        ),
        in_specs=[smem, smem] + [vmem] * 6 + [hbm] * 2,
        out_specs=(hbm,) * 2 + (vmem,) * 5,
        scratch_shapes=[
            pltpu.VMEM((UNITS, 2, 2, 2, 2, 2 * ROWS, D), bf),
            pltpu.VMEM((UNITS, 2, 2, 2, 2, 2, 16, WIRE), bf),
            pltpu.VMEM((UNITS, 2, 2, 2, 2, 16, WIRE), bf),
            pltpu.VMEM((tokens, D), bf),
            pltpu.VMEM((3, tokens, D), bf),
            pltpu.VMEM((D, tokens), bf),
            pltpu.VMEM((slots, FF), bf),
            pltpu.VMEM((slots, FF), bf),
            pltpu.VMEM((2, SEQ_LEN, PMAX), bf),
            pltpu.VMEM((2, PMAX, SEQ_LEN), bf),
            pltpu.VMEM((slots, D), bf),
            pltpu.VMEM((slots, D), bf),
            pltpu.VMEM((slots, D), f32),
            pltpu.VMEM((slots, D), f32),
            pltpu.VMEM((slots, D), bf),
            pltpu.VMEM((slots, D), f32),
            pltpu.VMEM((slots, D), f32),
            pltpu.VMEM((slots, D), bf),
            pltpu.VMEM((slots, D), bf),
            pltpu.VMEM((slots, D), bf),
            pltpu.VMEM((slots, D), bf),
            pltpu.VMEM((D, slots), bf),
            pltpu.VMEM((256, D), f32),
            pltpu.VMEM((256, D), f32),
            pltpu.VMEM((256, D), bf),
            pltpu.VMEM((256, D), bf),
            pltpu.VMEM((slots, D), bf),
            pltpu.VMEM((8, ROWS, D), f32),
            pltpu.VMEM((8, ROWS, HALF), f32),
            pltpu.VMEM((2, 2, 2, 2, 2, 16, 128), bf),
            pltpu.VMEM((16, D), f32),
            pltpu.VMEM((16, D), f32),
            pltpu.VMEM((2, 2, 2, 16, 128), f32),
            pltpu.VMEM((5, 2, 2, 2, 16, 128), f32),
            dma((UNITS, 7)),
            dma((UNITS, 7)),
            dma((UNITS, 7)),
            dma((UNITS, 7)),
            pltpu.SemaphoreType.REGULAR((4,)),
            dma((6,)),
            dma((2,)),
            dma((2,)),
            dma((10,)),
            dma((10,)),
        ],
        compiler_params=pltpu.CompilerParams(
            collective_id=0, has_side_effects=True, vmem_limit_bytes=63 * 2**20
        ),
    )(*args)


def sub_groups(sizes):
    sub = sizes[0] * sizes[1] // PARTS
    return [[sub * i + j for j in range(sub)] for i in range(PARTS)]


def whole_group(sizes, flat):
    if sizes[0] * sizes[1] == PARTS:
        return flat
    return lax.all_gather(flat, ("dp", "inner"), axis_index_groups=sub_groups(sizes), tiled=True)


def own_part(sizes, flat):
    if sizes[0] * sizes[1] == PARTS:
        return flat
    return lax.psum_scatter(
        flat, ("dp", "inner"), axis_index_groups=sub_groups(sizes), scatter_dimension=0, tiled=True
    )


def on_device(
    sizes,
    inputs,
    qkv_weight,
    out_weight,
    up_weight,
    down_weight,
    vectors,
    lengths,
    counts,
    positions,
    grad_values,
):
    wq, wo, w1, w2, vec = [
        whole_group(sizes, w) for w in (qkv_weight, out_weight, up_weight, down_weight, vectors)
    ]
    number = lax.axis_index("dp") * sizes[1] + lax.axis_index("inner")
    quarter = number // (sizes[0] * sizes[1] // PARTS) % 4
    size = vec.shape[0]
    frame = jnp.where(jnp.arange(4 * size) // size == quarter, jnp.tile(vec, 4), bf(0))
    frame = jnp.pad(frame, (0, 16 * 128 - 4 * size)).reshape(16, 128)
    layer_out, input_grad, g_qkv, g_out, g_up, g_down, g_vec = layer_call(
        sizes,
        lengths,
        counts,
        positions,
        frame,
        wq.reshape(ROWS, 3 * D),
        wo.reshape(ROWS, D),
        w1.reshape(ROWS, FF),
        w2.reshape(FF // PARTS, D),
        inputs,
        grad_values.reshape(-1, D),
    )
    g_vec = lax.dynamic_slice(g_vec.reshape(-1), (quarter * size,), (size,))
    flat = [own_part(sizes, g.reshape(-1)) for g in (g_qkv, g_out, g_up, g_down, g_vec)]
    return (layer_out, input_grad, *flat)


def solution(mesh):
    both = ("dp", "inner")
    rows, flat = P(both, None), P(both)
    return jax.shard_map(
        partial(on_device, (mesh.shape["dp"], mesh.shape["inner"])),
        mesh=mesh,
        in_specs=(rows, flat, flat, flat, flat, flat, flat, flat, rows, P(both, None, None)),
        out_specs=(rows, rows, flat, flat, flat, flat, flat),
        check_vma=False,
    )
```

```python
from functools import partial

import jax
import jax.numpy as jnp
from jax import lax
from jax.experimental import pallas as pl
from jax.experimental.pallas import tpu as pltpu
from jax.sharding import PartitionSpec as P

D = 768
H = 12
HD = 64
FF = 3072
SEQ_LEN = 512
PMAX = 128
norm_eps = 1e-05
masked_score = -1e30

bf = jnp.bfloat16
f32 = jnp.float32
MESH = pl.DeviceIdType.MESH
PARTS = 32
ROWS = D // PARTS
UNITS = 12
K_UNIT, V_UNIT, Q_UNIT, OUT_UNIT, UP_UNIT, DOWN_UNIT = 0, 1, 2, 3, 4, 8
CORE, X, Y, Z0, Z1 = range(5)
ALL = slice(None)
HALF = D // 2
WIRE = 3 * HALF

gather_types = (
    "ab", "ab", "ab", "e", "f", "ab", "e", "f", "ab", "e", "f", "ab",
)
gather_order = (
    "0z1", "2z1", "1z1", "3s0", "12v0", "7s0", "11z1", "9s0", "0z0", "10s0", "4s0", "12v1", "6s0",
    "2z0", "1z0", "5z1", "0B1", "0A1", "11z0", "12v2", "2B1", "2A1", "8z1", "1B1", "1A1", "0B2",
    "5z0", "10z1", "12v3", "0A2", "8z0", "4z1", "5B1", "11A1", "12v4", "2B2", "5A1", "2A2", "3z1",
    "9z1", "1A2", "8B1", "0C", "1B2", "6z1", "8A1", "5B2", "4z0", "11B1", "11A2", "3z0", "12v5",
    "1C", "2C", "10z0", "7z1", "5A2", "4s3", "11B2", "6z0", "3s3", "11C", "7z0", "9z0", "10s3",
    "6s3", "7s3", "9s3", "5C", "3C", "4C", "8A2", "6C", "8B2", "7C", "9C", "10C", "8C",
)
gather_counts = (
    0, 1, 4, 0, 34, 9, 3, 0, 8, 1, 0, 0, 0, 0, 1, 0, 0, 3, 0, 2, 0, 0, 1, 1, 3, 2, 0, 1, 2, 0, 2,
    0,
)
scatter_units = (4, 5, 6, 7, 8, 9, 10, 11, 3, 1, 0, 2)
scatter_types = (
    "f", "e", "ab", "f", "e", "ab", "f", "e", "ab", "f", "e", "ab",
)
scatter_order = (
    "0C", "1C", "0s3", "3C", "6C", "1s3", "7C", "4C", "8C", "3s3", "4s3", "0z0", "2C", "5C", "6s3",
    "1z0", "7s3", "0z1", "2A2", "3z0", "1z1", "2B2", "12v0", "9C", "10C", "6z0", "0s0", "8B2",
    "4z0", "9s3", "10s3", "11C", "2A1", "8A2", "5A2", "7z0", "11A2", "2B1", "5B2", "4z1", "6z1",
    "9z0", "12v1", "8B1", "7z1", "11B2", "10z0", "8A1", "5A1", "1s0", "9z1", "11A1", "3z1", "5B1",
    "11B1", "2z0", "10z1", "8z0", "4s0", "5z0", "6s0", "12v2", "9s0", "11z0", "7s0", "8z1", "12v3",
    "2z1", "4L", "5z1", "3s0", "10s0", "11z1", "12v4", "1L", "8L", "2L", "10L", "3L", "7L", "6L",
    "5L", "12v5", "9L", "11L", "0L",
)
scatter_counts = (
    0, 1, 1, 0, 4, 1, 1, 0, 2, 0, 0, 2, 1, 1, 2, 0, 2, 0, 2, 1, 4, 3, 6, 2, 0, 4, 3, 3, 3, 0, 2, 6,
    2, 0, 6, 2, 7, 2,
)


def parse(order):
    digits = [2 if o[1].isdigit() else 1 for o in order]
    return [(int(o[:d]), o[d:]) for o, d in zip(order, digits)]


class Place:
    def __init__(self, dp_size, inner_size):
        self.sub_size = dp_size * inner_size // PARTS
        self.inner_size = inner_size
        number = lax.axis_index("dp") * inner_size + lax.axis_index("inner")
        self.sub = number % self.sub_size
        self.group = number // self.sub_size
        self.bits = [(self.group // 2**b) % 2 for b in range(5)]
        self.c, self.x, self.y, self.z0, self.z1 = self.bits

    def partner(self, b):
        group = self.group + 2**b - 2 * 2**b * self.bits[b]
        number = group * self.sub_size + self.sub
        return (number // self.inner_size, number % self.inner_size)


def remote(src, dst, send_sem, recv_sem, device):
    return pltpu.make_async_remote_copy(
        src_ref=src,
        dst_ref=dst,
        send_sem=send_sem,
        recv_sem=recv_sem,
        device_id=device,
        device_id_type=MESH,
    )


def enter(place):
    barrier = pltpu.get_barrier_semaphore()
    for b in range(5):
        pl.semaphore_signal(barrier, inc=1, device_id=place.partner(b), device_id_type=MESH)
    pl.semaphore_wait(barrier, 5)


class Gather:
    def __init__(self, place, W, send, recv):
        self.place, self.W, self.send, self.recv = place, W, send, recv
        self.cols = pl.ds(pl.multiple_of(HALF * place.c, 128), HALF)
        x, y, z0, z1 = place.x, place.y, place.z0, place.z1
        every = (ALL, ALL, ALL, ALL)
        self.legs = {
            "ab": [
                ("z1", (), Z1, (z1, z0, y, x)),
                ("z0", ("z1",), Z0, (ALL, z0, y, x)),
                ("A1", ("z0",), Y, (0, ALL, y, x)),
                ("B1", ("z0",), X, (1, ALL, y, x)),
                ("A2", ("A1",), X, (0, ALL, ALL, x)),
                ("B2", ("B1",), Y, (1, ALL, y, ALL)),
                ("C", ("A2", "B2"), CORE, every),
            ],
            "e": [
                ("s0", (), X, (z1, z0, y, x)),
                ("z1", ("s0",), Z1, (z1, z0, y, ALL)),
                ("z0", ("z1",), Z0, (ALL, z0, y, ALL)),
                ("s3", ("z0",), Y, (ALL, ALL, y, ALL)),
                ("C", ("s3",), CORE, every),
            ],
            "f": [
                ("s0", (), Y, (z1, z0, y, x)),
                ("z1", ("s0",), Z1, (z1, z0, ALL, x)),
                ("z0", ("z1",), Z0, (ALL, z0, ALL, x)),
                ("s3", ("z0",), X, (ALL, ALL, ALL, x)),
                ("C", ("s3",), CORE, every),
            ],
        }
        self.got, self.sent = set(), []

    def copy(self, m, name):
        legs = self.legs[gather_types[m]]
        k = [leg[0] for leg in legs].index(name)
        _, after, b, index = legs[k]
        part = self.W.at[(m,) + index + (ALL, self.cols)]
        sems = self.send.at[m, k], self.recv.at[m, k]
        return remote(part, part, *sems, self.place.partner(b)), after

    def arrive(self, m, name="C"):
        if (m, name) not in self.got:
            self.got.add((m, name))
            self.copy(m, name)[0].wait_recv()

    def op(self, m, name):
        copy, after = self.copy(m, name)
        for a in after:
            self.arrive(m, a)
        copy.start()
        self.sent.append((m, name))

    def drain(self):
        for m, name in self.sent:
            self.copy(m, name)[0].wait_send()


class Scatter:
    def __init__(self, place, S, R, send, recv, ready, order, store):
        self.place, self.S, self.R, self.store = place, S, R, store
        self.send, self.recv, self.ready = send, recv, ready
        x, y, z0, z1 = place.x, place.y, place.z0, place.z1
        self.legs = {
            "ab": [
                ("A2", ("C",), X, (0, ALL, ALL, 1 - x), (0, ALL, ALL, 1 - x), (0, ALL, ALL, x), (0, ALL, ALL, x)),
                ("B2", ("C",), Y, (1, ALL, 1 - y, ALL), (1, ALL, 1 - y, ALL), (1, ALL, y, ALL), (1, ALL, y, ALL)),
                ("A1", ("A2",), Y, (0, ALL, 1 - y, x), (0, ALL, 1 - y, 1 - x), (0, ALL, y, x), (0, ALL, y, 1 - x)),
                ("B1", ("B2",), X, (1, ALL, y, 1 - x), (1, ALL, 1 - y, 1 - x), (1, ALL, y, x), (1, ALL, 1 - y, x)),
                ("z0", ("A1", "B1"), Z0, (ALL, 1 - z0, y, x), (ALL, 1 - z0, 1 - y, 1 - x), (ALL, z0, y, x), (ALL, z0, 1 - y, 1 - x)),
                ("z1", ("z0",), Z1, (1 - z1, z0, y, x), (1 - z1, 1 - z0, 1 - y, 1 - x), (z1, z0, y, x), (z1, 1 - z0, 1 - y, 1 - x)),
            ],
            "e": [
                ("s3", ("C",), Y, (ALL, ALL, 1 - y, ALL), (ALL, ALL, 1 - y, ALL), (ALL, ALL, y, ALL), (ALL, ALL, y, ALL)),
                ("z0", ("s3",), Z0, (ALL, 1 - z0, y, ALL), (ALL, 1 - z0, 1 - y, ALL), (ALL, z0, y, ALL), (ALL, z0, 1 - y, ALL)),
                ("z1", ("z0",), Z1, (1 - z1, z0, y, ALL), (1 - z1, 1 - z0, 1 - y, ALL), (z1, z0, y, ALL), (z1, 1 - z0, 1 - y, ALL)),
                ("s0", ("z1",), X, (z1, z0, y, 1 - x), (1 - z1, 1 - z0, 1 - y, 1 - x), (z1, z0, y, x), (1 - z1, 1 - z0, 1 - y, x)),
            ],
            "f": [
                ("s3", ("C",), X, (ALL, ALL, ALL, 1 - x), (ALL, ALL, ALL, 1 - x), (ALL, ALL, ALL, x), (ALL, ALL, ALL, x)),
                ("z0", ("s3",), Z0, (ALL, 1 - z0, ALL, x), (ALL, 1 - z0, ALL, 1 - x), (ALL, z0, ALL, x), (ALL, z0, ALL, 1 - x)),
                ("z1", ("z0",), Z1, (1 - z1, z0, ALL, x), (1 - z1, 1 - z0, ALL, 1 - x), (z1, z0, ALL, x), (z1, 1 - z0, ALL, 1 - x)),
                ("s0", ("z1",), Y, (z1, z0, 1 - y, x), (1 - z1, 1 - z0, 1 - y, 1 - x), (z1, z0, y, x), (1 - z1, 1 - z0, y, 1 - x)),
            ],
        }
        self.got, self.sent = set(), []
        self.turn = {}
        for m, name in order:
            if m < UNITS and "C" in self.leg(m, name)[1] and m not in self.turn:
                self.turn[m] = len(self.turn)
        self.heard = {b: 0 for b in (X, Y, Z0, Z1)}

    def leg(self, m, name):
        if name in "CL":
            return (name, (), CORE)
        return [leg for leg in self.legs[scatter_types[m]] if leg[0] == name][0]

    def copy(self, m, name):
        c = self.place.c
        if name == "C":
            sems = self.send.at[m, 0], self.recv.at[m, 0]
            return remote(self.S.at[m, 1 - c], self.R.at[m], *sems, self.place.partner(CORE))
        k = [leg[0] for leg in self.legs[scatter_types[m]]].index(name) + 1
        _, _, b, out, land, _, _ = self.leg(m, name)
        sems = self.send.at[m, k], self.recv.at[m, k]
        return remote(
            self.S.at[(m, c) + out], self.S.at[(m, 1 - c) + land], *sems, self.place.partner(b)
        )

    def add(self, m, name):
        if (m, name) in self.got:
            return
        self.got.add((m, name))
        c = self.place.c
        copy = self.copy(m, name)
        if name == "C":
            copy.wait_send()
            self.sent.remove((m, name))
            for b in (X, Y, Z0, Z1):
                pl.semaphore_signal(
                    self.ready.at[b - 1],
                    inc=1,
                    device_id=self.place.partner(b),
                    device_id_type=MESH,
                )
            copy.wait_recv()
            self.S[m, c] = self.S[m, c] + self.R[m]
            return
        copy.wait_recv()
        own, landed = self.leg(m, name)[5:]
        self.S[(m, c) + own] = self.S[(m, c) + own] + self.S[(m, 1 - c) + landed]

    def op(self, m, name):
        after, b = self.leg(m, name)[1:3]
        for a in after:
            self.add(m, a)
        if b != CORE:
            need = self.turn[m] + 1 - self.heard[b]
            if need > 0:
                pl.semaphore_wait(self.ready.at[b - 1], need)
                self.heard[b] += need
        self.copy(m, name).start()
        self.sent.append((m, name))

    def finish(self, m):
        name = self.legs[scatter_types[m]][-1][0]
        self.copy(m, name).wait_recv()
        c = self.place.c
        own, landed = self.leg(m, name)[5:]
        total = self.S[(m, c) + own].astype(f32) + self.S[(m, 1 - c) + landed].astype(f32)
        left, right = total[:8], total[8:]
        rows = [
            jnp.concatenate([v[:, HALF * k : HALF * k + HALF] for v in (left, right)], 1)
            for k in range(3)
        ]
        self.store(m, jnp.concatenate(rows, 0))

    def drain(self):
        for m, name in self.sent:
            self.copy(m, name).wait_send()
        for b in (X, Y, Z0, Z1):
            if UNITS > self.heard[b]:
                pl.semaphore_wait(self.ready.at[b - 1], UNITS - self.heard[b])


def wire(rows):
    halves = [
        jnp.concatenate([rows[8 * k : 8 * k + 8, h * HALF : h * HALF + HALF] for k in range(3)], 1)
        for h in range(2)
    ]
    return jnp.concatenate(halves, 0).astype(bf)


def dot(left, right, left_axis, right_axis):
    return lax.dot_general(
        left,
        right,
        (((left_axis,), (right_axis,)), ((), ())),
        preferred_element_type=f32,
    )


def norm(rows):
    centered = rows - jnp.mean(rows, -1, keepdims=True)
    rstd = lax.rsqrt(jnp.mean(centered * centered, -1, keepdims=True) + norm_eps)
    return centered * rstd, rstd


def norm_back(grad, rhat, rstd):
    inner = jnp.mean(grad * rhat, -1, keepdims=True)
    return rstd * (grad - jnp.mean(grad, -1, keepdims=True) - rhat * inner)


def col_sum(rows):
    return jnp.sum(rows.astype(f32), 0, keepdims=True)


def gelu_parts(u):
    phi = 0.5 + 0.5 * lax.erf(u * 0.7071067811865476)
    return u * phi, phi, jnp.exp(-0.5 * u * u) * 0.3989422804014327


class Chain:
    def __init__(self, hop, arrived, size):
        self.hop, self.arrived, self.size = hop, arrived, size

    def op(self, k):
        if k > 0:
            self.arrived(k - 1)
        if k < self.size:
            self.hop(k).start()


class Schedule:
    def __init__(self, engine, chain, order, counts):
        self.engine, self.chain, self.order, self.counts = engine, chain, list(order), list(counts)

    def run(self, n):
        for _ in range(n):
            m, name = self.order.pop(0)
            if m == UNITS:
                self.chain.op(int(name[1:]))
            elif name == "L":
                self.engine.finish(m)
            else:
                self.engine.op(m, name)

    def before(self):
        self.run(self.counts.pop(0))

    def loop(self, n, body, needs=None):
        counts = [self.counts.pop(0) for _ in range(n)]

        @pl.loop(0, n)
        def _(i):
            for k in range(n):
                if counts[k] or needs:

                    @pl.when(i == k)
                    def _():
                        self.run(counts[k])
                        if needs:
                            needs(k)

            body(i)

    def rest(self):
        self.run(len(self.order))


def layer_kernel(
    sizes,
    lengths, counts, positions, vec_in, wq, wo, w1, w2, x_in, gv_in,
    layer_out, input_grad, g_qkv, g_out, g_up, g_down, g_vec,
    W, S, R, xs, J, ctx_t, act_g, slope_g, pick_t, pick, x_g, q_g, r1_g, n1_g, nl_g, d_two, d_one,
    f_grad, a_grad, c_grad, dq_g, ctx_gt, acc, n1_t, nl_t, out_t, gv, raw, wide, vec_all, vec, vgrad,
    vsum, vland,
    g_send, g_recv, s_send, s_recv, ready, first, in_sem, out_sem, v_send, v_recv,
):
    place = Place(*sizes)
    c, x, y, z0, z1 = place.bits
    chip = (z1, z0, y, x)
    load_x = pltpu.make_async_copy(x_in, xs, in_sem.at[0])
    load_gv = pltpu.make_async_copy(gv_in, gv, in_sem.at[1])
    weights = ((wq, 0), (wo, 432), (w1, 576), (w2, 1152))
    own = [
        pltpu.make_async_copy(w, raw.at[c, at : at + w.shape[0]], in_sem.at[2 + i])
        for i, (w, at) in enumerate(weights)
    ]
    pair = [
        remote(w, raw.at[c, at : at + w.shape[0]], first.at[2 * i], first.at[2 * i + 1], place.partner(CORE))
        for i, (w, at) in enumerate(weights)
    ]
    for copy in own:
        copy.start()
    load_x.start()
    load_gv.start()
    enter(place)
    G = Gather(place, W, g_send, g_recv)

    vec_order = (CORE, X, Y, Z0, Z1)

    def vec_hop(k):
        at = [z1, z0, y, x, c]
        for done in vec_order[:k]:
            at[4 - done] = ALL
        part = vec_all.at[tuple(at)]
        return remote(part, part, v_send.at[k], v_recv.at[k], place.partner(vec_order[k]))

    pair[0].start()
    vec_all[chip + (c,)] = vec_in[...]
    for copy in pair[1:]:
        copy.start()
    chain = Chain(vec_hop, lambda k: vec_hop(k).wait_recv(), 5)
    plan = Schedule(G, chain, parse(gather_order), gather_counts)

    def lay(u, at, stride, n):
        for j in range(3):
            col = 3 * c + j
            if u < DOWN_UNIT:
                rows = [wide[i, pl.ds(at + col, n, stride=stride), :] for i in range(2)]
                block = jnp.concatenate(rows, 0)
            else:
                block = wide[(u - DOWN_UNIT) // 2, pl.ds(at + col, n, stride=stride), :]
            W[(u,) + chip + (ALL, pl.ds(pl.multiple_of(128 * col, 128), 128))] = block.astype(bf)

    parts = (
        [(K_UNIT, 6, 18, ROWS), (V_UNIT, 12, 18, ROWS), (Q_UNIT, 0, 18, ROWS)],
        [(OUT_UNIT, 432, 6, ROWS)],
        [(UP_UNIT + j, 576 + 6 * j, 24, ROWS) for j in range(4)],
        [(DOWN_UNIT + q, 1152 + 6 * 48 * (q % 2), 6, 48) for q in range(4)],
    )
    for i, (w, at) in enumerate(weights):
        plan.before()
        own[i].wait()
        pair[i].wait_recv()
        rows = slice(at, at + w.shape[0])
        wide[:, rows] = raw[:, rows].astype(f32)
        for part in parts[i]:
            lay(*part)

    def bias(i):
        return vec[pl.ds(i, 1), :]

    def unit(u):
        return W[u].reshape(D, D)

    def down_block(j):
        parts = [W[DOWN_UNIT + q, j // 2, j % 2, y, x] for y in range(2) for x in range(2) for q in range(4)]
        return jnp.concatenate(parts, 0)

    plan.before()
    load_x.wait()
    load_gv.wait()
    for s in range(2):
        place_id = lax.broadcasted_iota(jnp.int32, (SEQ_LEN, PMAX), 0)
        slot_id = lax.broadcasted_iota(jnp.int32, (SEQ_LEN, PMAX), 1)
        match = (positions[s : s + 1, :] == place_id) & (slot_id < counts[s])
        hot = jnp.where(match, 1.0, 0.0)
        pick_t[s] = hot.astype(bf)
        pick[s] = hot.T.astype(bf)
        x_g[PMAX * s : PMAX * s + PMAX] = dot(pick[s], xs[SEQ_LEN * s : SEQ_LEN * s + SEQ_LEN], 1, 0).astype(bf)

    def project(i, u, b):
        def body(t):
            rows = pl.ds(pl.multiple_of(512 * t, 512), 512)
            y = dot(xs[rows, :], unit(u), 1, 0)
            J[i, rows, :] = (y if b is None else y + bias(b)).astype(bf)

        plan.before()
        G.arrive(u)
        plan.loop(2, body)

    project(1, K_UNIT, None)
    plan.before()
    gathered = jnp.sum(vec_all[...].astype(f32).reshape(8, 4, 16, 128), 1)
    for r in range(72):
        vec[r // 6 : r // 6 + 1, 128 * (r % 6) : 128 * (r % 6) + 128] = gathered[r // 9, r % 9 : r % 9 + 1]
    project(2, V_UNIT, 1)
    project(0, Q_UNIT, 0)

    lane_id = lax.broadcasted_iota(jnp.int32, (SEQ_LEN, 128), 1)
    key_id = lax.broadcasted_iota(jnp.int32, (SEQ_LEN, 128), 0)
    scale = bf(HD**-0.5)

    def pair_at(it):
        s, p = it // 6, it % 6
        rows = pl.ds(pl.multiple_of(s * SEQ_LEN, SEQ_LEN), SEQ_LEN)
        cols = pl.ds(pl.multiple_of(p * 128, 128), 128)
        mask = jnp.where(key_id < lengths[s], 0.0, masked_score).astype(bf)
        return s, rows, cols, mask

    def attend(it):
        s, rows, cols, mask = pair_at(it)
        q, k, v = J[0, rows, cols], J[1, rows, cols] * scale, J[2, rows, cols]
        v_t = v.T
        for h in range(2):
            mine = lane_id // HD == h
            scores = dot(jnp.where(mine, k, mask), jnp.where(mine, q, bf(1 / HD)), 1, 1)
            e = jnp.exp(scores - jnp.max(scores, 0, keepdims=True))
            total = jnp.sum(e, 0, keepdims=True)
            o = dot(v_t[HD * h : HD * h + HD], e.astype(bf), 1, 0) * (1.0 / total)
            at = pl.multiple_of((it % 6) * 128 + HD * h, HD)
            ctx_t[pl.ds(at, HD), rows] = o.astype(bf)

    plan.loop(12, attend)

    plan.before()
    G.arrive(OUT_UNIT)
    for s in range(2):
        rows = slice(SEQ_LEN * s, SEQ_LEN * s + SEQ_LEN)
        slots = slice(PMAX * s, PMAX * s + PMAX)
        ctx_gt[:, slots] = dot(ctx_t[:, rows], pick[s], 1, 1).astype(bf)
        q_g[slots, :] = dot(pick[s], J[0, rows, :], 1, 0).astype(bf)
    r1 = x_g[...].astype(f32) + (dot(ctx_gt[...], unit(OUT_UNIT), 0, 0) + bias(2))
    r1_g[...] = r1
    n1 = norm(r1)[0] * bias(3) + bias(4)
    n1_g[...] = n1
    nl_g[...] = n1.astype(bf)

    def up_listed(q):
        cols = pl.ds(pl.multiple_of(D * q, D), D)
        u = dot(nl_g[...], unit(UP_UNIT + q), 1, 0) + bias(5 + q)
        a, phi, density = gelu_parts(u)
        act_g[:, cols] = a.astype(bf)
        slope_g[:, cols] = (phi + u * density).astype(bf)

    plan.loop(4, up_listed, lambda q: G.arrive(UP_UNIT + q))
    plan.rest()
    for u in range(DOWN_UNIT, UNITS):
        G.arrive(u)

    acc[...] = n1_g[...] + bias(9)

    @pl.loop(0, 4)
    def _(q):
        cols = pl.ds(pl.multiple_of(D * q, D), D)
        acc[...] += dot(act_g[:, cols], down_block(q), 1, 0)

    rhat, rstd = norm(acc[...])
    used = [jnp.sum(pick[s].astype(f32), 1, keepdims=True) for s in range(2)]
    cot = jnp.where(jnp.concatenate(used, 0) > 0.5, gv[...].astype(f32), 0.0)
    vgrad[10:11, :] = col_sum(cot * rhat)
    vgrad[11:12, :] = col_sum(cot)
    two = norm_back(cot * bias(10), rhat, rstd)
    d_two[...] = two
    f_grad[...] = two.astype(bf)
    vgrad[9:10, :] = col_sum(f_grad[...])

    def store_unit(m, grad):
        u = scatter_units[m]
        if u in (K_UNIT, V_UNIT, Q_UNIT):
            out, stride, at = g_qkv, 18, 6 * ((u + 1) % 3)
        elif u == OUT_UNIT:
            out, stride, at = g_out, 6, 0
        elif u < DOWN_UNIT:
            out, stride, at = g_up, 24, 6 * (u - UP_UNIT)
        else:
            out, stride, at = g_down, 6, 6 * ROWS * (u - DOWN_UNIT)
        for j in range(6):
            out[pl.ds(at + j, ROWS, stride=stride), :] = grad[:, 128 * j : 128 * j + 128]

    hops = [
        (CORE, (ALL, ALL, ALL), (ALL, ALL, ALL)),
        (X, (ALL, ALL, ALL), (ALL, ALL, ALL)),
        (Y, (ALL, ALL, 1 - y), (ALL, ALL, y)),
        (Z0, (ALL, 1 - z0, y), (ALL, z0, y)),
        (Z1, (1 - z1, z0, y), (z1, z0, y)),
    ]

    def hop(k):
        b, out, _ = hops[k]
        return remote(vsum.at[out], vland.at[(k,) + out], v_send.at[5 + k], v_recv.at[5 + k], place.partner(b))

    def hop_arrived(k):
        copy = hop(k)
        copy.wait_send()
        copy.wait_recv()
        own = hops[k][2]
        vsum[own] = vsum[own] + vland[(k,) + own]

    T = Scatter(place, S, R, s_send, s_recv, ready, parse(scatter_order), store_unit)
    plan = Schedule(T, Chain(hop, hop_arrived, 5), parse(scatter_order), scatter_counts)
    message = {u: m for m, u in enumerate(scatter_units)}

    def put(m, grad):
        for i in range(PARTS):
            S[m, i % 2, i // 16, i // 8 % 2, i // 4 % 2, i // 2 % 2] = wire(grad[ROWS * i : ROWS * i + ROWS])

    def ffn_back(q):
        cols = pl.ds(pl.multiple_of(D * q, D), D)
        fg = f_grad[...]
        pre = (dot(fg, down_block(q), 1, 1) * slope_g[:, cols].astype(f32)).astype(bf)
        vgrad[pl.ds(5 + q, 1), :] = col_sum(pre)
        put(message[UP_UNIT] + q, dot(nl_g[...], pre, 0, 0))
        d_two[...] += dot(pre, unit(UP_UNIT + q), 1, 1)
        down = dot(act_g[:, cols], fg, 0, 0)
        for i in range(8):
            for t in range(4):
                at = 96 * i + ROWS * t
                S[message[DOWN_UNIT] + t, i % 2, q // 2, q % 2, i // 4, i // 2 % 2] = wire(down[at : at + ROWS])

    plan.loop(4, ffn_back)
    plan.before()
    rhat, rstd = norm(r1_g[...])
    g = d_two[...]
    vgrad[3:4, :] = col_sum(g * rhat)
    vgrad[4:5, :] = col_sum(g)
    one = norm_back(g * bias(3), rhat, rstd)
    d_one[...] = one
    a_grad[...] = one.astype(bf)
    vgrad[2:3, :] = col_sum(a_grad[...])
    put(message[OUT_UNIT], dot(ctx_gt[...], a_grad[...], 1, 0))
    c_grad[...] = dot(a_grad[...], unit(OUT_UNIT), 1, 1).astype(bf)

    slot_lane = lax.broadcasted_iota(jnp.int32, (PMAX, 128), 1)

    def attend_back(it):
        s, rows, cols, mask = pair_at(it)
        slots = pl.ds(pl.multiple_of(s * PMAX, PMAX), PMAX)
        q, g = q_g[slots, cols], c_grad[slots, cols]
        k, v = J[1, rows, cols] * scale, J[2, rows, cols]
        none = jnp.zeros_like(q)
        both = lambda t: jnp.concatenate(
            [jnp.where(slot_lane < HD, t, none), jnp.where(slot_lane < HD, none, t)], 0
        )
        q2, g2 = both(q), both(g)
        ones = jnp.full((2 * PMAX, 128), 1 / 128, bf)
        scores = dot(jnp.concatenate([k, mask], 1), jnp.concatenate([q2, ones], 1), 1, 1)
        e = jnp.exp(scores - jnp.max(scores, 0, keepdims=True))
        probs = e * (1.0 / jnp.sum(e, 0, keepdims=True))
        d_probs = dot(v, g2, 1, 1)
        row_dot = jnp.sum(probs * d_probs, 0, keepdims=True)
        d_scores = (probs * (d_probs - row_dot)).astype(bf)
        dv = dot(probs.astype(bf), g2, 1, 0)
        dk = dot(d_scores, q2 * scale, 1, 0)
        dq2 = dot(d_scores, k, 0, 0)
        dq = jnp.where(slot_lane < HD, dq2[:PMAX], dq2[PMAX:])
        dq_g[slots, cols] = dq.astype(bf)
        J[1, rows, cols] = dk.astype(bf)
        J[2, rows, cols] = dv.astype(bf)

    plan.loop(12, attend_back)
    plan.before()
    put(message[V_UNIT], dot(xs[...], J[2], 0, 0))
    vgrad[1:2, :] = col_sum(J[2])
    plan.before()
    put(message[K_UNIT], dot(xs[...], J[1], 0, 0))
    plan.before()
    put(message[Q_UNIT], dot(x_g[...], dq_g[...], 0, 0))
    vgrad[0:1, :] = col_sum(dq_g[...])

    for r in range(72):
        vsum[r // 36, r // 18 % 2, r // 9 % 2, r % 9 : r % 9 + 1] = vgrad[r // 6 : r // 6 + 1, 128 * (r % 6) : 128 * (r % 6) + 128]

    def ffn_all(it):
        t, q = it // 4, it % 4
        rows = pl.ds(pl.multiple_of(256 * t, 256), 256)

        @pl.when(q == 0)
        def _():
            r = xs[rows, :].astype(f32) + (dot(ctx_t[:, rows], unit(OUT_UNIT), 0, 0) + bias(2))
            n = norm(r)[0] * bias(3) + bias(4)
            n1_t[...] = n
            nl_t[...] = n.astype(bf)
            acc[...] = n + bias(9)

        a = gelu_parts(dot(nl_t[...], unit(UP_UNIT + q), 1, 0) + bias(5 + q))[0]
        acc[...] += dot(a.astype(bf), down_block(q), 1, 0)

        @pl.when(q == 3)
        def _():
            done = pltpu.make_async_copy(out_t, layer_out.at[rows, :], out_sem.at[0])

            @pl.when(t > 0)
            def _():
                done.wait()

            out_t[...] = (norm(acc[...])[0] * bias(10) + bias(11)).astype(bf)
            done.start()

    plan.loop(16, ffn_all)

    def grad_in(s):
        rows = pl.ds(pl.multiple_of(s * SEQ_LEN, SEQ_LEN), SEQ_LEN)
        slots = pl.ds(pl.multiple_of(s * PMAX, PMAX), PMAX)
        t = d_one[slots, :] + dot(dq_g[slots, :], unit(Q_UNIT), 1, 1)
        high = t.astype(bf)
        low = (t - high.astype(f32)).astype(bf)
        total = dot(pick_t[s], high, 1, 0) + dot(pick_t[s], low, 1, 0)
        total += dot(J[1, rows, :], unit(K_UNIT), 1, 1)
        total += dot(J[2, rows, :], unit(V_UNIT), 1, 1)
        J[0, rows, :] = total.astype(bf)

    plan.loop(2, grad_in)
    store = pltpu.make_async_copy(J.at[0], input_grad, out_sem.at[1])
    store.start()
    plan.rest()
    g_vec[...] = vsum[z1, z0, y]
    pltpu.make_async_copy(out_t, layer_out.at[0:256, :], out_sem.at[0]).wait()
    store.wait()
    for copy in pair:
        copy.wait_send()
    for k in range(5):
        vec_hop(k).wait_send()
    G.drain()
    T.drain()


def layer_call(sizes, *args):
    vmem = pl.BlockSpec(memory_space=pltpu.VMEM)
    smem = pl.BlockSpec(memory_space=pltpu.SMEM)
    hbm = pl.BlockSpec(memory_space=pl.ANY)
    tokens = 2 * SEQ_LEN
    slots = 2 * PMAX
    dma = pltpu.SemaphoreType.DMA
    return pl.pallas_call(
        partial(layer_kernel, sizes),
        out_shape=(
            jax.ShapeDtypeStruct((tokens, D), bf),
            jax.ShapeDtypeStruct((tokens, D), bf),
            jax.ShapeDtypeStruct((432, 128), f32),
            jax.ShapeDtypeStruct((144, 128), f32),
            jax.ShapeDtypeStruct((576, 128), f32),
            jax.ShapeDtypeStruct((576, 128), f32),
            jax.ShapeDtypeStruct((16, 128), f32),
        ),
        in_specs=[smem, smem] + [vmem] * 2 + [hbm] * 6,
        out_specs=(hbm,) * 2 + (vmem,) * 5,
        scratch_shapes=[
            pltpu.VMEM((UNITS, 2, 2, 2, 2, 2 * ROWS, D), bf),
            pltpu.VMEM((UNITS, 2, 2, 2, 2, 2, 16, WIRE), bf),
            pltpu.VMEM((UNITS, 2, 2, 2, 2, 16, WIRE), bf),
            pltpu.VMEM((tokens, D), bf),
            pltpu.VMEM((3, tokens, D), bf),
            pltpu.VMEM((D, tokens), bf),
            pltpu.VMEM((slots, FF), bf),
            pltpu.VMEM((slots, FF), bf),
            pltpu.VMEM((2, SEQ_LEN, PMAX), bf),
            pltpu.VMEM((2, PMAX, SEQ_LEN), bf),
            pltpu.VMEM((slots, D), bf),
            pltpu.VMEM((slots, D), bf),
            pltpu.VMEM((slots, D), f32),
            pltpu.VMEM((slots, D), f32),
            pltpu.VMEM((slots, D), bf),
            pltpu.VMEM((slots, D), f32),
            pltpu.VMEM((slots, D), f32),
            pltpu.VMEM((slots, D), bf),
            pltpu.VMEM((slots, D), bf),
            pltpu.VMEM((slots, D), bf),
            pltpu.VMEM((slots, D), bf),
            pltpu.VMEM((D, slots), bf),
            pltpu.VMEM((256, D), f32),
            pltpu.VMEM((256, D), f32),
            pltpu.VMEM((256, D), bf),
            pltpu.VMEM((256, D), bf),
            pltpu.VMEM((slots, D), bf),
            pltpu.VMEM((2, 1728, 128), bf),
            pltpu.VMEM((2, 1728, 128), f32),
            pltpu.VMEM((2, 2, 2, 2, 2, 16, 128), bf),
            pltpu.VMEM((16, D), f32),
            pltpu.VMEM((16, D), f32),
            pltpu.VMEM((2, 2, 2, 16, 128), f32),
            pltpu.VMEM((5, 2, 2, 2, 16, 128), f32),
            dma((UNITS, 7)),
            dma((UNITS, 7)),
            dma((UNITS, 7)),
            dma((UNITS, 7)),
            pltpu.SemaphoreType.REGULAR((4,)),
            dma((8,)),
            dma((6,)),
            dma((2,)),
            dma((10,)),
            dma((10,)),
        ],
        compiler_params=pltpu.CompilerParams(
            collective_id=0, has_side_effects=True, vmem_limit_bytes=63 * 2**20
        ),
    )(*args)


def settle_kernel(n, *refs):
    ins, outs, held, sems = refs[:n], refs[n : 2 * n], refs[2 * n : 3 * n], refs[-1]
    loads = [pltpu.make_async_copy(ins[i], held[i], sems.at[i]) for i in range(n)]
    stores = [pltpu.make_async_copy(held[i], outs[i], sems.at[n + i]) for i in range(n)]
    for load in loads:
        load.start()
    for load, store in zip(loads, stores):
        load.wait()
        store.start()
    for store in stores:
        store.wait()


def settle(*arrays):
    hbm = pl.BlockSpec(memory_space=pltpu.HBM)
    n = len(arrays)
    return pl.pallas_call(
        partial(settle_kernel, n),
        out_shape=[jax.ShapeDtypeStruct(a.shape, a.dtype) for a in arrays],
        in_specs=[pl.BlockSpec(memory_space=pl.ANY)] * n,
        out_specs=[hbm] * n,
        scratch_shapes=[pltpu.VMEM(a.shape, a.dtype) for a in arrays]
        + [pltpu.SemaphoreType.DMA((2 * n,))],
        compiler_params=pltpu.CompilerParams(vmem_limit_bytes=63 * 2**20),
    )(*arrays)


def sub_groups(sizes):
    sub = sizes[0] * sizes[1] // PARTS
    return [[sub * i + j for j in range(sub)] for i in range(PARTS)]


def whole_group(sizes, flat):
    if sizes[0] * sizes[1] == PARTS:
        return flat
    return lax.all_gather(flat, ("dp", "inner"), axis_index_groups=sub_groups(sizes), tiled=True)


def own_part(sizes, flat):
    if sizes[0] * sizes[1] == PARTS:
        return flat
    return lax.psum_scatter(
        flat, ("dp", "inner"), axis_index_groups=sub_groups(sizes), scatter_dimension=0, tiled=True
    )


def on_device(
    sizes,
    inputs,
    qkv_weight,
    out_weight,
    up_weight,
    down_weight,
    vectors,
    lengths,
    counts,
    positions,
    grad_values,
):
    wq, wo, w1, w2, vec = [
        whole_group(sizes, w) for w in (qkv_weight, out_weight, up_weight, down_weight, vectors)
    ]
    number = lax.axis_index("dp") * sizes[1] + lax.axis_index("inner")
    quarter = number // (sizes[0] * sizes[1] // PARTS) % 4
    size = vec.shape[0]
    frame = lax.dynamic_update_slice(jnp.zeros((16 * 128,), bf), vec, (quarter * size,)).reshape(16, 128)
    layer_out, input_grad, g_qkv, g_out, g_up, g_down, g_vec = layer_call(
        sizes,
        lengths,
        counts,
        positions,
        frame,
        wq.reshape(-1, 128),
        wo.reshape(-1, 128),
        w1.reshape(-1, 128),
        w2.reshape(-1, 128),
        inputs,
        grad_values.reshape(-1, D),
    )
    g_vec = lax.dynamic_slice(g_vec.reshape(-1), (quarter * size,), (size,))
    layer_out, input_grad, g_qkv, g_out, g_up, g_down = settle(
        layer_out, input_grad, g_qkv, g_out, g_up, g_down
    )
    flat = [own_part(sizes, g.reshape(-1)) for g in (g_qkv, g_out, g_up, g_down, g_vec)]
    return (layer_out, input_grad, *flat)


def solution(mesh):
    both = ("dp", "inner")
    rows, flat = P(both, None), P(both)
    return jax.shard_map(
        partial(on_device, (mesh.shape["dp"], mesh.shape["inner"])),
        mesh=mesh,
        in_specs=(rows, flat, flat, flat, flat, flat, flat, flat, rows, P(both, None, None)),
        out_specs=(rows, rows, flat, flat, flat, flat, flat),
        check_vma=False,
    )
```

```python
from functools import partial

import jax
import jax.numpy as jnp
from jax import lax
from jax.experimental import pallas as pl
from jax.experimental.pallas import tpu as pltpu
from jax.sharding import PartitionSpec as P

D = 768
H = 12
HD = 64
FF = 3072
SEQ_LEN = 512
PMAX = 128
norm_eps = 1e-05
masked_score = -1e30

bf = jnp.bfloat16
f32 = jnp.float32
MESH = pl.DeviceIdType.MESH
PARTS = 32
ROWS = D // PARTS
UNITS = 12
K_UNIT, V_UNIT, Q_UNIT, OUT_UNIT, UP_UNIT, DOWN_UNIT = 0, 1, 2, 3, 4, 8
CORE, X, Y, Z0, Z1 = range(5)
ALL = slice(None)
HALF = D // 2
WIRE = 3 * HALF

gather_types = (
    "ab", "ab", "ab", "ab", "ab", "gx", "gx", "ab", "ab", "ab", "ab", "gy",
)
gather_order = (
    "1z1", "12v0", "0z1", "5s0", "12v1", "2z1", "6s0", "9z1", "11s0", "1z0", "5s1", "12v2", "11s1",
    "6s1", "0z0", "2z0", "1A1", "1B1", "0A1", "9z0", "0B1", "12v3", "8z1", "4z1", "10z1", "2A1",
    "2B1", "0B2", "7z1", "0A2", "3z1", "4z0", "8z0", "12v4", "1A2", "1B2", "0C", "3z0", "2B2",
    "7z0", "5z1", "2A2", "10z0", "4B1", "8B1", "4A1", "12v5", "1C", "3B1", "3A1", "8A1", "6z1",
    "9A1", "2C", "9B1", "7B1", "4B2", "4A2", "11z1", "10A1", "8A2", "10B1", "5z0", "7A1", "3A2",
    "6z0", "3B2", "9A2", "8B2", "4C", "9B2", "7A2", "7B2", "10A2", "3C", "10B2", "11z0", "5C",
    "6C", "9C", "7C", "8C", "10C", "11C",
)
gather_counts = (
    0, 2, 1, 4, 35, 0, 4, 5, 3, 2, 0, 2, 2, 0, 0, 0, 4, 3, 3, 1, 0, 1, 1, 0, 0, 4, 0, 2, 1, 1, 1,
    2,
)
scatter_units = (4, 5, 6, 7, 8, 9, 10, 11, 3, 1, 0, 2)
scatter_types = (
    "gx", "ab", "gy", "ab", "gx", "ab", "ab", "ab", "ab", "ab", "ab", "ab",
)
scatter_order = (
    "0C", "1C", "3C", "2C", "0z0", "1B2", "1A2", "3B2", "6C", "3A2", "5C", "2z0", "1A1", "7C",
    "6A2", "4C", "6B2", "8C", "1B1", "0z1", "7A2", "7B2", "8A2", "5B2", "4z0", "3B1", "6A1", "8B2",
    "2z1", "5A2", "3A1", "9C", "7A1", "7B1", "12v0", "4z1", "12v1", "5B1", "6B1", "10C", "9A2",
    "8A1", "5A1", "3z0", "7z0", "8B1", "11C", "10B2", "1z0", "9B2", "10A2", "12v2", "5z0", "3z1",
    "9A1", "6z0", "11A2", "9B1", "11B2", "8z0", "5z1", "10B1", "1z1", "10A1", "6z1", "12v3", "2s1",
    "11B1", "4s1", "9z0", "8z1", "11A1", "0s1", "7z1", "12v4", "10z0", "11z0", "2s0", "9z1", "0s0",
    "6L", "10z1", "4s0", "11z1", "3L", "2L", "0L", "9L", "1L", "5L", "7L", "12v5", "8L", "4L",
    "10L", "11L",
)
scatter_counts = (
    0, 1, 1, 0, 1, 4, 0, 1, 2, 9, 1, 2, 2, 1, 1, 2, 2, 4, 1, 8, 5, 4, 4, 5, 5, 8, 2, 7,
)


def parse(order):
    digits = [2 if o[1].isdigit() else 1 for o in order]
    return [(int(o[:d]), o[d:]) for o, d in zip(order, digits)]


class Place:
    def __init__(self, dp_size, inner_size):
        self.sub_size = dp_size * inner_size // PARTS
        self.inner_size = inner_size
        number = lax.axis_index("dp") * inner_size + lax.axis_index("inner")
        self.sub = number % self.sub_size
        self.group = number // self.sub_size
        self.bits = [(self.group // 2**b) % 2 for b in range(5)]
        self.c, self.x, self.y, self.z0, self.z1 = self.bits

    def partner(self, b):
        group = self.group + 2**b - 2 * 2**b * self.bits[b]
        number = group * self.sub_size + self.sub
        return (number // self.inner_size, number % self.inner_size)


def remote(src, dst, send_sem, recv_sem, device):
    return pltpu.make_async_remote_copy(
        src_ref=src,
        dst_ref=dst,
        send_sem=send_sem,
        recv_sem=recv_sem,
        device_id=device,
        device_id_type=MESH,
    )


def enter(place):
    barrier = pltpu.get_barrier_semaphore()
    for b in range(5):
        pl.semaphore_signal(barrier, inc=1, device_id=place.partner(b), device_id_type=MESH)
    pl.semaphore_wait(barrier, 5)


class Gather:
    def __init__(self, place, W, V, send, recv):
        self.place, self.W, self.V, self.send, self.recv = place, W, V, send, recv
        self.cols = pl.ds(pl.multiple_of(HALF * place.c, 128), HALF)
        x, y, z0, z1 = place.x, place.y, place.z0, place.z1
        every = (ALL, ALL, ALL, ALL)
        self.legs = {
            "ab": [
                ("z1", (), Z1, (z1, z0, y, x)),
                ("z0", ("z1",), Z0, (ALL, z0, y, x)),
                ("A1", ("z0",), Y, (0, ALL, y, x)),
                ("B1", ("z0",), X, (1, ALL, y, x)),
                ("A2", ("A1",), X, (0, ALL, ALL, x)),
                ("B2", ("B1",), Y, (1, ALL, y, ALL)),
                ("C", ("A2", "B2"), CORE, every),
            ],
            "e": [
                ("s0", (), X, (z1, z0, y, x)),
                ("z1", ("s0",), Z1, (z1, z0, y, ALL)),
                ("z0", ("z1",), Z0, (ALL, z0, y, ALL)),
                ("s3", ("z0",), Y, (ALL, ALL, y, ALL)),
                ("C", ("s3",), CORE, every),
            ],
            "f": [
                ("s0", (), Y, (z1, z0, y, x)),
                ("z1", ("s0",), Z1, (z1, z0, ALL, x)),
                ("z0", ("z1",), Z0, (ALL, z0, ALL, x)),
                ("s3", ("z0",), X, (ALL, ALL, ALL, x)),
                ("C", ("s3",), CORE, every),
            ],
            "gx": [
                ("s0", (), X, (z1, z0, y, x)),
                ("s1", ("s0",), Y, (z1, z0, y, ALL)),
                ("z1", ("s1",), Z1, (z1, z0, ALL, ALL)),
                ("z0", ("z1",), Z0, (ALL, z0, ALL, ALL)),
                ("C", ("z0",), CORE, every),
            ],
            "gy": [
                ("s0", (), Y, (z1, z0, y, x)),
                ("s1", ("s0",), X, (z1, z0, ALL, x)),
                ("z1", ("s1",), Z1, (z1, z0, ALL, ALL)),
                ("z0", ("z1",), Z0, (ALL, z0, ALL, ALL)),
                ("C", ("z0",), CORE, every),
            ],
        }
        self.got, self.sent = set(), []

    def copy(self, m, name):
        legs = self.legs[gather_types[m]]
        k = [leg[0] for leg in legs].index(name)
        _, after, b, index = legs[k]
        if m < DOWN_UNIT:
            part = self.W.at[(m,) + index + (ALL, self.cols)]
        else:
            part = self.V.at[index + (m - DOWN_UNIT, ALL, self.cols)]
        sems = self.send.at[m, k], self.recv.at[m, k]
        return remote(part, part, *sems, self.place.partner(b)), after

    def arrive(self, m, name="C"):
        if (m, name) not in self.got:
            self.got.add((m, name))
            self.copy(m, name)[0].wait_recv()

    def op(self, m, name):
        copy, after = self.copy(m, name)
        for a in after:
            self.arrive(m, a)
        copy.start()
        self.sent.append((m, name))

    def drain(self):
        for m, name in self.sent:
            self.copy(m, name)[0].wait_send()


class Scatter:
    def __init__(self, place, S, R, N, send, recv, ready, order, store):
        self.place, self.S, self.R, self.N, self.store = place, S, R, N, store
        self.send, self.recv, self.ready = send, recv, ready
        x, y, z0, z1 = place.x, place.y, place.z0, place.z1
        self.legs = {
            "ab": [
                ("A2", ("C",), X, (0, ALL, ALL, 1 - x), (0, ALL, ALL, 1 - x), (0, ALL, ALL, x), (0, ALL, ALL, x)),
                ("B2", ("C",), Y, (1, ALL, 1 - y, ALL), (1, ALL, 1 - y, ALL), (1, ALL, y, ALL), (1, ALL, y, ALL)),
                ("A1", ("A2",), Y, (0, ALL, 1 - y, x), (0, ALL, 1 - y, 1 - x), (0, ALL, y, x), (0, ALL, y, 1 - x)),
                ("B1", ("B2",), X, (1, ALL, y, 1 - x), (1, ALL, 1 - y, 1 - x), (1, ALL, y, x), (1, ALL, 1 - y, x)),
                ("z0", ("A1", "B1"), Z0, (ALL, 1 - z0, y, x), (ALL, 1 - z0, 1 - y, 1 - x), (ALL, z0, y, x), (ALL, z0, 1 - y, 1 - x)),
                ("z1", ("z0",), Z1, (1 - z1, z0, y, x), (1 - z1, 1 - z0, 1 - y, 1 - x), (z1, z0, y, x), (z1, 1 - z0, 1 - y, 1 - x)),
            ],
            "e": [
                ("s3", ("C",), Y, (ALL, ALL, 1 - y, ALL), (ALL, ALL, 1 - y, ALL), (ALL, ALL, y, ALL), (ALL, ALL, y, ALL)),
                ("z0", ("s3",), Z0, (ALL, 1 - z0, y, ALL), (ALL, 1 - z0, 1 - y, ALL), (ALL, z0, y, ALL), (ALL, z0, 1 - y, ALL)),
                ("z1", ("z0",), Z1, (1 - z1, z0, y, ALL), (1 - z1, 1 - z0, 1 - y, ALL), (z1, z0, y, ALL), (z1, 1 - z0, 1 - y, ALL)),
                ("s0", ("z1",), X, (z1, z0, y, 1 - x), (1 - z1, 1 - z0, 1 - y, 1 - x), (z1, z0, y, x), (1 - z1, 1 - z0, 1 - y, x)),
            ],
            "f": [
                ("s3", ("C",), X, (ALL, ALL, ALL, 1 - x), (ALL, ALL, ALL, 1 - x), (ALL, ALL, ALL, x), (ALL, ALL, ALL, x)),
                ("z0", ("s3",), Z0, (ALL, 1 - z0, ALL, x), (ALL, 1 - z0, ALL, 1 - x), (ALL, z0, ALL, x), (ALL, z0, ALL, 1 - x)),
                ("z1", ("z0",), Z1, (1 - z1, z0, ALL, x), (1 - z1, 1 - z0, ALL, 1 - x), (z1, z0, ALL, x), (z1, 1 - z0, ALL, 1 - x)),
                ("s0", ("z1",), Y, (z1, z0, 1 - y, x), (1 - z1, 1 - z0, 1 - y, 1 - x), (z1, z0, y, x), (1 - z1, 1 - z0, y, 1 - x)),
            ],
            "gx": [
                ("z0", ("C",), Z0, (ALL, 1 - z0, ALL, ALL), (ALL, 1 - z0, ALL, ALL), (ALL, z0, ALL, ALL), (ALL, z0, ALL, ALL)),
                ("z1", ("z0",), Z1, (1 - z1, z0, ALL, ALL), (1 - z1, 1 - z0, ALL, ALL), (z1, z0, ALL, ALL), (z1, 1 - z0, ALL, ALL)),
                ("s1", ("z1",), Y, (z1, z0, 1 - y, ALL), (1 - z1, 1 - z0, 1 - y, ALL), (z1, z0, y, ALL), (1 - z1, 1 - z0, y, ALL)),
                ("s0", ("s1",), X, (z1, z0, y, 1 - x), (1 - z1, 1 - z0, 1 - y, 1 - x), (z1, z0, y, x), (1 - z1, 1 - z0, 1 - y, x)),
            ],
            "gy": [
                ("z0", ("C",), Z0, (ALL, 1 - z0, ALL, ALL), (ALL, 1 - z0, ALL, ALL), (ALL, z0, ALL, ALL), (ALL, z0, ALL, ALL)),
                ("z1", ("z0",), Z1, (1 - z1, z0, ALL, ALL), (1 - z1, 1 - z0, ALL, ALL), (z1, z0, ALL, ALL), (z1, 1 - z0, ALL, ALL)),
                ("s1", ("z1",), X, (z1, z0, ALL, 1 - x), (1 - z1, 1 - z0, ALL, 1 - x), (z1, z0, ALL, x), (1 - z1, 1 - z0, ALL, x)),
                ("s0", ("s1",), Y, (z1, z0, 1 - y, x), (1 - z1, 1 - z0, 1 - y, 1 - x), (z1, z0, y, x), (1 - z1, 1 - z0, y, 1 - x)),
            ],
        }
        self.got, self.sent = set(), []
        self.turn = {}
        for m, name in order:
            if m < UNITS and "C" in self.leg(m, name)[1] and m not in self.turn:
                self.turn[m] = len(self.turn)
        self.heard = {b: 0 for b in (X, Y, Z0, Z1)}

    def leg(self, m, name):
        if name in "CL":
            return (name, (), CORE)
        return [leg for leg in self.legs[scatter_types[m]] if leg[0] == name][0]

    def copy(self, m, name):
        c = self.place.c
        if name == "C":
            sems = self.send.at[m, 0], self.recv.at[m, 0]
            return remote(self.S.at[m, 1 - c], self.R.at[m], *sems, self.place.partner(CORE))
        k = [leg[0] for leg in self.legs[scatter_types[m]]].index(name) + 1
        _, after, b, out, land, _, _ = self.leg(m, name)
        sems = self.send.at[m, k], self.recv.at[m, k]
        there = self.N.at[self.early(m, name)] if "C" in after else self.S.at[(m, 1 - c) + land]
        return remote(self.S.at[(m, c) + out], there, *sems, self.place.partner(b))

    def early(self, m, name):
        return {"A2": (m, 0), "B2": (m, 1)}.get(name, (m,))

    def add(self, m, name):
        if (m, name) in self.got:
            return
        self.got.add((m, name))
        c = self.place.c
        copy = self.copy(m, name)
        if name == "C":
            copy.wait_send()
            self.sent.remove((m, name))
            for b in (X, Y, Z0, Z1):
                pl.semaphore_signal(
                    self.ready.at[b - 1],
                    inc=1,
                    device_id=self.place.partner(b),
                    device_id_type=MESH,
                )
            copy.wait_recv()
            self.S[m, c] = self.S[m, c] + self.R[m]
            return
        copy.wait_recv()
        _, after, _, _, _, own, landed = self.leg(m, name)
        came = self.N[self.early(m, name)] if "C" in after else self.S[(m, 1 - c) + landed]
        self.S[(m, c) + own] = self.S[(m, c) + own] + came

    def op(self, m, name):
        after, b = self.leg(m, name)[1:3]
        for a in after:
            self.add(m, a)
        if b != CORE and "C" not in after:
            need = self.turn[m] + 1 - self.heard[b]
            if need > 0:
                pl.semaphore_wait(self.ready.at[b - 1], need)
                self.heard[b] += need
        self.copy(m, name).start()
        self.sent.append((m, name))

    def finish(self, m):
        name = self.legs[scatter_types[m]][-1][0]
        self.copy(m, name).wait_recv()
        c = self.place.c
        own, landed = self.leg(m, name)[5:]
        total = self.S[(m, c) + own].astype(f32) + self.S[(m, 1 - c) + landed].astype(f32)
        left, right = total[:8], total[8:]
        rows = [
            jnp.concatenate([v[:, HALF * k : HALF * k + HALF] for v in (left, right)], 1)
            for k in range(3)
        ]
        self.store(m, jnp.concatenate(rows, 0))

    def drain(self):
        for m, name in self.sent:
            self.copy(m, name).wait_send()
        for b in (X, Y, Z0, Z1):
            if UNITS > self.heard[b]:
                pl.semaphore_wait(self.ready.at[b - 1], UNITS - self.heard[b])


def wire(rows):
    halves = [
        jnp.concatenate([rows[8 * k : 8 * k + 8, h * HALF : h * HALF + HALF] for k in range(3)], 1)
        for h in range(2)
    ]
    return jnp.concatenate(halves, 0).astype(bf)


def dot(left, right, left_axis, right_axis):
    return lax.dot_general(
        left,
        right,
        (((left_axis,), (right_axis,)), ((), ())),
        preferred_element_type=f32,
    )


def norm(rows):
    centered = rows - jnp.mean(rows, -1, keepdims=True)
    rstd = lax.rsqrt(jnp.mean(centered * centered, -1, keepdims=True) + norm_eps)
    return centered * rstd, rstd


def norm_back(grad, rhat, rstd):
    inner = jnp.mean(grad * rhat, -1, keepdims=True)
    return rstd * (grad - jnp.mean(grad, -1, keepdims=True) - rhat * inner)


def col_sum(rows):
    return jnp.sum(rows.astype(f32), 0, keepdims=True)


def normal_cdf(u):
    return 0.5 + 0.5 * lax.erf(u * 0.7071067811865476)


def normal_density(u):
    return jnp.exp(-0.5 * u * u) * 0.3989422804014327


class Chain:
    def __init__(self, hop, arrived, size):
        self.hop, self.arrived, self.size = hop, arrived, size

    def op(self, k):
        if k > 0:
            self.arrived(k - 1)
        if k < self.size:
            self.hop(k).start()


class Schedule:
    def __init__(self, engine, chain, order, counts):
        self.engine, self.chain, self.order, self.counts = engine, chain, list(order), list(counts)

    def run(self, n):
        for _ in range(n):
            m, name = self.order.pop(0)
            if m == UNITS:
                self.chain.op(int(name[1:]))
            elif name == "L":
                self.engine.finish(m)
            else:
                self.engine.op(m, name)

    def before(self):
        self.run(self.counts.pop(0))

    def loop(self, n, body, needs=None):
        counts = [self.counts.pop(0) for _ in range(n)]

        @pl.loop(0, n)
        def _(i):
            for k in range(n):
                if counts[k] or needs:

                    @pl.when(i == k)
                    def _():
                        self.run(counts[k])
                        if needs:
                            needs(k)

            body(i)

    def rest(self):
        self.run(len(self.order))


def layer_kernel(
    sizes,
    lengths, counts, positions, vec_in, wq, wo, w1, w2, x_in, gv_in,
    layer_out, input_grad, g_qkv, g_out, g_up, g_down, g_vec,
    W, V, S, R, N, xs, J, ctx_t, act_g, slope_g, pick_t, x_g, q_g, res_g, acc_g, nl_g,
    f_grad, dq_g, ctx_gt, acc, nl_t, out_t, wide, vec_all, vec, vgrad,
    vsum, vland,
    g_send, g_recv, s_send, s_recv, ready, first, in_sem, out_sem, v_send, v_recv,
):
    place = Place(*sizes)
    c, x, y, z0, z1 = place.bits
    chip = (z1, z0, y, x)
    load_x = pltpu.make_async_copy(x_in, xs, in_sem.at[0])
    load_gv = pltpu.make_async_copy(gv_in, dq_g, in_sem.at[1])
    weights = ((wq, 0, 0), (wo, 0, 432), (w1, 1, 0), (w2, 2, 0))

    def flat_part(w, block, at):
        cols = pl.ds(pl.multiple_of(HALF * c + 128 * block, 128), 128)
        return out_t.at[at : at + w.shape[0], cols]

    own = [
        pltpu.make_async_copy(w, flat_part(w, block, at), in_sem.at[2 + i])
        for i, (w, block, at) in enumerate(weights)
    ]
    pair = [
        remote(w, flat_part(w, block, at), first.at[2 * i], first.at[2 * i + 1], place.partner(CORE))
        for i, (w, block, at) in enumerate(weights)
    ]
    for copy in own:
        copy.start()
    load_x.start()
    load_gv.start()
    enter(place)
    G = Gather(place, W, V, g_send, g_recv)

    vec_order = (CORE, X, Y, Z0, Z1)

    def vec_hop(k):
        at = [z1, z0, y, x, c]
        for done in vec_order[:k]:
            at[4 - done] = ALL
        part = vec_all.at[tuple(at)]
        return remote(part, part, v_send.at[k], v_recv.at[k], place.partner(vec_order[k]))

    pair[0].start()
    vec_all[chip + (c,)] = vec_in[...]
    for copy in pair[1:]:
        copy.start()
    chain = Chain(vec_hop, lambda k: vec_hop(k).wait_recv(), 5)
    plan = Schedule(G, chain, parse(gather_order), gather_counts)

    def lay(u, at, stride, n):
        for j in range(3):
            col = 3 * c + j
            if u < DOWN_UNIT:
                rows = [wide[i, pl.ds(at + col, n, stride=stride), :] for i in range(2)]
                block = jnp.concatenate(rows, 0)
            else:
                block = wide[(u - DOWN_UNIT) // 2, pl.ds(at + col, n, stride=stride), :]
            cols = pl.ds(pl.multiple_of(128 * col, 128), 128)
            if u < DOWN_UNIT:
                W[(u,) + chip + (ALL, cols)] = block.astype(bf)
            else:
                V[chip + (u - DOWN_UNIT, ALL, cols)] = block.astype(bf)

    parts = (
        [(K_UNIT, 6, 18, ROWS), (V_UNIT, 12, 18, ROWS), (Q_UNIT, 0, 18, ROWS)],
        [(OUT_UNIT, 0, 6, ROWS)],
        [(UP_UNIT + j, 6 * j, 24, ROWS) for j in range(4)],
        [(DOWN_UNIT + q, 6 * 48 * (q % 2), 6, 48) for q in range(4)],
    )
    for i, (w, block, at) in enumerate(weights):
        plan.before()
        own[i].wait()
        pair[i].wait_recv()
        n = w.shape[0]
        for k in range(2):
            col = HALF * k + 128 * block
            wide[k, :n] = out_t[at : at + n, col : col + 128].astype(f32)
        for part in parts[i]:
            lay(*part)

    def bias(i):
        return vec[pl.ds(i, 1), :]

    def unit(u):
        return W[u].reshape(D, D)

    def down_block(j):
        return V[j // 2, j % 2].reshape(D, D)

    plan.before()
    load_x.wait()
    load_gv.wait()
    for s in range(2):
        place_id = lax.broadcasted_iota(jnp.int32, (SEQ_LEN, PMAX), 0)
        slot_id = lax.broadcasted_iota(jnp.int32, (SEQ_LEN, PMAX), 1)
        match = (positions[s : s + 1, :] == place_id) & (slot_id < counts[s])
        hot = jnp.where(match, 1.0, 0.0)
        pick_t[s] = hot.astype(bf)
        x_g[PMAX * s : PMAX * s + PMAX] = dot(pick_t[s], xs[SEQ_LEN * s : SEQ_LEN * s + SEQ_LEN], 0, 0).astype(bf)

    def project(i, u, b):
        def body(t):
            rows = pl.ds(pl.multiple_of(512 * t, 512), 512)
            y = dot(xs[rows, :], unit(u), 1, 0)
            J[i, rows, :] = (y if b is None else y + bias(b)).astype(bf)

        plan.before()
        G.arrive(u)
        plan.loop(2, body)

    project(1, K_UNIT, None)
    plan.before()
    gathered = jnp.sum(vec_all[...].astype(f32).reshape(8, 4, 16, 128), 1)
    for r in range(72):
        vec[r // 6 : r // 6 + 1, 128 * (r % 6) : 128 * (r % 6) + 128] = gathered[r // 9, r % 9 : r % 9 + 1]
    project(2, V_UNIT, 1)
    project(0, Q_UNIT, 0)

    lane_id = lax.broadcasted_iota(jnp.int32, (SEQ_LEN, 128), 1)
    key_id = lax.broadcasted_iota(jnp.int32, (SEQ_LEN, 128), 0)
    scale = bf(HD**-0.5)

    def pair_at(it):
        s, p = it // 6, it % 6
        rows = pl.ds(pl.multiple_of(s * SEQ_LEN, SEQ_LEN), SEQ_LEN)
        cols = pl.ds(pl.multiple_of(p * 128, 128), 128)
        mask = jnp.where(key_id < lengths[s], 0.0, masked_score).astype(bf)
        return s, rows, cols, mask

    def attend(it):
        s, rows, cols, mask = pair_at(it)
        q, k, v = J[0, rows, cols], J[1, rows, cols] * scale, J[2, rows, cols]
        v_t = v.T
        for h in range(2):
            mine = lane_id // HD == h
            scores = dot(jnp.where(mine, k, mask), jnp.where(mine, q, bf(1 / HD)), 1, 1)
            e = jnp.exp(scores - jnp.max(scores, 0, keepdims=True))
            total = jnp.sum(e, 0, keepdims=True)
            o = dot(v_t[HD * h : HD * h + HD], e.astype(bf), 1, 0) * (1.0 / total)
            at = pl.multiple_of((it % 6) * 128 + HD * h, HD)
            ctx_t[pl.ds(at, HD), rows] = o.astype(bf)

    plan.loop(12, attend)

    plan.before()
    G.arrive(OUT_UNIT)
    for s in range(2):
        rows = slice(SEQ_LEN * s, SEQ_LEN * s + SEQ_LEN)
        slots = slice(PMAX * s, PMAX * s + PMAX)
        ctx_gt[:, slots] = dot(ctx_t[:, rows], pick_t[s], 1, 0).astype(bf)
        q_g[slots, :] = dot(pick_t[s], J[0, rows, :], 0, 0).astype(bf)
    r1 = x_g[...].astype(f32) + (dot(ctx_gt[...], unit(OUT_UNIT), 0, 0) + bias(2))
    res_g[...] = r1
    n1 = norm(r1)[0] * bias(3) + bias(4)
    acc_g[...] = n1 + bias(9)
    nl_g[...] = n1.astype(bf)

    def up_listed(q):
        cols = pl.ds(pl.multiple_of(D * q, D), D)
        u = dot(nl_g[...], unit(UP_UNIT + q), 1, 0) + bias(5 + q)
        phi = normal_cdf(u)
        act_g[:, cols] = (u * phi).astype(bf)
        slope_g[:, cols] = (phi + u * normal_density(u)).astype(bf)

    plan.loop(4, up_listed, lambda q: G.arrive(UP_UNIT + q))
    plan.rest()
    for u in range(DOWN_UNIT, UNITS):
        G.arrive(u)

    @pl.loop(0, 4)
    def _(q):
        cols = pl.ds(pl.multiple_of(D * q, D), D)
        acc_g[...] += dot(act_g[:, cols], down_block(q), 1, 0)

    rhat, rstd = norm(acc_g[...])
    used = [dot(pick_t[s], jnp.ones((SEQ_LEN, 128), bf), 0, 0)[:, :1] for s in range(2)]
    cot = jnp.where(jnp.concatenate(used, 0) > 0.5, dq_g[...].astype(f32), 0.0)
    vgrad[10:11, :] = col_sum(cot * rhat)
    vgrad[11:12, :] = col_sum(cot)
    two = norm_back(cot * bias(10), rhat, rstd)
    acc_g[...] = two
    f_grad[...] = two.astype(bf)
    vgrad[9:10, :] = col_sum(f_grad[...])

    def store_unit(m, grad):
        u = scatter_units[m]
        if u in (K_UNIT, V_UNIT, Q_UNIT):
            out, stride, at = g_qkv, 18, 6 * ((u + 1) % 3)
        elif u == OUT_UNIT:
            out, stride, at = g_out, 6, 0
        elif u < DOWN_UNIT:
            out, stride, at = g_up, 24, 6 * (u - UP_UNIT)
        else:
            out, stride, at = g_down, 6, 6 * ROWS * (u - DOWN_UNIT)
        for j in range(6):
            out[pl.ds(at + j, ROWS, stride=stride), :] = grad[:, 128 * j : 128 * j + 128]

    whole = (ALL, ALL, ALL)
    hops = [
        (CORE, whole, (0,) + whole, whole, (0,) + whole),
        (X, whole, (1,) + whole, whole, (1,) + whole),
        (Y, (ALL, ALL, 1 - y), (2, ALL, ALL, 1 - y), (ALL, ALL, y), (2, ALL, ALL, y)),
        (Z0, (ALL, 1 - z0, y), (2, ALL, 1 - z0, 1 - y), (ALL, z0, y), (2, ALL, z0, 1 - y)),
        (Z1, (1 - z1, z0, y), (2, 1 - z1, 1 - z0, 1 - y), (z1, z0, y), (2, z1, 1 - z0, 1 - y)),
    ]

    def hop(k):
        b, out, land, _, _ = hops[k]
        return remote(vsum.at[out], vland.at[land], v_send.at[5 + k], v_recv.at[5 + k], place.partner(b))

    def hop_arrived(k):
        copy = hop(k)
        copy.wait_send()
        copy.wait_recv()
        own, landed = hops[k][3:]
        vsum[own] = vsum[own] + vland[landed]

    T = Scatter(place, S, R, N, s_send, s_recv, ready, parse(scatter_order), store_unit)
    plan = Schedule(T, Chain(hop, hop_arrived, 5), parse(scatter_order), scatter_counts)
    message = {u: m for m, u in enumerate(scatter_units)}

    def put(m, grad):
        for i in range(PARTS):
            S[m, i % 2, i // 16, i // 8 % 2, i // 4 % 2, i // 2 % 2] = wire(grad[ROWS * i : ROWS * i + ROWS])

    def up_back(q):
        cols = pl.ds(pl.multiple_of(D * q, D), D)
        pre = (dot(f_grad[...], down_block(q), 1, 1) * slope_g[:, cols].astype(f32)).astype(bf)
        slope_g[:, cols] = pre
        put(message[UP_UNIT] + q, dot(nl_g[...], pre, 0, 0))

    def down_back(q):
        cols = pl.ds(pl.multiple_of(D * q, D), D)
        pre = slope_g[:, cols]
        vgrad[pl.ds(5 + q, 1), :] = col_sum(pre)
        acc_g[...] += dot(pre, unit(UP_UNIT + q), 1, 1)
        down = dot(act_g[:, cols], f_grad[...], 0, 0)
        for i in range(8):
            for t in range(4):
                at = 96 * i + ROWS * t
                S[message[DOWN_UNIT] + t, i % 2, q // 2, q % 2, i // 4, i // 2 % 2] = wire(down[at : at + ROWS])

    plan.loop(4, up_back)
    plan.loop(4, down_back)
    plan.before()
    rhat, rstd = norm(res_g[...])
    g = acc_g[...]
    vgrad[3:4, :] = col_sum(g * rhat)
    vgrad[4:5, :] = col_sum(g)
    one = norm_back(g * bias(3), rhat, rstd)
    res_g[...] = one
    f_grad[...] = one.astype(bf)
    vgrad[2:3, :] = col_sum(f_grad[...])
    put(message[OUT_UNIT], dot(ctx_gt[...], f_grad[...], 1, 0))
    nl_g[...] = dot(f_grad[...], unit(OUT_UNIT), 1, 1).astype(bf)

    slot_lane = lax.broadcasted_iota(jnp.int32, (PMAX, 128), 1)

    def attend_back(it):
        for k in range(2):
            pair_back(2 * it + k)

    def pair_back(it):
        s, rows, cols, mask = pair_at(it)
        slots = pl.ds(pl.multiple_of(s * PMAX, PMAX), PMAX)
        q, g = q_g[slots, cols], nl_g[slots, cols]
        k, v = J[1, rows, cols] * scale, J[2, rows, cols]
        none = jnp.zeros_like(q)
        both = lambda t: jnp.concatenate(
            [jnp.where(slot_lane < HD, t, none), jnp.where(slot_lane < HD, none, t)], 0
        )
        q2, g2 = both(q), both(g)
        ones = jnp.full((2 * PMAX, 128), 1 / 128, bf)
        scores = dot(jnp.concatenate([k, mask], 1), jnp.concatenate([q2, ones], 1), 1, 1)
        e = jnp.exp(scores - jnp.max(scores, 0, keepdims=True))
        probs = e * (1.0 / jnp.sum(e, 0, keepdims=True))
        d_probs = dot(v, g2, 1, 1)
        row_dot = jnp.sum(probs * d_probs, 0, keepdims=True)
        d_scores = (probs * (d_probs - row_dot)).astype(bf)
        dv = dot(probs.astype(bf), g2, 1, 0)
        dk = dot(d_scores, q2 * scale, 1, 0)
        dq2 = dot(d_scores, k, 0, 0)
        dq = jnp.where(slot_lane < HD, dq2[:PMAX], dq2[PMAX:])
        dq_g[slots, cols] = dq.astype(bf)
        J[1, rows, cols] = dk.astype(bf)
        J[2, rows, cols] = dv.astype(bf)

    plan.loop(6, attend_back)
    plan.before()
    put(message[V_UNIT], dot(xs[...], J[2], 0, 0))
    vgrad[1:2, :] = col_sum(J[2])
    plan.before()
    put(message[K_UNIT], dot(xs[...], J[1], 0, 0))
    plan.before()
    put(message[Q_UNIT], dot(x_g[...], dq_g[...], 0, 0))
    vgrad[0:1, :] = col_sum(dq_g[...])

    for r in range(72):
        vsum[r // 36, r // 18 % 2, r // 9 % 2, r % 9 : r % 9 + 1] = vgrad[r // 6 : r // 6 + 1, 128 * (r % 6) : 128 * (r % 6) + 128]

    def ffn_all(it):
        t, q = it // 4, it % 4
        rows = pl.ds(pl.multiple_of(512 * t, 512), 512)

        @pl.when(q == 0)
        def _():
            r = xs[rows, :].astype(f32) + (dot(ctx_t[:, rows], unit(OUT_UNIT), 0, 0) + bias(2))
            n = norm(r)[0] * bias(3) + bias(4)
            nl_t[...] = n.astype(bf)
            acc[...] = n + bias(9)

        half = [slice(0, 256), slice(256, 512)]
        up = [dot(nl_t[h, :], unit(UP_UNIT + q), 1, 0) + bias(5 + q) for h in half]
        for h, u in zip(half, up):
            acc[h, :] += dot((u * normal_cdf(u)).astype(bf), down_block(q), 1, 0)

        @pl.when(q == 3)
        def _():
            done = pltpu.make_async_copy(out_t.at[0:512], layer_out.at[rows, :], out_sem.at[0])

            @pl.when(t > 0)
            def _():
                done.wait()

            out_t[:512, :] = (norm(acc[...])[0] * bias(10) + bias(11)).astype(bf)
            done.start()

    plan.loop(8, ffn_all)

    def grad_in(s):
        rows = pl.ds(pl.multiple_of(s * SEQ_LEN, SEQ_LEN), SEQ_LEN)
        slots = pl.ds(pl.multiple_of(s * PMAX, PMAX), PMAX)
        t = res_g[slots, :] + dot(dq_g[slots, :], unit(Q_UNIT), 1, 1)
        high = t.astype(bf)
        low = (t - high.astype(f32)).astype(bf)
        total = dot(pick_t[s], high, 1, 0) + dot(pick_t[s], low, 1, 0)
        total += dot(J[1, rows, :], unit(K_UNIT), 1, 1)
        total += dot(J[2, rows, :], unit(V_UNIT), 1, 1)
        J[0, rows, :] = total.astype(bf)

    plan.loop(2, grad_in)
    store = pltpu.make_async_copy(J.at[0], input_grad, out_sem.at[1])
    store.start()
    plan.rest()
    g_vec[...] = vsum[z1, z0, y]
    pltpu.make_async_copy(out_t.at[0:512], layer_out.at[0:512, :], out_sem.at[0]).wait()
    store.wait()
    for copy in pair:
        copy.wait_send()
    for k in range(5):
        vec_hop(k).wait_send()
    G.drain()
    T.drain()


def layer_call(sizes, *args):
    vmem = pl.BlockSpec(memory_space=pltpu.VMEM)
    smem = pl.BlockSpec(memory_space=pltpu.SMEM)
    hbm = pl.BlockSpec(memory_space=pl.ANY)
    tokens = 2 * SEQ_LEN
    slots = 2 * PMAX
    dma = pltpu.SemaphoreType.DMA
    return pl.pallas_call(
        partial(layer_kernel, sizes),
        out_shape=(
            jax.ShapeDtypeStruct((tokens, D), bf),
            jax.ShapeDtypeStruct((tokens, D), bf),
            jax.ShapeDtypeStruct((432, 128), f32),
            jax.ShapeDtypeStruct((144, 128), f32),
            jax.ShapeDtypeStruct((576, 128), f32),
            jax.ShapeDtypeStruct((576, 128), f32),
            jax.ShapeDtypeStruct((16, 128), f32),
        ),
        in_specs=[smem, smem] + [vmem] * 2 + [hbm] * 6,
        out_specs=(hbm,) * 2 + (vmem,) * 5,
        scratch_shapes=[
            pltpu.VMEM((DOWN_UNIT, 2, 2, 2, 2, 2 * ROWS, D), bf),
            pltpu.VMEM((2, 2, 2, 2, 4, 2 * ROWS, D), bf),
            pltpu.VMEM((UNITS, 2, 2, 2, 2, 2, 16, WIRE), bf),
            pltpu.VMEM((UNITS, 2, 2, 2, 2, 16, WIRE), bf),
            pltpu.VMEM((UNITS, 2, 2, 2, 16, WIRE), bf),
            pltpu.VMEM((tokens, D), bf),
            pltpu.VMEM((3, tokens, D), bf),
            pltpu.VMEM((D, tokens), bf),
            pltpu.VMEM((slots, FF), bf),
            pltpu.VMEM((slots, FF), bf),
            pltpu.VMEM((2, SEQ_LEN, PMAX), bf),
            pltpu.VMEM((slots, D), bf),
            pltpu.VMEM((slots, D), bf),
            pltpu.VMEM((slots, D), f32),
            pltpu.VMEM((slots, D), f32),
            pltpu.VMEM((slots, D), bf),
            pltpu.VMEM((slots, D), bf),
            pltpu.VMEM((slots, D), bf),
            pltpu.VMEM((D, slots), bf),
            pltpu.VMEM((512, D), f32),
            pltpu.VMEM((512, D), bf),
            pltpu.VMEM((576, D), bf),
            pltpu.VMEM((2, 576, 128), f32),
            pltpu.VMEM((2, 2, 2, 2, 2, 16, 128), bf),
            pltpu.VMEM((16, D), f32),
            pltpu.VMEM((16, D), f32),
            pltpu.VMEM((2, 2, 2, 16, 128), f32),
            pltpu.VMEM((3, 2, 2, 2, 16, 128), f32),
            dma((UNITS, 7)),
            dma((UNITS, 7)),
            dma((UNITS, 7)),
            dma((UNITS, 7)),
            pltpu.SemaphoreType.REGULAR((4,)),
            dma((8,)),
            dma((6,)),
            dma((2,)),
            dma((10,)),
            dma((10,)),
        ],
        compiler_params=pltpu.CompilerParams(
            collective_id=0, has_side_effects=True, vmem_limit_bytes=63 * 2**20
        ),
    )(*args)


settle_parts = 2


def settle_kernel(n, *refs):
    ins, outs, held, sems = refs[:n], refs[n : 2 * n], refs[2 * n : 3 * n], refs[-1]
    loads, stores = [], []
    for i in range(n):
        size = ins[i].shape[0] // settle_parts
        for k in range(settle_parts):
            rows = slice(size * k, size * k + size)
            j = settle_parts * i + k
            loads.append(pltpu.make_async_copy(ins[i].at[rows], held[i].at[rows], sems.at[0, j]))
            stores.append(pltpu.make_async_copy(held[i].at[rows], outs[i].at[rows], sems.at[1, j]))
    for load in loads:
        load.start()
    for load, store in zip(loads, stores):
        load.wait()
        store.start()
    for store in stores:
        store.wait()


def settle(*arrays):
    hbm = pl.BlockSpec(memory_space=pltpu.HBM)
    n = len(arrays)
    return pl.pallas_call(
        partial(settle_kernel, n),
        out_shape=[jax.ShapeDtypeStruct(a.shape, a.dtype) for a in arrays],
        in_specs=[pl.BlockSpec(memory_space=pl.ANY)] * n,
        out_specs=[hbm] * n,
        scratch_shapes=[pltpu.VMEM(a.shape, a.dtype) for a in arrays]
        + [pltpu.SemaphoreType.DMA((2, settle_parts * n))],
        compiler_params=pltpu.CompilerParams(vmem_limit_bytes=63 * 2**20),
    )(*arrays)


def sub_groups(sizes):
    sub = sizes[0] * sizes[1] // PARTS
    return [[sub * i + j for j in range(sub)] for i in range(PARTS)]


def whole_group(sizes, flat):
    if sizes[0] * sizes[1] == PARTS:
        return flat
    return lax.all_gather(flat, ("dp", "inner"), axis_index_groups=sub_groups(sizes), tiled=True)


def own_part(sizes, flat):
    if sizes[0] * sizes[1] == PARTS:
        return flat
    return lax.psum_scatter(
        flat, ("dp", "inner"), axis_index_groups=sub_groups(sizes), scatter_dimension=0, tiled=True
    )


def on_device(
    sizes,
    inputs,
    qkv_weight,
    out_weight,
    up_weight,
    down_weight,
    vectors,
    lengths,
    counts,
    positions,
    grad_values,
):
    wq, wo, w1, w2, vec = [
        whole_group(sizes, w) for w in (qkv_weight, out_weight, up_weight, down_weight, vectors)
    ]
    number = lax.axis_index("dp") * sizes[1] + lax.axis_index("inner")
    quarter = number // (sizes[0] * sizes[1] // PARTS) % 4
    size = vec.shape[0]
    frame = lax.dynamic_update_slice(jnp.zeros((16 * 128,), bf), vec, (quarter * size,)).reshape(16, 128)
    layer_out, input_grad, g_qkv, g_out, g_up, g_down, g_vec = layer_call(
        sizes,
        lengths,
        counts,
        positions,
        frame,
        wq.reshape(-1, 128),
        wo.reshape(-1, 128),
        w1.reshape(-1, 128),
        w2.reshape(-1, 128),
        inputs,
        grad_values.reshape(-1, D),
    )
    g_vec = lax.dynamic_slice(g_vec.reshape(-1), (quarter * size,), (size,))
    layer_out, input_grad, g_qkv, g_out, g_up, g_down = settle(
        layer_out, input_grad, g_qkv, g_out, g_up, g_down
    )
    flat = [own_part(sizes, g.reshape(-1)) for g in (g_qkv, g_out, g_up, g_down, g_vec)]
    return (layer_out, input_grad, *flat)


def solution(mesh):
    both = ("dp", "inner")
    rows, flat = P(both, None), P(both)
    return jax.shard_map(
        partial(on_device, (mesh.shape["dp"], mesh.shape["inner"])),
        mesh=mesh,
        in_specs=(rows, flat, flat, flat, flat, flat, flat, flat, rows, P(both, None, None)),
        out_specs=(rows, rows, flat, flat, flat, flat, flat),
        check_vma=False,
    )
```

```python
from functools import partial

import jax
import jax.numpy as jnp
from jax import lax
from jax.experimental import pallas as pl
from jax.experimental.pallas import tpu as pltpu
from jax.sharding import PartitionSpec as P

D = 768
H = 12
HD = 64
FF = 3072
SEQ_LEN = 512
PMAX = 128
norm_eps = 1e-05
masked_score = -1e30

bf = jnp.bfloat16
f32 = jnp.float32
MESH = pl.DeviceIdType.MESH
PARTS = 32
ROWS = D // PARTS
UNITS = 12
K_UNIT, V_UNIT, Q_UNIT, OUT_UNIT, UP_UNIT, DOWN_UNIT = 0, 1, 2, 3, 4, 8
CORE, X, Y, Z0, Z1 = range(5)
ALL = slice(None)
HALF = D // 2
WIRE = 3 * HALF

gather_types = (
    "ab", "ab", "ab", "ab", "gx", "ab", "gy", "ab", "ab", "gx", "ab", "ab",
)
gather_order = (
    "12v0", "0z1", "1z1", "12v1", "4s0", "6s0", "2z1", "9s0", "12v2", "5z1", "0z0", "4s1", "12v3",
    "6s1", "1z0", "9s1", "0B1", "3z1", "0A1", "2z0", "5z0", "1B1", "7z1", "1A1", "0B2", "0A2",
    "3z0", "2B1", "2A1", "8z1", "1B2", "10z1", "7z0", "11z1", "12v4", "1A2", "3A1", "0C", "2B2",
    "8z0", "10z0", "5A1", "5B1", "11z0", "2A2", "1C", "4z1", "3B1", "12v5", "6z1", "8B1", "10A1",
    "2C", "7B1", "8A1", "10B1", "7A1", "11A1", "9z1", "4z0", "11B1", "8B2", "3A2", "3B2", "5A2",
    "5B2", "6z0", "8A2", "7B2", "7A2", "11B2", "11A2", "10A2", "9z0", "3C", "5C", "4C", "10B2",
    "6C", "7C", "8C", "11C", "10C", "9C",
)
gather_counts = (
    1, 1, 2, 3, 25, 16, 1, 1, 1, 0, 1, 3, 3, 1, 3, 3, 0, 3, 2, 0, 0, 4, 1, 0, 0, 2, 3, 0, 1, 1, 1,
    1,
)
scatter_units = (4, 5, 6, 7, 8, 9, 10, 11, 3, 1, 0, 2)
scatter_types = (
    "gx", "ab", "gy", "ab", "ab", "gx", "ab", "ab", "ab", "ab", "ab", "ab",
)
scatter_order = (
    "0C", "1C", "2C", "3C", "0z0", "1A2", "1B2", "3B2", "3A2", "4C", "6C", "2z0", "7C", "1B1",
    "5C", "1A1", "8C", "4B2", "6A2", "3A1", "6B2", "7A2", "0z1", "5z0", "8B2", "4A2", "2z1", "3B1",
    "7B2", "4B1", "9C", "8A2", "6A1", "11C", "4A1", "12v0", "6B1", "11B2", "11A2", "12v1", "1z0",
    "5z1", "0s1", "7B1", "7A1", "3z0", "8A1", "11B1", "10C", "9A2", "6z0", "9B2", "11A1", "8B1",
    "7z0", "10A2", "4z0", "12v2", "1z1", "3z1", "10B2", "6z1", "9A1", "0s0", "9B1", "2s1", "4z1",
    "8z0", "11z0", "7z1", "10A1", "6L", "5s1", "4L", "12v3", "10B1", "0L", "8z1", "3L", "9z0",
    "11z1", "2s0", "10z0", "1L", "12v4", "7L", "5s0", "8L", "9z1", "10z1", "2L", "11L", "5L", "9L",
    "12v5", "10L",
)
scatter_counts = (
    0, 1, 1, 1, 0, 4, 0, 0, 6, 4, 4, 4, 1, 0, 3, 1, 1, 2, 4, 4, 6, 7, 6, 10, 0, 11, 8, 1,
)


def parse(order):
    digits = [2 if o[1].isdigit() else 1 for o in order]
    return [(int(o[:d]), o[d:]) for o, d in zip(order, digits)]


class Place:
    def __init__(self, dp_size, inner_size):
        self.sub_size = dp_size * inner_size // PARTS
        self.inner_size = inner_size
        number = lax.axis_index("dp") * inner_size + lax.axis_index("inner")
        self.sub = number % self.sub_size
        self.group = number // self.sub_size
        self.bits = [(self.group // 2**b) % 2 for b in range(5)]
        self.c, self.x, self.y, self.z0, self.z1 = self.bits

    def partner(self, b):
        group = self.group + 2**b - 2 * 2**b * self.bits[b]
        number = group * self.sub_size + self.sub
        return (number // self.inner_size, number % self.inner_size)


def remote(src, dst, send_sem, recv_sem, device):
    return pltpu.make_async_remote_copy(
        src_ref=src,
        dst_ref=dst,
        send_sem=send_sem,
        recv_sem=recv_sem,
        device_id=device,
        device_id_type=MESH,
    )


def enter(place):
    barrier = pltpu.get_barrier_semaphore()
    for b in range(5):
        pl.semaphore_signal(barrier, inc=1, device_id=place.partner(b), device_id_type=MESH)
    pl.semaphore_wait(barrier, 5)


class Gather:
    def __init__(self, place, W, V, send, recv):
        self.place, self.W, self.V, self.send, self.recv = place, W, V, send, recv
        self.cols = pl.ds(pl.multiple_of(HALF * place.c, 128), HALF)
        x, y, z0, z1 = place.x, place.y, place.z0, place.z1
        every = (ALL, ALL, ALL, ALL)
        self.legs = {
            "ab": [
                ("z1", (), Z1, (z1, z0, y, x)),
                ("z0", ("z1",), Z0, (ALL, z0, y, x)),
                ("A1", ("z0",), Y, (0, ALL, y, x)),
                ("B1", ("z0",), X, (1, ALL, y, x)),
                ("A2", ("A1",), X, (0, ALL, ALL, x)),
                ("B2", ("B1",), Y, (1, ALL, y, ALL)),
                ("C", ("A2", "B2"), CORE, every),
            ],
            "e": [
                ("s0", (), X, (z1, z0, y, x)),
                ("z1", ("s0",), Z1, (z1, z0, y, ALL)),
                ("z0", ("z1",), Z0, (ALL, z0, y, ALL)),
                ("s3", ("z0",), Y, (ALL, ALL, y, ALL)),
                ("C", ("s3",), CORE, every),
            ],
            "f": [
                ("s0", (), Y, (z1, z0, y, x)),
                ("z1", ("s0",), Z1, (z1, z0, ALL, x)),
                ("z0", ("z1",), Z0, (ALL, z0, ALL, x)),
                ("s3", ("z0",), X, (ALL, ALL, ALL, x)),
                ("C", ("s3",), CORE, every),
            ],
            "gx": [
                ("s0", (), X, (z1, z0, y, x)),
                ("s1", ("s0",), Y, (z1, z0, y, ALL)),
                ("z1", ("s1",), Z1, (z1, z0, ALL, ALL)),
                ("z0", ("z1",), Z0, (ALL, z0, ALL, ALL)),
                ("C", ("z0",), CORE, every),
            ],
            "gy": [
                ("s0", (), Y, (z1, z0, y, x)),
                ("s1", ("s0",), X, (z1, z0, ALL, x)),
                ("z1", ("s1",), Z1, (z1, z0, ALL, ALL)),
                ("z0", ("z1",), Z0, (ALL, z0, ALL, ALL)),
                ("C", ("z0",), CORE, every),
            ],
        }
        self.got, self.sent = set(), []

    def copy(self, m, name):
        legs = self.legs[gather_types[m]]
        k = [leg[0] for leg in legs].index(name)
        _, after, b, index = legs[k]
        if m < DOWN_UNIT:
            part = self.W.at[(m,) + index + (ALL, self.cols)]
        else:
            part = self.V.at[index + (m - DOWN_UNIT, ALL, self.cols)]
        sems = self.send.at[m, k], self.recv.at[m, k]
        return remote(part, part, *sems, self.place.partner(b)), after

    def arrive(self, m, name="C"):
        if (m, name) not in self.got:
            self.got.add((m, name))
            self.copy(m, name)[0].wait_recv()

    def op(self, m, name):
        copy, after = self.copy(m, name)
        for a in after:
            self.arrive(m, a)
        copy.start()
        self.sent.append((m, name))

    def drain(self):
        for m, name in self.sent:
            self.copy(m, name)[0].wait_send()


class Scatter:
    def __init__(self, place, S, R, N, send, recv, ready, order, store):
        self.place, self.S, self.R, self.N, self.store = place, S, R, N, store
        self.send, self.recv, self.ready = send, recv, ready
        x, y, z0, z1 = place.x, place.y, place.z0, place.z1
        self.legs = {
            "ab": [
                ("A2", ("C",), X, (0, ALL, ALL, 1 - x), (0, ALL, ALL, 1 - x), (0, ALL, ALL, x), (0, ALL, ALL, x)),
                ("B2", ("C",), Y, (1, ALL, 1 - y, ALL), (1, ALL, 1 - y, ALL), (1, ALL, y, ALL), (1, ALL, y, ALL)),
                ("A1", ("A2",), Y, (0, ALL, 1 - y, x), (0, ALL, 1 - y, 1 - x), (0, ALL, y, x), (0, ALL, y, 1 - x)),
                ("B1", ("B2",), X, (1, ALL, y, 1 - x), (1, ALL, 1 - y, 1 - x), (1, ALL, y, x), (1, ALL, 1 - y, x)),
                ("z0", ("A1", "B1"), Z0, (ALL, 1 - z0, y, x), (ALL, 1 - z0, 1 - y, 1 - x), (ALL, z0, y, x), (ALL, z0, 1 - y, 1 - x)),
                ("z1", ("z0",), Z1, (1 - z1, z0, y, x), (1 - z1, 1 - z0, 1 - y, 1 - x), (z1, z0, y, x), (z1, 1 - z0, 1 - y, 1 - x)),
            ],
            "e": [
                ("s3", ("C",), Y, (ALL, ALL, 1 - y, ALL), (ALL, ALL, 1 - y, ALL), (ALL, ALL, y, ALL), (ALL, ALL, y, ALL)),
                ("z0", ("s3",), Z0, (ALL, 1 - z0, y, ALL), (ALL, 1 - z0, 1 - y, ALL), (ALL, z0, y, ALL), (ALL, z0, 1 - y, ALL)),
                ("z1", ("z0",), Z1, (1 - z1, z0, y, ALL), (1 - z1, 1 - z0, 1 - y, ALL), (z1, z0, y, ALL), (z1, 1 - z0, 1 - y, ALL)),
                ("s0", ("z1",), X, (z1, z0, y, 1 - x), (1 - z1, 1 - z0, 1 - y, 1 - x), (z1, z0, y, x), (1 - z1, 1 - z0, 1 - y, x)),
            ],
            "f": [
                ("s3", ("C",), X, (ALL, ALL, ALL, 1 - x), (ALL, ALL, ALL, 1 - x), (ALL, ALL, ALL, x), (ALL, ALL, ALL, x)),
                ("z0", ("s3",), Z0, (ALL, 1 - z0, ALL, x), (ALL, 1 - z0, ALL, 1 - x), (ALL, z0, ALL, x), (ALL, z0, ALL, 1 - x)),
                ("z1", ("z0",), Z1, (1 - z1, z0, ALL, x), (1 - z1, 1 - z0, ALL, 1 - x), (z1, z0, ALL, x), (z1, 1 - z0, ALL, 1 - x)),
                ("s0", ("z1",), Y, (z1, z0, 1 - y, x), (1 - z1, 1 - z0, 1 - y, 1 - x), (z1, z0, y, x), (1 - z1, 1 - z0, y, 1 - x)),
            ],
            "gx": [
                ("z0", ("C",), Z0, (ALL, 1 - z0, ALL, ALL), (ALL, 1 - z0, ALL, ALL), (ALL, z0, ALL, ALL), (ALL, z0, ALL, ALL)),
                ("z1", ("z0",), Z1, (1 - z1, z0, ALL, ALL), (1 - z1, 1 - z0, ALL, ALL), (z1, z0, ALL, ALL), (z1, 1 - z0, ALL, ALL)),
                ("s1", ("z1",), Y, (z1, z0, 1 - y, ALL), (1 - z1, 1 - z0, 1 - y, ALL), (z1, z0, y, ALL), (1 - z1, 1 - z0, y, ALL)),
                ("s0", ("s1",), X, (z1, z0, y, 1 - x), (1 - z1, 1 - z0, 1 - y, 1 - x), (z1, z0, y, x), (1 - z1, 1 - z0, 1 - y, x)),
            ],
            "gy": [
                ("z0", ("C",), Z0, (ALL, 1 - z0, ALL, ALL), (ALL, 1 - z0, ALL, ALL), (ALL, z0, ALL, ALL), (ALL, z0, ALL, ALL)),
                ("z1", ("z0",), Z1, (1 - z1, z0, ALL, ALL), (1 - z1, 1 - z0, ALL, ALL), (z1, z0, ALL, ALL), (z1, 1 - z0, ALL, ALL)),
                ("s1", ("z1",), X, (z1, z0, ALL, 1 - x), (1 - z1, 1 - z0, ALL, 1 - x), (z1, z0, ALL, x), (1 - z1, 1 - z0, ALL, x)),
                ("s0", ("s1",), Y, (z1, z0, 1 - y, x), (1 - z1, 1 - z0, 1 - y, 1 - x), (z1, z0, y, x), (1 - z1, 1 - z0, y, 1 - x)),
            ],
        }
        self.got, self.sent = set(), []
        self.turn = {}
        for m, name in order:
            if m < UNITS and "C" in self.leg(m, name)[1] and m not in self.turn:
                self.turn[m] = len(self.turn)
        self.heard = {b: 0 for b in (X, Y, Z0, Z1)}

    def leg(self, m, name):
        if name in "CL":
            return (name, (), CORE)
        return [leg for leg in self.legs[scatter_types[m]] if leg[0] == name][0]

    def copy(self, m, name):
        c = self.place.c
        if name == "C":
            sems = self.send.at[m, 0], self.recv.at[m, 0]
            return remote(self.S.at[m, 1 - c], self.R.at[m], *sems, self.place.partner(CORE))
        k = [leg[0] for leg in self.legs[scatter_types[m]]].index(name) + 1
        _, after, b, out, land, _, _ = self.leg(m, name)
        sems = self.send.at[m, k], self.recv.at[m, k]
        there = self.N.at[self.early(m, name)] if "C" in after else self.S.at[(m, 1 - c) + land]
        return remote(self.S.at[(m, c) + out], there, *sems, self.place.partner(b))

    def early(self, m, name):
        return {"A2": (m, 0), "B2": (m, 1)}.get(name, (m,))

    def add(self, m, name):
        if (m, name) in self.got:
            return
        self.got.add((m, name))
        c = self.place.c
        copy = self.copy(m, name)
        if name == "C":
            copy.wait_send()
            self.sent.remove((m, name))
            for b in (X, Y, Z0, Z1):
                pl.semaphore_signal(
                    self.ready.at[b - 1],
                    inc=1,
                    device_id=self.place.partner(b),
                    device_id_type=MESH,
                )
            copy.wait_recv()
            self.S[m, c] = self.S[m, c] + self.R[m]
            return
        copy.wait_recv()
        _, after, _, _, _, own, landed = self.leg(m, name)
        came = self.N[self.early(m, name)] if "C" in after else self.S[(m, 1 - c) + landed]
        self.S[(m, c) + own] = self.S[(m, c) + own] + came

    def op(self, m, name):
        after, b = self.leg(m, name)[1:3]
        for a in after:
            self.add(m, a)
        if b != CORE and "C" not in after:
            need = self.turn[m] + 1 - self.heard[b]
            if need > 0:
                pl.semaphore_wait(self.ready.at[b - 1], need)
                self.heard[b] += need
        self.copy(m, name).start()
        self.sent.append((m, name))

    def finish(self, m):
        name = self.legs[scatter_types[m]][-1][0]
        self.copy(m, name).wait_recv()
        c = self.place.c
        own, landed = self.leg(m, name)[5:]
        total = self.S[(m, c) + own].astype(f32) + self.S[(m, 1 - c) + landed].astype(f32)
        left, right = total[:8], total[8:]
        rows = [
            jnp.concatenate([v[:, HALF * k : HALF * k + HALF] for v in (left, right)], 1)
            for k in range(3)
        ]
        self.store(m, jnp.concatenate(rows, 0))

    def drain(self):
        for m, name in self.sent:
            self.copy(m, name).wait_send()
        for b in (X, Y, Z0, Z1):
            if UNITS > self.heard[b]:
                pl.semaphore_wait(self.ready.at[b - 1], UNITS - self.heard[b])


def wire(rows):
    halves = [
        jnp.concatenate([rows[8 * k : 8 * k + 8, h * HALF : h * HALF + HALF] for k in range(3)], 1)
        for h in range(2)
    ]
    return jnp.concatenate(halves, 0).astype(bf)


def dot(left, right, left_axis, right_axis):
    return lax.dot_general(
        left,
        right,
        (((left_axis,), (right_axis,)), ((), ())),
        preferred_element_type=f32,
    )


def norm(rows):
    centered = rows - jnp.mean(rows, -1, keepdims=True)
    rstd = lax.rsqrt(jnp.mean(centered * centered, -1, keepdims=True) + norm_eps)
    return centered * rstd, rstd


def norm_back(grad, rhat, rstd):
    inner = jnp.mean(grad * rhat, -1, keepdims=True)
    return rstd * (grad - jnp.mean(grad, -1, keepdims=True) - rhat * inner)


def col_sum(rows):
    return jnp.sum(rows.astype(f32), 0, keepdims=True)


def normal_cdf(u):
    return 0.5 + 0.5 * lax.erf(u * 0.7071067811865476)


def normal_density(u):
    return jnp.exp(-0.5 * u * u) * 0.3989422804014327


class Chain:
    def __init__(self, hop, arrived, size):
        self.hop, self.arrived, self.size = hop, arrived, size

    def op(self, k):
        if k > 0:
            self.arrived(k - 1)
        if k < self.size:
            self.hop(k).start()


class Schedule:
    def __init__(self, engine, chain, order, counts):
        self.engine, self.chain, self.order, self.counts = engine, chain, list(order), list(counts)

    def run(self, n):
        for _ in range(n):
            m, name = self.order.pop(0)
            if m == UNITS:
                self.chain.op(int(name[1:]))
            elif name == "L":
                self.engine.finish(m)
            else:
                self.engine.op(m, name)

    def before(self):
        self.run(self.counts.pop(0))

    def loop(self, n, body, needs=None):
        counts = [self.counts.pop(0) for _ in range(n)]

        @pl.loop(0, n)
        def _(i):
            for k in range(n):
                if counts[k] or needs:

                    @pl.when(i == k)
                    def _():
                        self.run(counts[k])
                        if needs:
                            needs(k)

            body(i)

    def rest(self):
        self.run(len(self.order))


def layer_kernel(
    sizes,
    lengths, counts, positions, vec_in, wq, wo, w1, w2, x_in, gv_in,
    layer_out, input_grad, g_qkv, g_out, g_up, g_down, g_vec,
    W, V, S, R, N, xs, J, ctx_t, act_g, slope_g, pick_t, x_g, q_g, res_g, acc_g, nl_g,
    f_grad, dq_g, ctx_gt, acc, nl_t, out_t, wide, vec_all, vec, vgrad,
    vsum, vland,
    g_send, g_recv, s_send, s_recv, ready, first, in_sem, out_sem, v_send, v_recv,
):
    place = Place(*sizes)
    c, x, y, z0, z1 = place.bits
    chip = (z1, z0, y, x)
    load_x = pltpu.make_async_copy(x_in, xs, in_sem.at[0])
    load_gv = pltpu.make_async_copy(gv_in, dq_g, in_sem.at[1])
    weights = ((wq, 0, 0), (wo, 0, 432), (w1, 1, 0), (w2, 2, 0))

    def flat_part(w, block, at):
        cols = pl.ds(pl.multiple_of(HALF * c + 128 * block, 128), 128)
        return out_t.at[at : at + w.shape[0], cols]

    own = [
        pltpu.make_async_copy(w, flat_part(w, block, at), in_sem.at[2 + i])
        for i, (w, block, at) in enumerate(weights)
    ]
    pair = [
        remote(w, flat_part(w, block, at), first.at[2 * i], first.at[2 * i + 1], place.partner(CORE))
        for i, (w, block, at) in enumerate(weights)
    ]
    for copy in own:
        copy.start()
    load_x.start()
    load_gv.start()
    enter(place)
    G = Gather(place, W, V, g_send, g_recv)

    vec_order = (CORE, X, Y, Z0, Z1)

    def vec_hop(k):
        at = [z1, z0, y, x, c]
        for done in vec_order[:k]:
            at[4 - done] = ALL
        part = vec_all.at[tuple(at)]
        return remote(part, part, v_send.at[k], v_recv.at[k], place.partner(vec_order[k]))

    pair[0].start()
    vec_all[chip + (c,)] = vec_in[...]
    for copy in pair[1:]:
        copy.start()
    chain = Chain(vec_hop, lambda k: vec_hop(k).wait_recv(), 5)
    plan = Schedule(G, chain, parse(gather_order), gather_counts)

    def lay(u, at, stride, n):
        for j in range(3):
            col = 3 * c + j
            if u < DOWN_UNIT:
                rows = [wide[i, pl.ds(at + col, n, stride=stride), :] for i in range(2)]
                block = jnp.concatenate(rows, 0)
            else:
                block = wide[(u - DOWN_UNIT) // 2, pl.ds(at + col, n, stride=stride), :]
            cols = pl.ds(pl.multiple_of(128 * col, 128), 128)
            if u < DOWN_UNIT:
                W[(u,) + chip + (ALL, cols)] = block.astype(bf)
            else:
                V[chip + (u - DOWN_UNIT, ALL, cols)] = block.astype(bf)

    parts = (
        [(K_UNIT, 6, 18, ROWS), (V_UNIT, 12, 18, ROWS), (Q_UNIT, 0, 18, ROWS)],
        [(OUT_UNIT, 0, 6, ROWS)],
        [(UP_UNIT + j, 6 * j, 24, ROWS) for j in range(4)],
        [(DOWN_UNIT + q, 6 * 48 * (q % 2), 6, 48) for q in range(4)],
    )
    for i, (w, block, at) in enumerate(weights):
        plan.before()
        own[i].wait()
        pair[i].wait_recv()
        n = w.shape[0]
        for k in range(2):
            col = HALF * k + 128 * block
            wide[k, :n] = out_t[at : at + n, col : col + 128].astype(f32)
        for part in parts[i]:
            lay(*part)

    def bias(i):
        return vec[pl.ds(i, 1), :]

    def unit(u):
        return W[u].reshape(D, D)

    def down_block(j):
        return V[j // 2, j % 2].reshape(D, D)

    plan.before()
    load_x.wait()
    load_gv.wait()
    for s in range(2):
        place_id = lax.broadcasted_iota(jnp.int32, (SEQ_LEN, PMAX), 0)
        slot_id = lax.broadcasted_iota(jnp.int32, (SEQ_LEN, PMAX), 1)
        match = (positions[s : s + 1, :] == place_id) & (slot_id < counts[s])
        hot = jnp.where(match, 1.0, 0.0)
        pick_t[s] = hot.astype(bf)
        x_g[PMAX * s : PMAX * s + PMAX] = dot(pick_t[s], xs[SEQ_LEN * s : SEQ_LEN * s + SEQ_LEN], 0, 0).astype(bf)

    def project(i, u, b):
        def body(t):
            rows = pl.ds(pl.multiple_of(512 * t, 512), 512)
            y = dot(xs[rows, :], unit(u), 1, 0)
            J[i, rows, :] = (y if b is None else y + bias(b)).astype(bf)

        plan.before()
        G.arrive(u)
        plan.loop(2, body)

    project(1, K_UNIT, None)
    plan.before()
    gathered = jnp.sum(vec_all[...].astype(f32).reshape(8, 4, 16, 128), 1)
    for r in range(72):
        vec[r // 6 : r // 6 + 1, 128 * (r % 6) : 128 * (r % 6) + 128] = gathered[r // 9, r % 9 : r % 9 + 1]
    project(2, V_UNIT, 1)
    project(0, Q_UNIT, 0)

    lane_id = lax.broadcasted_iota(jnp.int32, (SEQ_LEN, 128), 1)
    key_id = lax.broadcasted_iota(jnp.int32, (SEQ_LEN, 128), 0)
    scale = bf(HD**-0.5)

    def pair_at(it):
        s, p = it // 6, it % 6
        rows = pl.ds(pl.multiple_of(s * SEQ_LEN, SEQ_LEN), SEQ_LEN)
        cols = pl.ds(pl.multiple_of(p * 128, 128), 128)
        mask = jnp.where(key_id < lengths[s], 0.0, masked_score).astype(bf)
        return s, rows, cols, mask

    def attend(it):
        s, rows, cols, mask = pair_at(it)
        q, k, v = J[0, rows, cols], J[1, rows, cols] * scale, J[2, rows, cols]
        v_t = v.T
        for h in range(2):
            mine = lane_id // HD == h
            scores = dot(jnp.where(mine, k, mask), jnp.where(mine, q, bf(1 / HD)), 1, 1)
            e = jnp.exp(scores - jnp.max(scores, 0, keepdims=True))
            total = jnp.sum(e, 0, keepdims=True)
            o = dot(v_t[HD * h : HD * h + HD], e.astype(bf), 1, 0) * (1.0 / total)
            at = pl.multiple_of((it % 6) * 128 + HD * h, HD)
            ctx_t[pl.ds(at, HD), rows] = o.astype(bf)

    plan.loop(12, attend)

    plan.before()
    G.arrive(OUT_UNIT)
    for s in range(2):
        rows = slice(SEQ_LEN * s, SEQ_LEN * s + SEQ_LEN)
        slots = slice(PMAX * s, PMAX * s + PMAX)
        ctx_gt[:, slots] = dot(ctx_t[:, rows], pick_t[s], 1, 0).astype(bf)
        q_g[slots, :] = dot(pick_t[s], J[0, rows, :], 0, 0).astype(bf)
    r1 = x_g[...].astype(f32) + (dot(ctx_gt[...], unit(OUT_UNIT), 0, 0) + bias(2))
    res_g[...] = r1
    n1 = norm(r1)[0] * bias(3) + bias(4)
    acc_g[...] = n1 + bias(9)
    nl_g[...] = n1.astype(bf)

    def up_listed(q):
        cols = pl.ds(pl.multiple_of(D * q, D), D)
        u = dot(nl_g[...], unit(UP_UNIT + q), 1, 0) + bias(5 + q)
        phi = normal_cdf(u)
        act_g[:, cols] = (u * phi).astype(bf)
        slope_g[:, cols] = (phi + u * normal_density(u)).astype(bf)

    plan.loop(4, up_listed, lambda q: G.arrive(UP_UNIT + q))
    plan.rest()
    for u in range(DOWN_UNIT, UNITS):
        G.arrive(u)

    @pl.loop(0, 4)
    def _(q):
        cols = pl.ds(pl.multiple_of(D * q, D), D)
        acc_g[...] += dot(act_g[:, cols], down_block(q), 1, 0)

    rhat, rstd = norm(acc_g[...])
    used = [dot(pick_t[s], jnp.ones((SEQ_LEN, 128), bf), 0, 0)[:, :1] for s in range(2)]
    cot = jnp.where(jnp.concatenate(used, 0) > 0.5, dq_g[...].astype(f32), 0.0)
    vgrad[10:11, :] = col_sum(cot * rhat)
    vgrad[11:12, :] = col_sum(cot)
    two = norm_back(cot * bias(10), rhat, rstd)
    acc_g[...] = two
    f_grad[...] = two.astype(bf)
    vgrad[9:10, :] = col_sum(f_grad[...])

    def store_unit(m, grad):
        u = scatter_units[m]
        if u in (K_UNIT, V_UNIT, Q_UNIT):
            out, stride, at = g_qkv, 18, 6 * ((u + 1) % 3)
        elif u == OUT_UNIT:
            out, stride, at = g_out, 6, 0
        elif u < DOWN_UNIT:
            out, stride, at = g_up, 24, 6 * (u - UP_UNIT)
        else:
            out, stride, at = g_down, 6, 6 * ROWS * (u - DOWN_UNIT)
        for j in range(6):
            out[pl.ds(at + j, ROWS, stride=stride), :] = grad[:, 128 * j : 128 * j + 128]

    whole = (ALL, ALL, ALL)
    hops = [
        (CORE, whole, (0,) + whole, whole, (0,) + whole),
        (X, whole, (1,) + whole, whole, (1,) + whole),
        (Y, (ALL, ALL, 1 - y), (2, ALL, ALL, 1 - y), (ALL, ALL, y), (2, ALL, ALL, y)),
        (Z0, (ALL, 1 - z0, y), (2, ALL, 1 - z0, 1 - y), (ALL, z0, y), (2, ALL, z0, 1 - y)),
        (Z1, (1 - z1, z0, y), (2, 1 - z1, 1 - z0, 1 - y), (z1, z0, y), (2, z1, 1 - z0, 1 - y)),
    ]

    def hop(k):
        b, out, land, _, _ = hops[k]
        return remote(vsum.at[out], vland.at[land], v_send.at[5 + k], v_recv.at[5 + k], place.partner(b))

    def hop_arrived(k):
        copy = hop(k)
        copy.wait_send()
        copy.wait_recv()
        own, landed = hops[k][3:]
        vsum[own] = vsum[own] + vland[landed]

    T = Scatter(place, S, R, N, s_send, s_recv, ready, parse(scatter_order), store_unit)
    plan = Schedule(T, Chain(hop, hop_arrived, 5), parse(scatter_order), scatter_counts)
    message = {u: m for m, u in enumerate(scatter_units)}

    def put(m, grad):
        for i in range(PARTS):
            S[m, i % 2, i // 16, i // 8 % 2, i // 4 % 2, i // 2 % 2] = wire(grad[ROWS * i : ROWS * i + ROWS])

    def up_back(q):
        cols = pl.ds(pl.multiple_of(D * q, D), D)
        pre = (dot(f_grad[...], down_block(q), 1, 1) * slope_g[:, cols].astype(f32)).astype(bf)
        slope_g[:, cols] = pre
        put(message[UP_UNIT] + q, dot(nl_g[...], pre, 0, 0))

    def down_back(q):
        cols = pl.ds(pl.multiple_of(D * q, D), D)
        pre = slope_g[:, cols]
        vgrad[pl.ds(5 + q, 1), :] = col_sum(pre)
        acc_g[...] += dot(pre, unit(UP_UNIT + q), 1, 1)
        down = dot(act_g[:, cols], f_grad[...], 0, 0)
        for i in range(8):
            for t in range(4):
                at = 96 * i + ROWS * t
                S[message[DOWN_UNIT] + t, i % 2, q // 2, q % 2, i // 4, i // 2 % 2] = wire(down[at : at + ROWS])

    plan.loop(4, up_back)
    plan.loop(4, down_back)
    plan.before()
    rhat, rstd = norm(res_g[...])
    g = acc_g[...]
    vgrad[3:4, :] = col_sum(g * rhat)
    vgrad[4:5, :] = col_sum(g)
    one = norm_back(g * bias(3), rhat, rstd)
    res_g[...] = one
    f_grad[...] = one.astype(bf)
    vgrad[2:3, :] = col_sum(f_grad[...])
    put(message[OUT_UNIT], dot(ctx_gt[...], f_grad[...], 1, 0))
    nl_g[...] = dot(f_grad[...], unit(OUT_UNIT), 1, 1).astype(bf)

    slot_lane = lax.broadcasted_iota(jnp.int32, (PMAX, 128), 1)

    def attend_back(it):
        at = [pair_at(2 * it + k) for k in range(2)]
        none = jnp.zeros((PMAX, 128), bf)
        ones = jnp.full((2 * PMAX, 128), 1 / 128, bf)

        def both(t):
            parts = [jnp.where(slot_lane < HD, t, none), jnp.where(slot_lane < HD, none, t)]
            return jnp.concatenate(parts, 0)

        slots = [pl.ds(pl.multiple_of(s * PMAX, PMAX), PMAX) for s, _, _, _ in at]
        q2 = [both(q_g[sl, cols]) for sl, (_, _, cols, _) in zip(slots, at)]
        g2 = [both(nl_g[sl, cols]) for sl, (_, _, cols, _) in zip(slots, at)]
        keys = [J[1, rows, cols] * scale for _, rows, cols, _ in at]
        scores = [
            dot(jnp.concatenate([k, a[3]], 1), jnp.concatenate([q, ones], 1), 1, 1)
            for k, q, a in zip(keys, q2, at)
        ]
        d_probs = [dot(J[2, rows, cols], g, 1, 1) for g, (_, rows, cols, _) in zip(g2, at)]
        for i, (_, rows, cols, _) in enumerate(at):
            e = jnp.exp(scores[i] - jnp.max(scores[i], 0, keepdims=True))
            probs = e * (1.0 / jnp.sum(e, 0, keepdims=True))
            row_dot = jnp.sum(probs * d_probs[i], 0, keepdims=True)
            d_scores = (probs * (d_probs[i] - row_dot)).astype(bf)
            J[2, rows, cols] = dot(probs.astype(bf), g2[i], 1, 0).astype(bf)
            J[1, rows, cols] = dot(d_scores, q2[i] * scale, 1, 0).astype(bf)
            dq2 = dot(d_scores, keys[i], 0, 0)
            dq_g[slots[i], cols] = jnp.where(slot_lane < HD, dq2[:PMAX], dq2[PMAX:]).astype(bf)

    plan.loop(6, attend_back)
    plan.before()
    put(message[V_UNIT], dot(xs[...], J[2], 0, 0))
    vgrad[1:2, :] = col_sum(J[2])
    plan.before()
    put(message[K_UNIT], dot(xs[...], J[1], 0, 0))
    plan.before()
    put(message[Q_UNIT], dot(x_g[...], dq_g[...], 0, 0))
    vgrad[0:1, :] = col_sum(dq_g[...])

    for r in range(72):
        vsum[r // 36, r // 18 % 2, r // 9 % 2, r % 9 : r % 9 + 1] = vgrad[r // 6 : r // 6 + 1, 128 * (r % 6) : 128 * (r % 6) + 128]

    def ffn_all(it):
        t, q = it // 4, it % 4
        rows = pl.ds(pl.multiple_of(512 * t, 512), 512)

        @pl.when(q == 0)
        def _():
            r = xs[rows, :].astype(f32) + (dot(ctx_t[:, rows], unit(OUT_UNIT), 0, 0) + bias(2))
            n = norm(r)[0] * bias(3) + bias(4)
            nl_t[...] = n.astype(bf)
            acc[...] = n + bias(9)

        half = [slice(0, 256), slice(256, 512)]
        up = [dot(nl_t[h, :], unit(UP_UNIT + q), 1, 0) + bias(5 + q) for h in half]
        for h, u in zip(half, up):
            acc[h, :] += dot((u * normal_cdf(u)).astype(bf), down_block(q), 1, 0)

        @pl.when(q == 3)
        def _():
            done = pltpu.make_async_copy(out_t.at[0:512], layer_out.at[rows, :], out_sem.at[0])

            @pl.when(t > 0)
            def _():
                done.wait()

            out_t[:512, :] = (norm(acc[...])[0] * bias(10) + bias(11)).astype(bf)
            done.start()

    plan.loop(8, ffn_all)

    def grad_in(s):
        rows = pl.ds(pl.multiple_of(s * SEQ_LEN, SEQ_LEN), SEQ_LEN)
        slots = pl.ds(pl.multiple_of(s * PMAX, PMAX), PMAX)
        t = res_g[slots, :] + dot(dq_g[slots, :], unit(Q_UNIT), 1, 1)
        high = t.astype(bf)
        low = (t - high.astype(f32)).astype(bf)
        total = dot(pick_t[s], high, 1, 0) + dot(pick_t[s], low, 1, 0)
        total += dot(J[1, rows, :], unit(K_UNIT), 1, 1)
        total += dot(J[2, rows, :], unit(V_UNIT), 1, 1)
        J[0, rows, :] = total.astype(bf)

    plan.loop(2, grad_in)
    store = pltpu.make_async_copy(J.at[0], input_grad, out_sem.at[1])
    store.start()
    plan.rest()
    g_vec[...] = vsum[z1, z0, y]
    pltpu.make_async_copy(out_t.at[0:512], layer_out.at[0:512, :], out_sem.at[0]).wait()
    store.wait()
    for copy in pair:
        copy.wait_send()
    for k in range(5):
        vec_hop(k).wait_send()
    G.drain()
    T.drain()


def layer_call(sizes, *args):
    vmem = pl.BlockSpec(memory_space=pltpu.VMEM)
    smem = pl.BlockSpec(memory_space=pltpu.SMEM)
    hbm = pl.BlockSpec(memory_space=pl.ANY)
    tokens = 2 * SEQ_LEN
    slots = 2 * PMAX
    dma = pltpu.SemaphoreType.DMA
    return pl.pallas_call(
        partial(layer_kernel, sizes),
        out_shape=(
            jax.ShapeDtypeStruct((tokens, D), bf),
            jax.ShapeDtypeStruct((tokens, D), bf),
            jax.ShapeDtypeStruct((432, 128), f32),
            jax.ShapeDtypeStruct((144, 128), f32),
            jax.ShapeDtypeStruct((576, 128), f32),
            jax.ShapeDtypeStruct((576, 128), f32),
            jax.ShapeDtypeStruct((16, 128), f32),
        ),
        in_specs=[smem, smem] + [vmem] * 2 + [hbm] * 6,
        out_specs=(hbm,) * 2 + (vmem,) * 5,
        scratch_shapes=[
            pltpu.VMEM((DOWN_UNIT, 2, 2, 2, 2, 2 * ROWS, D), bf),
            pltpu.VMEM((2, 2, 2, 2, 4, 2 * ROWS, D), bf),
            pltpu.VMEM((UNITS, 2, 2, 2, 2, 2, 16, WIRE), bf),
            pltpu.VMEM((UNITS, 2, 2, 2, 2, 16, WIRE), bf),
            pltpu.VMEM((UNITS, 2, 2, 2, 16, WIRE), bf),
            pltpu.VMEM((tokens, D), bf),
            pltpu.VMEM((3, tokens, D), bf),
            pltpu.VMEM((D, tokens), bf),
            pltpu.VMEM((slots, FF), bf),
            pltpu.VMEM((slots, FF), bf),
            pltpu.VMEM((2, SEQ_LEN, PMAX), bf),
            pltpu.VMEM((slots, D), bf),
            pltpu.VMEM((slots, D), bf),
            pltpu.VMEM((slots, D), f32),
            pltpu.VMEM((slots, D), f32),
            pltpu.VMEM((slots, D), bf),
            pltpu.VMEM((slots, D), bf),
            pltpu.VMEM((slots, D), bf),
            pltpu.VMEM((D, slots), bf),
            pltpu.VMEM((512, D), f32),
            pltpu.VMEM((512, D), bf),
            pltpu.VMEM((576, D), bf),
            pltpu.VMEM((2, 576, 128), f32),
            pltpu.VMEM((2, 2, 2, 2, 2, 16, 128), bf),
            pltpu.VMEM((16, D), f32),
            pltpu.VMEM((16, D), f32),
            pltpu.VMEM((2, 2, 2, 16, 128), f32),
            pltpu.VMEM((3, 2, 2, 2, 16, 128), f32),
            dma((UNITS, 7)),
            dma((UNITS, 7)),
            dma((UNITS, 7)),
            dma((UNITS, 7)),
            pltpu.SemaphoreType.REGULAR((4,)),
            dma((8,)),
            dma((6,)),
            dma((2,)),
            dma((10,)),
            dma((10,)),
        ],
        compiler_params=pltpu.CompilerParams(
            collective_id=0, has_side_effects=True, vmem_limit_bytes=63 * 2**20
        ),
    )(*args)


settle_parts = 2


def settle_kernel(n, *refs):
    ins, outs, held, sems = refs[:n], refs[n : 2 * n], refs[2 * n : 3 * n], refs[-1]
    loads, stores = [], []
    for i in range(n):
        size = ins[i].shape[0] // settle_parts
        for k in range(settle_parts):
            rows = slice(size * k, size * k + size)
            j = settle_parts * i + k
            loads.append(pltpu.make_async_copy(ins[i].at[rows], held[i].at[rows], sems.at[0, j]))
            stores.append(pltpu.make_async_copy(held[i].at[rows], outs[i].at[rows], sems.at[1, j]))
    for load in loads:
        load.start()
    for load, store in zip(loads, stores):
        load.wait()
        store.start()
    for store in stores:
        store.wait()


def settle(*arrays):
    hbm = pl.BlockSpec(memory_space=pltpu.HBM)
    n = len(arrays)
    return pl.pallas_call(
        partial(settle_kernel, n),
        out_shape=[jax.ShapeDtypeStruct(a.shape, a.dtype) for a in arrays],
        in_specs=[pl.BlockSpec(memory_space=pl.ANY)] * n,
        out_specs=[hbm] * n,
        scratch_shapes=[pltpu.VMEM(a.shape, a.dtype) for a in arrays]
        + [pltpu.SemaphoreType.DMA((2, settle_parts * n))],
        compiler_params=pltpu.CompilerParams(vmem_limit_bytes=63 * 2**20),
    )(*arrays)


def sub_groups(sizes):
    sub = sizes[0] * sizes[1] // PARTS
    return [[sub * i + j for j in range(sub)] for i in range(PARTS)]


def whole_group(sizes, flat):
    if sizes[0] * sizes[1] == PARTS:
        return flat
    return lax.all_gather(flat, ("dp", "inner"), axis_index_groups=sub_groups(sizes), tiled=True)


def own_part(sizes, flat):
    if sizes[0] * sizes[1] == PARTS:
        return flat
    return lax.psum_scatter(
        flat, ("dp", "inner"), axis_index_groups=sub_groups(sizes), scatter_dimension=0, tiled=True
    )


def on_device(
    sizes,
    inputs,
    qkv_weight,
    out_weight,
    up_weight,
    down_weight,
    vectors,
    lengths,
    counts,
    positions,
    grad_values,
):
    wq, wo, w1, w2, vec = [
        whole_group(sizes, w) for w in (qkv_weight, out_weight, up_weight, down_weight, vectors)
    ]
    number = lax.axis_index("dp") * sizes[1] + lax.axis_index("inner")
    quarter = number // (sizes[0] * sizes[1] // PARTS) % 4
    size = vec.shape[0]
    frame = lax.dynamic_update_slice(jnp.zeros((16 * 128,), bf), vec, (quarter * size,)).reshape(16, 128)
    layer_out, input_grad, g_qkv, g_out, g_up, g_down, g_vec = layer_call(
        sizes,
        lengths,
        counts,
        positions,
        frame,
        wq.reshape(-1, 128),
        wo.reshape(-1, 128),
        w1.reshape(-1, 128),
        w2.reshape(-1, 128),
        inputs,
        grad_values.reshape(-1, D),
    )
    g_vec = lax.dynamic_slice(g_vec.reshape(-1), (quarter * size,), (size,))
    layer_out, input_grad, g_qkv, g_out, g_up, g_down = settle(
        layer_out, input_grad, g_qkv, g_out, g_up, g_down
    )
    flat = [own_part(sizes, g.reshape(-1)) for g in (g_qkv, g_out, g_up, g_down, g_vec)]
    return (layer_out, input_grad, *flat)


def solution(mesh):
    both = ("dp", "inner")
    rows, flat = P(both, None), P(both)
    return jax.shard_map(
        partial(on_device, (mesh.shape["dp"], mesh.shape["inner"])),
        mesh=mesh,
        in_specs=(rows, flat, flat, flat, flat, flat, flat, flat, rows, P(both, None, None)),
        out_specs=(rows, rows, flat, flat, flat, flat, flat),
        check_vma=False,
    )
```

```python
from functools import partial

import jax
import jax.numpy as jnp
from jax import lax
from jax.experimental import pallas as pl
from jax.experimental.pallas import tpu as pltpu
from jax.sharding import PartitionSpec as P

D = 768
H = 12
HD = 64
FF = 3072
SEQ_LEN = 512
PMAX = 128
norm_eps = 1e-05
masked_score = -1e30

bf = jnp.bfloat16
f32 = jnp.float32
MESH = pl.DeviceIdType.MESH
PARTS = 32
ROWS = D // PARTS
UNITS = 12
K_UNIT, V_UNIT, Q_UNIT, OUT_UNIT, UP_UNIT, DOWN_UNIT = 0, 1, 2, 3, 4, 8
CORE, X, Y, Z0, Z1 = range(5)
ALL = slice(None)
HALF = D // 2
WIRE = 3 * HALF

gather_types = (
    "ab", "ab", "ab", "ab", "gx", "ab", "gy", "ab", "ab", "gx", "ab", "ab",
)
gather_order = (
    "12v0", "0z1", "1z1", "12v1", "4s0", "6s0", "2z1", "9s0", "12v2", "5z1", "0z0", "4s1", "12v3",
    "6s1", "1z0", "9s1", "0B1", "3z1", "0A1", "2z0", "5z0", "1B1", "7z1", "1A1", "0B2", "0A2",
    "3z0", "2B1", "2A1", "8z1", "1B2", "10z1", "7z0", "11z1", "12v4", "1A2", "3A1", "0C", "2B2",
    "8z0", "10z0", "5A1", "5B1", "11z0", "2A2", "1C", "4z1", "3B1", "12v5", "6z1", "8B1", "10A1",
    "2C", "7B1", "8A1", "10B1", "7A1", "11A1", "9z1", "4z0", "11B1", "8B2", "3A2", "3B2", "5A2",
    "5B2", "6z0", "8A2", "7B2", "7A2", "11B2", "11A2", "10A2", "9z0", "3C", "5C", "4C", "10B2",
    "6C", "7C", "8C", "11C", "10C", "9C",
)
gather_counts = (
    1, 1, 2, 3, 25, 16, 1, 1, 1, 0, 1, 3, 3, 1, 3, 3, 0, 3, 2, 0, 0, 4, 1, 0, 0, 2, 3, 0, 1, 1, 1,
    1,
)
scatter_units = (4, 5, 6, 7, 8, 9, 10, 11, 3, 1, 0, 2)
scatter_types = (
    "gx", "ab", "gy", "ab", "ab", "gx", "ab", "ab", "ab", "ab", "ab", "ab",
)
scatter_order = (
    "0C", "1C", "2C", "3C", "0z0", "1A2", "1B2", "3B2", "3A2", "4C", "6C", "2z0", "7C", "1B1",
    "5C", "1A1", "8C", "4B2", "6A2", "3A1", "6B2", "7A2", "0z1", "5z0", "8B2", "4A2", "2z1", "3B1",
    "7B2", "4B1", "9C", "8A2", "6A1", "11C", "4A1", "12v0", "6B1", "11B2", "11A2", "12v1", "1z0",
    "5z1", "0s1", "7B1", "7A1", "3z0", "8A1", "11B1", "10C", "9A2", "6z0", "9B2", "11A1", "8B1",
    "7z0", "10A2", "4z0", "12v2", "1z1", "3z1", "10B2", "6z1", "9A1", "0s0", "9B1", "2s1", "4z1",
    "8z0", "11z0", "7z1", "10A1", "6L", "5s1", "4L", "12v3", "10B1", "0L", "8z1", "3L", "9z0",
    "11z1", "2s0", "10z0", "1L", "12v4", "7L", "5s0", "8L", "9z1", "10z1", "2L", "11L", "5L", "9L",
    "12v5", "10L",
)
scatter_counts = (
    0, 1, 1, 1, 0, 4, 0, 0, 6, 4, 4, 4, 1, 0, 3, 1, 1, 2, 4, 4, 6, 7, 6, 10, 0, 11, 8, 1,
)


def parse(order):
    digits = [2 if o[1].isdigit() else 1 for o in order]
    return [(int(o[:d]), o[d:]) for o, d in zip(order, digits)]


class Place:
    def __init__(self, dp_size, inner_size):
        self.sub_size = dp_size * inner_size // PARTS
        self.inner_size = inner_size
        number = lax.axis_index("dp") * inner_size + lax.axis_index("inner")
        self.sub = number % self.sub_size
        self.group = number // self.sub_size
        self.bits = [(self.group // 2**b) % 2 for b in range(5)]
        self.c, self.x, self.y, self.z0, self.z1 = self.bits

    def partner(self, b):
        group = self.group + 2**b - 2 * 2**b * self.bits[b]
        number = group * self.sub_size + self.sub
        return (number // self.inner_size, number % self.inner_size)


def remote(src, dst, send_sem, recv_sem, device):
    return pltpu.make_async_remote_copy(
        src_ref=src,
        dst_ref=dst,
        send_sem=send_sem,
        recv_sem=recv_sem,
        device_id=device,
        device_id_type=MESH,
    )


def enter(place):
    barrier = pltpu.get_barrier_semaphore()
    for b in range(5):
        pl.semaphore_signal(barrier, inc=1, device_id=place.partner(b), device_id_type=MESH)
    pl.semaphore_wait(barrier, 5)


class Gather:
    def __init__(self, place, W, V, send, recv):
        self.place, self.W, self.V, self.send, self.recv = place, W, V, send, recv
        self.cols = pl.ds(pl.multiple_of(HALF * place.c, 128), HALF)
        x, y, z0, z1 = place.x, place.y, place.z0, place.z1
        every = (ALL, ALL, ALL, ALL)
        self.legs = {
            "ab": [
                ("z1", (), Z1, (z1, z0, y, x)),
                ("z0", ("z1",), Z0, (ALL, z0, y, x)),
                ("A1", ("z0",), Y, (0, ALL, y, x)),
                ("B1", ("z0",), X, (1, ALL, y, x)),
                ("A2", ("A1",), X, (0, ALL, ALL, x)),
                ("B2", ("B1",), Y, (1, ALL, y, ALL)),
                ("C", ("A2", "B2"), CORE, every),
            ],
            "e": [
                ("s0", (), X, (z1, z0, y, x)),
                ("z1", ("s0",), Z1, (z1, z0, y, ALL)),
                ("z0", ("z1",), Z0, (ALL, z0, y, ALL)),
                ("s3", ("z0",), Y, (ALL, ALL, y, ALL)),
                ("C", ("s3",), CORE, every),
            ],
            "f": [
                ("s0", (), Y, (z1, z0, y, x)),
                ("z1", ("s0",), Z1, (z1, z0, ALL, x)),
                ("z0", ("z1",), Z0, (ALL, z0, ALL, x)),
                ("s3", ("z0",), X, (ALL, ALL, ALL, x)),
                ("C", ("s3",), CORE, every),
            ],
            "gx": [
                ("s0", (), X, (z1, z0, y, x)),
                ("s1", ("s0",), Y, (z1, z0, y, ALL)),
                ("z1", ("s1",), Z1, (z1, z0, ALL, ALL)),
                ("z0", ("z1",), Z0, (ALL, z0, ALL, ALL)),
                ("C", ("z0",), CORE, every),
            ],
            "gy": [
                ("s0", (), Y, (z1, z0, y, x)),
                ("s1", ("s0",), X, (z1, z0, ALL, x)),
                ("z1", ("s1",), Z1, (z1, z0, ALL, ALL)),
                ("z0", ("z1",), Z0, (ALL, z0, ALL, ALL)),
                ("C", ("z0",), CORE, every),
            ],
        }
        self.got, self.sent = set(), []

    def copy(self, m, name):
        legs = self.legs[gather_types[m]]
        k = [leg[0] for leg in legs].index(name)
        _, after, b, index = legs[k]
        if m < DOWN_UNIT:
            part = self.W.at[(m,) + index + (ALL, self.cols)]
        else:
            part = self.V.at[index + (m - DOWN_UNIT, ALL, self.cols)]
        sems = self.send.at[m, k], self.recv.at[m, k]
        return remote(part, part, *sems, self.place.partner(b)), after

    def arrive(self, m, name="C"):
        if (m, name) not in self.got:
            self.got.add((m, name))
            self.copy(m, name)[0].wait_recv()

    def op(self, m, name):
        copy, after = self.copy(m, name)
        for a in after:
            self.arrive(m, a)
        copy.start()
        self.sent.append((m, name))

    def drain(self):
        for m, name in self.sent:
            self.copy(m, name)[0].wait_send()


class Scatter:
    def __init__(self, place, S, R, N, send, recv, ready, order, store):
        self.place, self.S, self.R, self.N, self.store = place, S, R, N, store
        self.send, self.recv, self.ready = send, recv, ready
        x, y, z0, z1 = place.x, place.y, place.z0, place.z1
        self.legs = {
            "ab": [
                ("A2", ("C",), X, (0, ALL, ALL, 1 - x), (0, ALL, ALL, 1 - x), (0, ALL, ALL, x), (0, ALL, ALL, x)),
                ("B2", ("C",), Y, (1, ALL, 1 - y, ALL), (1, ALL, 1 - y, ALL), (1, ALL, y, ALL), (1, ALL, y, ALL)),
                ("A1", ("A2",), Y, (0, ALL, 1 - y, x), (0, ALL, 1 - y, 1 - x), (0, ALL, y, x), (0, ALL, y, 1 - x)),
                ("B1", ("B2",), X, (1, ALL, y, 1 - x), (1, ALL, 1 - y, 1 - x), (1, ALL, y, x), (1, ALL, 1 - y, x)),
                ("z0", ("A1", "B1"), Z0, (ALL, 1 - z0, y, x), (ALL, 1 - z0, 1 - y, 1 - x), (ALL, z0, y, x), (ALL, z0, 1 - y, 1 - x)),
                ("z1", ("z0",), Z1, (1 - z1, z0, y, x), (1 - z1, 1 - z0, 1 - y, 1 - x), (z1, z0, y, x), (z1, 1 - z0, 1 - y, 1 - x)),
            ],
            "e": [
                ("s3", ("C",), Y, (ALL, ALL, 1 - y, ALL), (ALL, ALL, 1 - y, ALL), (ALL, ALL, y, ALL), (ALL, ALL, y, ALL)),
                ("z0", ("s3",), Z0, (ALL, 1 - z0, y, ALL), (ALL, 1 - z0, 1 - y, ALL), (ALL, z0, y, ALL), (ALL, z0, 1 - y, ALL)),
                ("z1", ("z0",), Z1, (1 - z1, z0, y, ALL), (1 - z1, 1 - z0, 1 - y, ALL), (z1, z0, y, ALL), (z1, 1 - z0, 1 - y, ALL)),
                ("s0", ("z1",), X, (z1, z0, y, 1 - x), (1 - z1, 1 - z0, 1 - y, 1 - x), (z1, z0, y, x), (1 - z1, 1 - z0, 1 - y, x)),
            ],
            "f": [
                ("s3", ("C",), X, (ALL, ALL, ALL, 1 - x), (ALL, ALL, ALL, 1 - x), (ALL, ALL, ALL, x), (ALL, ALL, ALL, x)),
                ("z0", ("s3",), Z0, (ALL, 1 - z0, ALL, x), (ALL, 1 - z0, ALL, 1 - x), (ALL, z0, ALL, x), (ALL, z0, ALL, 1 - x)),
                ("z1", ("z0",), Z1, (1 - z1, z0, ALL, x), (1 - z1, 1 - z0, ALL, 1 - x), (z1, z0, ALL, x), (z1, 1 - z0, ALL, 1 - x)),
                ("s0", ("z1",), Y, (z1, z0, 1 - y, x), (1 - z1, 1 - z0, 1 - y, 1 - x), (z1, z0, y, x), (1 - z1, 1 - z0, y, 1 - x)),
            ],
            "gx": [
                ("z0", ("C",), Z0, (ALL, 1 - z0, ALL, ALL), (ALL, 1 - z0, ALL, ALL), (ALL, z0, ALL, ALL), (ALL, z0, ALL, ALL)),
                ("z1", ("z0",), Z1, (1 - z1, z0, ALL, ALL), (1 - z1, 1 - z0, ALL, ALL), (z1, z0, ALL, ALL), (z1, 1 - z0, ALL, ALL)),
                ("s1", ("z1",), Y, (z1, z0, 1 - y, ALL), (1 - z1, 1 - z0, 1 - y, ALL), (z1, z0, y, ALL), (1 - z1, 1 - z0, y, ALL)),
                ("s0", ("s1",), X, (z1, z0, y, 1 - x), (1 - z1, 1 - z0, 1 - y, 1 - x), (z1, z0, y, x), (1 - z1, 1 - z0, 1 - y, x)),
            ],
            "gy": [
                ("z0", ("C",), Z0, (ALL, 1 - z0, ALL, ALL), (ALL, 1 - z0, ALL, ALL), (ALL, z0, ALL, ALL), (ALL, z0, ALL, ALL)),
                ("z1", ("z0",), Z1, (1 - z1, z0, ALL, ALL), (1 - z1, 1 - z0, ALL, ALL), (z1, z0, ALL, ALL), (z1, 1 - z0, ALL, ALL)),
                ("s1", ("z1",), X, (z1, z0, ALL, 1 - x), (1 - z1, 1 - z0, ALL, 1 - x), (z1, z0, ALL, x), (1 - z1, 1 - z0, ALL, x)),
                ("s0", ("s1",), Y, (z1, z0, 1 - y, x), (1 - z1, 1 - z0, 1 - y, 1 - x), (z1, z0, y, x), (1 - z1, 1 - z0, y, 1 - x)),
            ],
        }
        self.got, self.sent = set(), []
        self.turn = {}
        for m, name in order:
            if m < UNITS and "C" in self.leg(m, name)[1] and m not in self.turn:
                self.turn[m] = len(self.turn)
        self.heard = {b: 0 for b in (X, Y, Z0, Z1)}

    def leg(self, m, name):
        if name in "CL":
            return (name, (), CORE)
        return [leg for leg in self.legs[scatter_types[m]] if leg[0] == name][0]

    def copy(self, m, name):
        c = self.place.c
        if name == "C":
            sems = self.send.at[m, 0], self.recv.at[m, 0]
            return remote(self.S.at[m, 1 - c], self.R.at[m], *sems, self.place.partner(CORE))
        k = [leg[0] for leg in self.legs[scatter_types[m]]].index(name) + 1
        _, after, b, out, land, _, _ = self.leg(m, name)
        sems = self.send.at[m, k], self.recv.at[m, k]
        there = self.N.at[self.early(m, name)] if "C" in after else self.S.at[(m, 1 - c) + land]
        return remote(self.S.at[(m, c) + out], there, *sems, self.place.partner(b))

    def early(self, m, name):
        return {"A2": (m, 0), "B2": (m, 1)}.get(name, (m,))

    def add(self, m, name):
        if (m, name) in self.got:
            return
        self.got.add((m, name))
        c = self.place.c
        copy = self.copy(m, name)
        if name == "C":
            copy.wait_send()
            self.sent.remove((m, name))
            for b in (X, Y, Z0, Z1):
                pl.semaphore_signal(
                    self.ready.at[b - 1],
                    inc=1,
                    device_id=self.place.partner(b),
                    device_id_type=MESH,
                )
            copy.wait_recv()
            self.S[m, c] = self.S[m, c] + self.R[m]
            return
        copy.wait_recv()
        _, after, _, _, _, own, landed = self.leg(m, name)
        came = self.N[self.early(m, name)] if "C" in after else self.S[(m, 1 - c) + landed]
        self.S[(m, c) + own] = self.S[(m, c) + own] + came

    def op(self, m, name):
        after, b = self.leg(m, name)[1:3]
        for a in after:
            self.add(m, a)
        if b != CORE and "C" not in after:
            need = self.turn[m] + 1 - self.heard[b]
            if need > 0:
                pl.semaphore_wait(self.ready.at[b - 1], need)
                self.heard[b] += need
        self.copy(m, name).start()
        self.sent.append((m, name))

    def finish(self, m):
        name = self.legs[scatter_types[m]][-1][0]
        self.copy(m, name).wait_recv()
        c = self.place.c
        own, landed = self.leg(m, name)[5:]
        total = self.S[(m, c) + own].astype(f32) + self.S[(m, 1 - c) + landed].astype(f32)
        left, right = total[:8], total[8:]
        rows = [
            jnp.concatenate([v[:, HALF * k : HALF * k + HALF] for v in (left, right)], 1)
            for k in range(3)
        ]
        self.store(m, jnp.concatenate(rows, 0))

    def drain(self):
        for m, name in self.sent:
            self.copy(m, name).wait_send()
        for b in (X, Y, Z0, Z1):
            if UNITS > self.heard[b]:
                pl.semaphore_wait(self.ready.at[b - 1], UNITS - self.heard[b])


def wire(rows):
    halves = [
        jnp.concatenate([rows[8 * k : 8 * k + 8, h * HALF : h * HALF + HALF] for k in range(3)], 1)
        for h in range(2)
    ]
    return jnp.concatenate(halves, 0).astype(bf)


def dot(left, right, left_axis, right_axis):
    return lax.dot_general(
        left,
        right,
        (((left_axis,), (right_axis,)), ((), ())),
        preferred_element_type=f32,
    )


def norm(rows):
    centered = rows - jnp.mean(rows, -1, keepdims=True)
    rstd = lax.rsqrt(jnp.mean(centered * centered, -1, keepdims=True) + norm_eps)
    return centered * rstd, rstd


def norm_back(grad, rhat, rstd):
    inner = jnp.mean(grad * rhat, -1, keepdims=True)
    return rstd * (grad - jnp.mean(grad, -1, keepdims=True) - rhat * inner)


def col_sum(rows):
    return jnp.sum(rows.astype(f32), 0, keepdims=True)


def normal_cdf(u):
    return 0.5 + 0.5 * lax.erf(u * 0.7071067811865476)


def normal_density(u):
    return jnp.exp(-0.5 * u * u) * 0.3989422804014327


class Chain:
    def __init__(self, hop, arrived, size):
        self.hop, self.arrived, self.size = hop, arrived, size

    def op(self, k):
        if k > 0:
            self.arrived(k - 1)
        if k < self.size:
            self.hop(k).start()


class Schedule:
    def __init__(self, engine, chain, order, counts):
        self.engine, self.chain, self.order, self.counts = engine, chain, list(order), list(counts)

    def run(self, n):
        for _ in range(n):
            m, name = self.order.pop(0)
            if m == UNITS:
                self.chain.op(int(name[1:]))
            elif name == "L":
                self.engine.finish(m)
            else:
                self.engine.op(m, name)

    def before(self):
        self.run(self.counts.pop(0))

    def loop(self, n, body, needs=None):
        counts = [self.counts.pop(0) for _ in range(n)]

        @pl.loop(0, n)
        def _(i):
            for k in range(n):
                if counts[k] or needs:

                    @pl.when(i == k)
                    def _():
                        self.run(counts[k])
                        if needs:
                            needs(k)

            body(i)

    def rest(self):
        self.run(len(self.order))


def layer_kernel(
    sizes,
    lengths, counts, positions, vec_in, wq, wo, w1, w2, x_in, gv_in,
    layer_out, input_grad, g_qkv, g_out, g_up, g_down, g_vec,
    W, V, S, R, N, xs, J, ctx_t, act_g, slope_g, pick_t, x_g, q_g, res_g, acc_g, nl_g,
    f_grad, dq_g, ctx_gt, acc, nl_t, out_t, wide, vec_all, vec, vgrad,
    vsum, vland,
    g_send, g_recv, s_send, s_recv, ready, first, in_sem, out_sem, v_send, v_recv,
):
    place = Place(*sizes)
    c, x, y, z0, z1 = place.bits
    chip = (z1, z0, y, x)
    load_x = pltpu.make_async_copy(x_in, xs, in_sem.at[0])
    load_gv = pltpu.make_async_copy(gv_in, dq_g, in_sem.at[1])
    weights = ((wq, 0, 0), (wo, 0, 432), (w1, 1, 0), (w2, 2, 0))

    def flat_part(w, block, at):
        cols = pl.ds(pl.multiple_of(HALF * c + 128 * block, 128), 128)
        return out_t.at[at : at + w.shape[0], cols]

    own = [
        pltpu.make_async_copy(w, flat_part(w, block, at), in_sem.at[2 + i])
        for i, (w, block, at) in enumerate(weights)
    ]
    pair = [
        remote(w, flat_part(w, block, at), first.at[2 * i], first.at[2 * i + 1], place.partner(CORE))
        for i, (w, block, at) in enumerate(weights)
    ]
    for copy in own:
        copy.start()
    load_x.start()
    load_gv.start()
    enter(place)
    G = Gather(place, W, V, g_send, g_recv)

    vec_order = (CORE, X, Y, Z0, Z1)

    def vec_hop(k):
        at = [z1, z0, y, x, c]
        for done in vec_order[:k]:
            at[4 - done] = ALL
        part = vec_all.at[tuple(at)]
        return remote(part, part, v_send.at[k], v_recv.at[k], place.partner(vec_order[k]))

    pair[0].start()
    vec_all[chip + (c,)] = vec_in[...]
    for copy in pair[1:]:
        copy.start()
    chain = Chain(vec_hop, lambda k: vec_hop(k).wait_recv(), 5)
    plan = Schedule(G, chain, parse(gather_order), gather_counts)

    def lay(u, at, stride, n):
        for j in range(3):
            col = 3 * c + j
            if u < DOWN_UNIT:
                rows = [wide[i, pl.ds(at + col, n, stride=stride), :] for i in range(2)]
                block = jnp.concatenate(rows, 0)
            else:
                block = wide[(u - DOWN_UNIT) // 2, pl.ds(at + col, n, stride=stride), :]
            cols = pl.ds(pl.multiple_of(128 * col, 128), 128)
            if u < DOWN_UNIT:
                W[(u,) + chip + (ALL, cols)] = block.astype(bf)
            else:
                V[chip + (u - DOWN_UNIT, ALL, cols)] = block.astype(bf)

    parts = (
        [(K_UNIT, 6, 18, ROWS), (V_UNIT, 12, 18, ROWS), (Q_UNIT, 0, 18, ROWS)],
        [(OUT_UNIT, 0, 6, ROWS)],
        [(UP_UNIT + j, 6 * j, 24, ROWS) for j in range(4)],
        [(DOWN_UNIT + q, 6 * 48 * (q % 2), 6, 48) for q in range(4)],
    )
    for i, (w, block, at) in enumerate(weights):
        plan.before()
        own[i].wait()
        pair[i].wait_recv()
        n = w.shape[0]
        for k in range(2):
            col = HALF * k + 128 * block
            wide[k, :n] = out_t[at : at + n, col : col + 128].astype(f32)
        for part in parts[i]:
            lay(*part)

    def bias(i):
        return vec[pl.ds(i, 1), :]

    def unit(u):
        return W[u].reshape(D, D)

    def down_block(j):
        return V[j // 2, j % 2].reshape(D, D)

    plan.before()
    load_x.wait()
    load_gv.wait()
    for s in range(2):
        place_id = lax.broadcasted_iota(jnp.int32, (SEQ_LEN, PMAX), 0)
        slot_id = lax.broadcasted_iota(jnp.int32, (SEQ_LEN, PMAX), 1)
        match = (positions[s : s + 1, :] == place_id) & (slot_id < counts[s])
        hot = jnp.where(match, 1.0, 0.0)
        pick_t[s] = hot.astype(bf)
        x_g[PMAX * s : PMAX * s + PMAX] = dot(pick_t[s], xs[SEQ_LEN * s : SEQ_LEN * s + SEQ_LEN], 0, 0).astype(bf)

    def project(i, u, b):
        def body(t):
            rows = pl.ds(pl.multiple_of(512 * t, 512), 512)
            y = dot(xs[rows, :], unit(u), 1, 0)
            J[i, rows, :] = (y if b is None else y + bias(b)).astype(bf)

        plan.before()
        G.arrive(u)
        plan.loop(2, body)

    project(1, K_UNIT, None)
    plan.before()
    gathered = jnp.sum(vec_all[...].astype(f32).reshape(8, 4, 16, 128), 1)
    for r in range(72):
        vec[r // 6 : r // 6 + 1, 128 * (r % 6) : 128 * (r % 6) + 128] = gathered[r // 9, r % 9 : r % 9 + 1]
    project(2, V_UNIT, 1)
    project(0, Q_UNIT, 0)

    lane_id = lax.broadcasted_iota(jnp.int32, (SEQ_LEN, 128), 1)
    key_id = lax.broadcasted_iota(jnp.int32, (SEQ_LEN, 128), 0)
    scale = bf(HD**-0.5)

    def pair_at(it):
        s, p = it // 6, it % 6
        rows = pl.ds(pl.multiple_of(s * SEQ_LEN, SEQ_LEN), SEQ_LEN)
        cols = pl.ds(pl.multiple_of(p * 128, 128), 128)
        mask = jnp.where(key_id < lengths[s], 0.0, masked_score).astype(bf)
        return s, rows, cols, mask

    def attend(it):
        s, rows, cols, mask = pair_at(it)
        q, k, v = J[0, rows, cols], J[1, rows, cols] * scale, J[2, rows, cols]
        v_t = v.T
        for h in range(2):
            mine = lane_id // HD == h
            scores = dot(jnp.where(mine, k, mask), jnp.where(mine, q, bf(1 / HD)), 1, 1)
            e = jnp.exp(scores - jnp.max(scores, 0, keepdims=True))
            total = jnp.sum(e, 0, keepdims=True)
            o = dot(v_t[HD * h : HD * h + HD], e.astype(bf), 1, 0) * (1.0 / total)
            at = pl.multiple_of((it % 6) * 128 + HD * h, HD)
            ctx_t[pl.ds(at, HD), rows] = o.astype(bf)

    plan.loop(12, attend)

    plan.before()
    G.arrive(OUT_UNIT)
    for s in range(2):
        rows = slice(SEQ_LEN * s, SEQ_LEN * s + SEQ_LEN)
        slots = slice(PMAX * s, PMAX * s + PMAX)
        ctx_gt[:, slots] = dot(ctx_t[:, rows], pick_t[s], 1, 0).astype(bf)
        q_g[slots, :] = dot(pick_t[s], J[0, rows, :], 0, 0).astype(bf)
    r1 = x_g[...].astype(f32) + (dot(ctx_gt[...], unit(OUT_UNIT), 0, 0) + bias(2))
    res_g[...] = r1
    n1 = norm(r1)[0] * bias(3) + bias(4)
    acc_g[...] = n1 + bias(9)
    nl_g[...] = n1.astype(bf)

    def up_listed(q):
        cols = pl.ds(pl.multiple_of(D * q, D), D)
        u = dot(nl_g[...], unit(UP_UNIT + q), 1, 0) + bias(5 + q)
        phi = normal_cdf(u)
        act_g[:, cols] = (u * phi).astype(bf)
        slope_g[:, cols] = (phi + u * normal_density(u)).astype(bf)

    plan.loop(4, up_listed, lambda q: G.arrive(UP_UNIT + q))
    plan.rest()
    for u in range(DOWN_UNIT, UNITS):
        G.arrive(u)

    @pl.loop(0, 4)
    def _(q):
        cols = pl.ds(pl.multiple_of(D * q, D), D)
        acc_g[...] += dot(act_g[:, cols], down_block(q), 1, 0)

    rhat, rstd = norm(acc_g[...])
    used = [dot(pick_t[s], jnp.ones((SEQ_LEN, 128), bf), 0, 0)[:, :1] for s in range(2)]
    cot = jnp.where(jnp.concatenate(used, 0) > 0.5, dq_g[...].astype(f32), 0.0)
    vgrad[10:11, :] = col_sum(cot * rhat)
    vgrad[11:12, :] = col_sum(cot)
    two = norm_back(cot * bias(10), rhat, rstd)
    acc_g[...] = two
    f_grad[...] = two.astype(bf)
    vgrad[9:10, :] = col_sum(f_grad[...])

    def store_unit(m, grad):
        u = scatter_units[m]
        if u in (K_UNIT, V_UNIT, Q_UNIT):
            out, stride, at = g_qkv, 18, 6 * ((u + 1) % 3)
        elif u == OUT_UNIT:
            out, stride, at = g_out, 6, 0
        elif u < DOWN_UNIT:
            out, stride, at = g_up, 24, 6 * (u - UP_UNIT)
        else:
            out, stride, at = g_down, 6, 6 * ROWS * (u - DOWN_UNIT)
        for j in range(6):
            out[pl.ds(at + j, ROWS, stride=stride), :] = grad[:, 128 * j : 128 * j + 128]

    whole = (ALL, ALL, ALL)
    hops = [
        (CORE, whole, (0,) + whole, whole, (0,) + whole),
        (X, whole, (1,) + whole, whole, (1,) + whole),
        (Y, (ALL, ALL, 1 - y), (2, ALL, ALL, 1 - y), (ALL, ALL, y), (2, ALL, ALL, y)),
        (Z0, (ALL, 1 - z0, y), (2, ALL, 1 - z0, 1 - y), (ALL, z0, y), (2, ALL, z0, 1 - y)),
        (Z1, (1 - z1, z0, y), (2, 1 - z1, 1 - z0, 1 - y), (z1, z0, y), (2, z1, 1 - z0, 1 - y)),
    ]

    def hop(k):
        b, out, land, _, _ = hops[k]
        return remote(vsum.at[out], vland.at[land], v_send.at[5 + k], v_recv.at[5 + k], place.partner(b))

    def hop_arrived(k):
        copy = hop(k)
        copy.wait_send()
        copy.wait_recv()
        own, landed = hops[k][3:]
        vsum[own] = vsum[own] + vland[landed]

    T = Scatter(place, S, R, N, s_send, s_recv, ready, parse(scatter_order), store_unit)
    plan = Schedule(T, Chain(hop, hop_arrived, 5), parse(scatter_order), scatter_counts)
    message = {u: m for m, u in enumerate(scatter_units)}

    def put(m, grad):
        for i in range(PARTS):
            S[m, i % 2, i // 16, i // 8 % 2, i // 4 % 2, i // 2 % 2] = wire(grad[ROWS * i : ROWS * i + ROWS])

    def up_back(q):
        cols = pl.ds(pl.multiple_of(D * q, D), D)
        pre = (dot(f_grad[...], down_block(q), 1, 1) * slope_g[:, cols].astype(f32)).astype(bf)
        slope_g[:, cols] = pre
        put(message[UP_UNIT] + q, dot(nl_g[...], pre, 0, 0))

    def down_back(q):
        cols = pl.ds(pl.multiple_of(D * q, D), D)
        pre = slope_g[:, cols]
        vgrad[pl.ds(5 + q, 1), :] = col_sum(pre)
        acc_g[...] += dot(pre, unit(UP_UNIT + q), 1, 1)
        down = dot(act_g[:, cols], f_grad[...], 0, 0)
        for i in range(8):
            for t in range(4):
                at = 96 * i + ROWS * t
                S[message[DOWN_UNIT] + t, i % 2, q // 2, q % 2, i // 4, i // 2 % 2] = wire(down[at : at + ROWS])

    plan.loop(4, up_back)
    plan.loop(4, down_back)
    plan.before()
    rhat, rstd = norm(res_g[...])
    g = acc_g[...]
    vgrad[3:4, :] = col_sum(g * rhat)
    vgrad[4:5, :] = col_sum(g)
    one = norm_back(g * bias(3), rhat, rstd)
    res_g[...] = one
    f_grad[...] = one.astype(bf)
    vgrad[2:3, :] = col_sum(f_grad[...])
    put(message[OUT_UNIT], dot(ctx_gt[...], f_grad[...], 1, 0))
    nl_g[...] = dot(f_grad[...], unit(OUT_UNIT), 1, 1).astype(bf)

    slot_lane = lax.broadcasted_iota(jnp.int32, (PMAX, 128), 1)

    def attend_back(it):
        at = [pair_at(2 * it + k) for k in range(2)]
        none = jnp.zeros((PMAX, 128), bf)
        ones = jnp.full((2 * PMAX, 128), 1 / 128, bf)

        def both(t):
            parts = [jnp.where(slot_lane < HD, t, none), jnp.where(slot_lane < HD, none, t)]
            return jnp.concatenate(parts, 0)

        slots = [pl.ds(pl.multiple_of(s * PMAX, PMAX), PMAX) for s, _, _, _ in at]
        q2 = [both(q_g[sl, cols]) for sl, (_, _, cols, _) in zip(slots, at)]
        g2 = [both(nl_g[sl, cols]) for sl, (_, _, cols, _) in zip(slots, at)]
        keys = [J[1, rows, cols] * scale for _, rows, cols, _ in at]
        scores = [
            dot(jnp.concatenate([k, a[3]], 1), jnp.concatenate([q, ones], 1), 1, 1)
            for k, q, a in zip(keys, q2, at)
        ]
        d_probs = [dot(J[2, rows, cols], g, 1, 1) for g, (_, rows, cols, _) in zip(g2, at)]
        for i, (_, rows, cols, _) in enumerate(at):
            e = jnp.exp(scores[i] - jnp.max(scores[i], 0, keepdims=True))
            probs = e * (1.0 / jnp.sum(e, 0, keepdims=True))
            row_dot = jnp.sum(probs * d_probs[i], 0, keepdims=True)
            d_scores = (probs * (d_probs[i] - row_dot)).astype(bf)
            J[2, rows, cols] = dot(probs.astype(bf), g2[i], 1, 0).astype(bf)
            J[1, rows, cols] = dot(d_scores, q2[i] * scale, 1, 0).astype(bf)
            dq2 = dot(d_scores, keys[i], 0, 0)
            dq_g[slots[i], cols] = jnp.where(slot_lane < HD, dq2[:PMAX], dq2[PMAX:]).astype(bf)

    plan.loop(6, attend_back)
    plan.before()
    put(message[V_UNIT], dot(xs[...], J[2], 0, 0))
    vgrad[1:2, :] = col_sum(J[2])
    plan.before()
    put(message[K_UNIT], dot(xs[...], J[1], 0, 0))
    plan.before()
    put(message[Q_UNIT], dot(x_g[...], dq_g[...], 0, 0))
    vgrad[0:1, :] = col_sum(dq_g[...])

    for r in range(72):
        vsum[r // 36, r // 18 % 2, r // 9 % 2, r % 9 : r % 9 + 1] = vgrad[r // 6 : r // 6 + 1, 128 * (r % 6) : 128 * (r % 6) + 128]

    def ffn_all(it):
        t, q = it // 4, it % 4
        rows = pl.ds(pl.multiple_of(512 * t, 512), 512)

        @pl.when(q == 0)
        def _():
            r = xs[rows, :].astype(f32) + (dot(ctx_t[:, rows], unit(OUT_UNIT), 0, 0) + bias(2))
            n = norm(r)[0] * bias(3) + bias(4)
            nl_t[...] = n.astype(bf)
            acc[...] = n + bias(9)

        half = [slice(0, 256), slice(256, 512)]
        up = [dot(nl_t[h, :], unit(UP_UNIT + q), 1, 0) + bias(5 + q) for h in half]
        for h, u in zip(half, up):
            acc[h, :] += dot((u * normal_cdf(u)).astype(bf), down_block(q), 1, 0)

        @pl.when(q == 3)
        def _():
            done = pltpu.make_async_copy(out_t.at[0:512], layer_out.at[rows, :], out_sem.at[0])

            @pl.when(t > 0)
            def _():
                done.wait()

            out_t[:512, :] = (norm(acc[...])[0] * bias(10) + bias(11)).astype(bf)
            done.start()

    plan.loop(8, ffn_all)

    def grad_in(s):
        rows = pl.ds(pl.multiple_of(s * SEQ_LEN, SEQ_LEN), SEQ_LEN)
        slots = pl.ds(pl.multiple_of(s * PMAX, PMAX), PMAX)
        t = res_g[slots, :] + dot(dq_g[slots, :], unit(Q_UNIT), 1, 1)
        high = t.astype(bf)
        low = (t - high.astype(f32)).astype(bf)
        total = dot(pick_t[s], high, 1, 0) + dot(pick_t[s], low, 1, 0)
        total += dot(J[1, rows, :], unit(K_UNIT), 1, 1)
        total += dot(J[2, rows, :], unit(V_UNIT), 1, 1)
        J[0, rows, :] = total.astype(bf)

    plan.loop(2, grad_in)
    store = pltpu.make_async_copy(J.at[0], input_grad, out_sem.at[1])
    store.start()
    plan.rest()
    g_vec[...] = vsum[z1, z0, y]
    pltpu.make_async_copy(out_t.at[0:512], layer_out.at[0:512, :], out_sem.at[0]).wait()
    store.wait()
    for copy in pair:
        copy.wait_send()
    for k in range(5):
        vec_hop(k).wait_send()
    G.drain()
    T.drain()


def layer_call(sizes, *args):
    vmem = pl.BlockSpec(memory_space=pltpu.VMEM)
    smem = pl.BlockSpec(memory_space=pltpu.SMEM)
    hbm = pl.BlockSpec(memory_space=pl.ANY)
    tokens = 2 * SEQ_LEN
    slots = 2 * PMAX
    dma = pltpu.SemaphoreType.DMA
    return pl.pallas_call(
        partial(layer_kernel, sizes),
        out_shape=(
            jax.ShapeDtypeStruct((tokens, D), bf),
            jax.ShapeDtypeStruct((tokens, D), bf),
            jax.ShapeDtypeStruct((432, 128), f32),
            jax.ShapeDtypeStruct((144, 128), f32),
            jax.ShapeDtypeStruct((576, 128), f32),
            jax.ShapeDtypeStruct((576, 128), f32),
            jax.ShapeDtypeStruct((16, 128), f32),
        ),
        in_specs=[smem, smem] + [vmem] * 2 + [hbm] * 6,
        out_specs=(hbm,) * 2 + (vmem,) * 5,
        scratch_shapes=[
            pltpu.VMEM((DOWN_UNIT, 2, 2, 2, 2, 2 * ROWS, D), bf),
            pltpu.VMEM((2, 2, 2, 2, 4, 2 * ROWS, D), bf),
            pltpu.VMEM((UNITS, 2, 2, 2, 2, 2, 16, WIRE), bf),
            pltpu.VMEM((UNITS, 2, 2, 2, 2, 16, WIRE), bf),
            pltpu.VMEM((UNITS, 2, 2, 2, 16, WIRE), bf),
            pltpu.VMEM((tokens, D), bf),
            pltpu.VMEM((3, tokens, D), bf),
            pltpu.VMEM((D, tokens), bf),
            pltpu.VMEM((slots, FF), bf),
            pltpu.VMEM((slots, FF), bf),
            pltpu.VMEM((2, SEQ_LEN, PMAX), bf),
            pltpu.VMEM((slots, D), bf),
            pltpu.VMEM((slots, D), bf),
            pltpu.VMEM((slots, D), f32),
            pltpu.VMEM((slots, D), f32),
            pltpu.VMEM((slots, D), bf),
            pltpu.VMEM((slots, D), bf),
            pltpu.VMEM((slots, D), bf),
            pltpu.VMEM((D, slots), bf),
            pltpu.VMEM((512, D), f32),
            pltpu.VMEM((512, D), bf),
            pltpu.VMEM((576, D), bf),
            pltpu.VMEM((2, 576, 128), f32),
            pltpu.VMEM((2, 2, 2, 2, 2, 16, 128), bf),
            pltpu.VMEM((16, D), f32),
            pltpu.VMEM((16, D), f32),
            pltpu.VMEM((2, 2, 2, 16, 128), f32),
            pltpu.VMEM((3, 2, 2, 2, 16, 128), f32),
            dma((UNITS, 7)),
            dma((UNITS, 7)),
            dma((UNITS, 7)),
            dma((UNITS, 7)),
            pltpu.SemaphoreType.REGULAR((4,)),
            dma((8,)),
            dma((6,)),
            dma((2,)),
            dma((10,)),
            dma((10,)),
        ],
        compiler_params=pltpu.CompilerParams(
            collective_id=0, has_side_effects=True, vmem_limit_bytes=63 * 2**20
        ),
    )(*args)


settle_parts = 4


def settle_kernel(n, *refs):
    ins, outs, held, sems = refs[:n], refs[n : 2 * n], refs[2 * n : 3 * n], refs[-1]
    loads, stores = [], []
    for i in range(n):
        parts = settle_parts if ins[i].shape[0] >= 1024 else 1
        size = ins[i].shape[0] // parts
        for k in range(parts):
            rows = slice(size * k, size * k + size)
            j = settle_parts * i + k
            loads.append(pltpu.make_async_copy(ins[i].at[rows], held[i].at[rows], sems.at[0, j]))
            stores.append(pltpu.make_async_copy(held[i].at[rows], outs[i].at[rows], sems.at[1, j]))
    for load in loads:
        load.start()
    for load, store in zip(loads, stores):
        load.wait()
        store.start()
    for store in stores:
        store.wait()


def settle(*arrays):
    hbm = pl.BlockSpec(memory_space=pltpu.HBM)
    n = len(arrays)
    return pl.pallas_call(
        partial(settle_kernel, n),
        out_shape=[jax.ShapeDtypeStruct(a.shape, a.dtype) for a in arrays],
        in_specs=[pl.BlockSpec(memory_space=pl.ANY)] * n,
        out_specs=[hbm] * n,
        scratch_shapes=[pltpu.VMEM(a.shape, a.dtype) for a in arrays]
        + [pltpu.SemaphoreType.DMA((2, settle_parts * n))],
        compiler_params=pltpu.CompilerParams(vmem_limit_bytes=63 * 2**20),
    )(*arrays)


def sub_groups(sizes):
    sub = sizes[0] * sizes[1] // PARTS
    return [[sub * i + j for j in range(sub)] for i in range(PARTS)]


def whole_group(sizes, flat):
    if sizes[0] * sizes[1] == PARTS:
        return flat
    return lax.all_gather(flat, ("dp", "inner"), axis_index_groups=sub_groups(sizes), tiled=True)


def own_part(sizes, flat):
    if sizes[0] * sizes[1] == PARTS:
        return flat
    return lax.psum_scatter(
        flat, ("dp", "inner"), axis_index_groups=sub_groups(sizes), scatter_dimension=0, tiled=True
    )


def on_device(
    sizes,
    inputs,
    qkv_weight,
    out_weight,
    up_weight,
    down_weight,
    vectors,
    lengths,
    counts,
    positions,
    grad_values,
):
    wq, wo, w1, w2, vec = [
        whole_group(sizes, w) for w in (qkv_weight, out_weight, up_weight, down_weight, vectors)
    ]
    number = lax.axis_index("dp") * sizes[1] + lax.axis_index("inner")
    quarter = number // (sizes[0] * sizes[1] // PARTS) % 4
    size = vec.shape[0]
    frame = lax.dynamic_update_slice(jnp.zeros((16 * 128,), bf), vec, (quarter * size,)).reshape(16, 128)
    layer_out, input_grad, g_qkv, g_out, g_up, g_down, g_vec = layer_call(
        sizes,
        lengths,
        counts,
        positions,
        frame,
        wq.reshape(-1, 128),
        wo.reshape(-1, 128),
        w1.reshape(-1, 128),
        w2.reshape(-1, 128),
        inputs,
        grad_values.reshape(-1, D),
    )
    g_vec = lax.dynamic_slice(g_vec.reshape(-1), (quarter * size,), (size,))
    layer_out, input_grad, g_qkv, g_out, g_up, g_down = settle(
        layer_out, input_grad, g_qkv, g_out, g_up, g_down
    )
    flat = [own_part(sizes, g.reshape(-1)) for g in (g_qkv, g_out, g_up, g_down, g_vec)]
    return (layer_out, input_grad, *flat)


def solution(mesh):
    both = ("dp", "inner")
    rows, flat = P(both, None), P(both)
    return jax.shard_map(
        partial(on_device, (mesh.shape["dp"], mesh.shape["inner"])),
        mesh=mesh,
        in_specs=(rows, flat, flat, flat, flat, flat, flat, flat, rows, P(both, None, None)),
        out_specs=(rows, rows, flat, flat, flat, flat, flat),
        check_vma=False,
    )
```
